32 devices in a mesh: parts: 32 (over z, y, x, core).
Axes of the slice: x: 2, y: 2, z: 4, core: 2. Of those that a mesh axis runs over, the one named last changes fastest.
Arguments:
- positions: float32 [3, 16384], P(None, 'parts'), may hold values from -6 to 6
- velocity: float32 [3, 16384], P(None, 'parts'), may hold values from -6 to 6
- inv_mass: float32 [16384], P('parts'), may hold values from 0.5 to 4
- swap_lists: int32 [3, 8192], P(None, 'parts'), may hold values from 0 to 511, as said below
- rim_list: int32 [4096], P('parts'), may hold values from 0 to 511, as said below
- contact_pair: int32 [2, 32768], P(None, 'parts'), may hold values from 0 to 767, as said below
- delassus: float32 [256, 128, 128], P('parts'), as said below
Outputs:
- new_velocity: float32 [3, 16384], P(None, 'parts')
- impulse: float32 [32768], P('parts')
The draws below stay inside these ranges and needn't reach their ends.
Inputs may be any that keep to these rules, and one draw needn't show every extreme that they name: `swap_lists`: the 256 slots of one part at one level are distinct. `rim_list`: the 128 slots of one part are distinct. `contact_pair`: the first index of a contact is a local grain; the two indices differ. `delassus`: tile diagonals lie between 4 and 8.
All inputs are finite; a program needn't handle non-finite values.
Results may differ from the reference program's by a relative error of at most 0.0003.
Values sent between devices are 32-bit elements; how exact they have to be, the bound alone decides.
No kernel may reach another device: no remote copies, remote signals or barrier semaphores. Data moves between devices by JAX's collectives and lax.ppermute only.
A program may use at most 64 MiB of HBM per device.

```python
import math
import jax
import jax.numpy as jnp
from jax import lax

GRAIN_DEV = 512
SWAP_ROWS = 256
RIM = 128
TILES_DEV = 8
TILE = 128
CONTACT_DEV = 1024
LEVELS = 3
ITERS = 2
GRAINS = 16384
CONTACTS = 32768


def distinct_slots(key, lists, keep):
    keys = jax.random.split(key, lists)
    return jax.vmap(lambda one: jax.random.permutation(one, GRAIN_DEV)[:keep])(keys).astype(jnp.int32)


def draw_swap_lists(key, part):
    count = GRAINS // GRAIN_DEV
    slots = distinct_slots(jax.random.fold_in(key, 11), LEVELS * count, SWAP_ROWS)
    return slots.reshape(LEVELS, count * SWAP_ROWS)


def draw_rim_list(key, part):
    count = GRAINS // GRAIN_DEV
    return distinct_slots(jax.random.fold_in(key, 23), count, RIM).reshape(count * RIM)


def draw_contact_pair(key, part):
    count = GRAINS // GRAIN_DEV
    key_one, key_two = jax.random.split(jax.random.fold_in(key, 37))
    first = jax.random.randint(key_one, (count, CONTACT_DEV), 0, GRAIN_DEV, dtype=jnp.int32)
    other = jax.random.randint(key_two, (count, CONTACT_DEV), 0, GRAIN_DEV + 2 * RIM - 1, dtype=jnp.int32)
    other = jnp.where(other >= first, other + 1, other)
    return jnp.stack([first, other]).reshape(2, count * CONTACT_DEV)


def draw_delassus(key, part):
    count = GRAINS // GRAIN_DEV
    key_one, key_two = jax.random.split(jax.random.fold_in(key, 41))
    off = 0.15 * jax.random.normal(key_one, (TILES_DEV * count, TILE, TILE), jnp.float32)
    diag = jax.random.uniform(key_two, (TILES_DEV * count, TILE), jnp.float32, 4.0, 8.0)
    eye = jnp.eye(TILE, dtype=jnp.float32)
    return off * (1.0 - eye) + diag[:, :, None] * eye


def steps_of(stream_key, shape, pieces, least, top_value):
    gain, own = 1.0, jax.random.fold_in(stream_key, 6)
    for dim, shards_of in pieces:
        heights = jnp.exp(jax.random.uniform(jax.random.fold_in(own, dim), (shards_of,), jnp.float32, least / len(pieces), top_value / len(pieces)))
        gain = gain * jnp.repeat(heights, shape[dim] // shards_of).reshape([-1 if axis == dim else 1 for axis in range(len(shape))])
    return gain


def centred(own_key, shape, spread, bound, shards=(), kind=jnp.bfloat16):
    entries = spread * jax.random.normal(own_key, shape, jnp.float32)
    if shards:
        entries = entries * steps_of(own_key, shape, shards, -0.22, 0.18)
    return jnp.clip(entries, -bound, bound).astype(kind)


def setup_inputs(seed: int = 0) -> dict:
    key_of = jax.random.split(jax.random.key(seed), 8)
    positions = centred(key_of[0], (3, GRAINS), 1.0, 6.0, ((1, 32),), jnp.float32)
    velocity = centred(key_of[1], (3, GRAINS), 1.0, 6.0, ((1, 32),), jnp.float32)
    inv_mass = jnp.clip(jnp.exp(math.log(4.0) - 2.0794415 * jax.random.uniform(key_of[2], (GRAINS,), jnp.float32) ** steps_of(key_of[2], (GRAINS,), ((0, 32),), -0.2, 0.2)), 0.5, 4.0)
    swap_lists = draw_swap_lists(jax.random.fold_in(key_of[7], 71), 0)
    rim_list = draw_rim_list(jax.random.fold_in(key_of[7], 71), 0)
    contact_pair = draw_contact_pair(jax.random.fold_in(key_of[7], 71), 0)
    delassus = draw_delassus(jax.random.fold_in(key_of[7], 71), 0)
    return {"positions": positions, "velocity": velocity, "inv_mass": inv_mass, "swap_lists": swap_lists, "rim_list": rim_list, "contact_pair": contact_pair, "delassus": delassus}


def shift_down(block):
    zeros = jnp.zeros_like(block[:, :1])
    return jnp.concatenate([zeros, block[:, :-1]], axis=1)


def shift_up(block):
    zeros = jnp.zeros_like(block[:, :1])
    return jnp.concatenate([block[:, 1:], zeros], axis=1)


def extend(field, rows, rim_slots):
    rim_rows = field[:, rows, rim_slots]
    return jnp.concatenate([field, shift_down(rim_rows), shift_up(rim_rows)], axis=2)


def reference(positions, velocity, inv_mass, swap_lists, rim_list, contact_pair, delassus):
    count = GRAINS // GRAIN_DEV
    bits = count.bit_length() - 1
    parts_ids = jnp.arange(count, dtype=jnp.int32)
    rows = parts_ids[:, None]
    pos = positions.reshape(3, count, GRAIN_DEV)
    vel = velocity.reshape(3, count, GRAIN_DEV)
    mass = inv_mass.reshape(1, count, GRAIN_DEV)
    for level in range(LEVELS):
        partner = parts_ids ^ (1 << (bits - 1 - level))
        slots = swap_lists[level].reshape(count, SWAP_ROWS)
        pos = pos.at[:, rows, slots].set(pos[:, rows, slots][:, partner])
        vel = vel.at[:, rows, slots].set(vel[:, rows, slots][:, partner])
        mass = mass.at[:, rows, slots].set(mass[:, rows, slots][:, partner])
    rim_slots = rim_list.reshape(count, RIM)
    ext_pos = extend(pos, rows, rim_slots)
    ext_vel = extend(vel, rows, rim_slots)
    first = contact_pair[0].reshape(count, CONTACT_DEV)
    second = contact_pair[1].reshape(count, CONTACT_DEV)
    normal = ext_pos[:, rows, first] - ext_pos[:, rows, second]
    tiles = delassus.reshape(count, TILES_DEV, TILE, TILE)
    diag = jnp.diagonal(tiles, axis1=2, axis2=3).reshape(count, CONTACT_DEV)
    lam = jnp.zeros((count, CONTACT_DEV), jnp.float32)
    current = vel
    for step in range(ITERS):
        speed = jnp.sum(normal * (ext_vel[:, rows, first] - ext_vel[:, rows, second]), axis=0)
        coupled = jnp.einsum("ptij,ptj->pti", tiles, lam.reshape(count, TILES_DEV, TILE), precision=lax.Precision.HIGHEST).reshape(count, CONTACT_DEV)
        lam = jnp.maximum(0.0, lam - (coupled + speed) / diag)
        force = normal * lam[None]
        partial_value = jnp.zeros((3, count, GRAIN_DEV + 2 * RIM), jnp.float32)
        partial_value = partial_value.at[:, rows, first].add(force).at[:, rows, second].add(-force)
        left_ghost = partial_value[:, :, GRAIN_DEV:GRAIN_DEV + RIM]
        right_ghost = partial_value[:, :, GRAIN_DEV + RIM:]
        incoming = shift_down(right_ghost) + shift_up(left_ghost)
        local = partial_value[:, :, :GRAIN_DEV].at[:, rows, rim_slots].add(incoming)
        current = vel + mass * local
        ext_vel = extend(current, rows, rim_slots)
    return current.reshape(3, GRAINS), lam.reshape(CONTACTS)
```

```python
import functools

import jax
import jax.numpy as jnp
from jax import lax
from jax.experimental import pallas as pl
from jax.experimental.pallas import tpu as pltpu
from jax.sharding import PartitionSpec as P

TILE = 128
LEVELS = 3
GROUP = 2**LEVELS
REACH = 4
FIELDS = 8
CHUNKS = 4
EXT_CHUNKS = 6
RIM_AT = 7
FIRST_AT = 32
SECOND_AT = 40
DIAG_AT = 48
RECORD = 56
LISTS_AT = 32
RAW = 40
FIXED = RECORD - FIRST_AT
BLOCK = 4
PARAMS = pltpu.CompilerParams(vmem_limit_bytes=32 * 2**20)
FROM_HBM = pltpu.CompilerParams(vmem_limit_bytes=63 * 2**20)
NT = (((1,), (1,)), ((), ()))


def rows_iota(shape):
    return lax.broadcasted_iota(jnp.int32, shape, 0)


def lanes_iota(shape):
    return lax.broadcasted_iota(jnp.int32, shape, 1)


def wide(row):
    return jnp.broadcast_to(row, (FIELDS, TILE))


def take(table, lane):
    return jnp.take_along_axis(table, lane, axis=1, mode="promise_in_bounds")


def look_up(rows, index):
    lane, high = index & (TILE - 1), index >> 7
    found = take(wide(rows[0]), lane)
    for h in range(1, len(rows)):
        found = jnp.where(high == h, take(wide(rows[h]), lane), found)
    return found


def one_hot(low_row):
    return (rows_iota((TILE, TILE)) == low_row).astype(jnp.float32).astype(jnp.bfloat16)


def inverse(slot_rows):
    left, right = [], []
    for at, row in enumerate(slot_rows):
        slots = row.astype(jnp.int32)
        place = (lanes_iota((FIELDS, TILE)) + (at * TILE + 1)).astype(jnp.float32)
        heads = jnp.where(wide(slots >> 7) == rows_iota((FIELDS, TILE)), place, 0.0)
        left.append(heads.astype(jnp.bfloat16))
        right.append(one_hot(slots & (TILE - 1)))
    total = lax.dot_general(
        jnp.concatenate(left, axis=1),
        jnp.concatenate(right, axis=1),
        NT,
        preferred_element_type=jnp.float32,
    )
    return total.astype(jnp.int32)


def pack_kernel(*refs):
    sources, out, held, sems = refs[:5], refs[5], refs[6:11], refs[11]
    copies = [
        pltpu.make_async_copy(source, target, sems.at[k])
        for k, (source, target) in enumerate(zip(sources, held))
    ]
    for copy in copies:
        copy.start()
    pos, vel, mass, lists, rim = held
    for copy in copies:
        copy.wait()
    first = out.at[0]
    for c in range(CHUNKS):
        lanes = pl.ds(c * TILE, TILE)
        first[pl.ds(FIELDS * c, 3), :] = pos[:, lanes]
        first[pl.ds(FIELDS * c + 3, 3), :] = vel[:, lanes]
        first[pl.ds(FIELDS * c + 6, 1), :] = mass[pl.ds(c, 1), :]
        spare = rim[...].astype(jnp.float32) if c == 0 else jnp.zeros((1, TILE), jnp.float32)
        first[pl.ds(FIELDS * c + 7, 1), :] = spare
    for level in range(LEVELS):
        for h in range(2):
            row = lists[pl.ds(level, 1), pl.ds(h * TILE, TILE)]
            first[pl.ds(LISTS_AT + 2 * level + h, 1), :] = row.astype(jnp.float32)
    first[pl.ds(LISTS_AT + 2 * LEVELS, 2), :] = jnp.zeros((2, TILE), jnp.float32)
    whole = first[...]
    for m in range(1, GROUP):
        out[m] = whole


def fixed_kernel(pair, tiles, out):
    eye = rows_iota((TILE, TILE)) == lanes_iota((TILE, TILE))
    for t in range(tiles.shape[0]):
        lanes = pl.ds(t * TILE, TILE)
        out[pl.ds(t, 1), :] = pair[pl.ds(0, 1), lanes].astype(jnp.float32)
        out[pl.ds(FIELDS + t, 1), :] = pair[pl.ds(1, 1), lanes].astype(jnp.float32)
        diag = jnp.sum(jnp.where(eye, tiles[t], 0.0), axis=0, keepdims=True)
        out[pl.ds(2 * FIELDS + t, 1), :] = diag


def compose_kernel(stride, raw, own):
    member = lax.axis_index("parts") // stride

    def list_rows(part, level):
        return [raw[part, pl.ds(LISTS_AT + 2 * level + h, 1), :] for h in range(2)]

    def table_rows(table):
        return [table[h : h + 1] for h in range(CHUNKS)]

    aims = [(member + which + (GROUP - 1)) % GROUP for which in range(3)]
    zero = jnp.zeros((FIELDS, TILE), jnp.int32)
    backs = {
        (which, x, level): table_rows(inverse(list_rows(aim ^ x, level)))
        for level in reversed(range(LEVELS))
        for x in range(2 ** (LEVELS - 1 - level))
        for which, aim in enumerate(aims)
    }
    slots = [rows_iota((FIELDS, TILE)) % CHUNKS * TILE + lanes_iota((FIELDS, TILE))] * 3
    shifts = [zero] * 3
    for level in reversed(range(LEVELS)):
        bit = GROUP >> (level + 1)
        candidates = range(2 ** (LEVELS - 1 - level))
        for which, aim in enumerate(aims):
            slot, shift = slots[which], shifts[which]
            place = zero
            for x in candidates:
                found = look_up(backs[which, x, level], slot)
                place = jnp.where(shift == x, found, place) if x else found
            moved = place > 0
            place = jnp.maximum(place - 1, 0)
            for x in candidates:
                found = look_up(list_rows(aim ^ x ^ bit, level), place).astype(jnp.int32)
                slot = jnp.where(moved & (shift == x), found, slot)
            slots[which] = slot
            shifts[which] = jnp.where(moved, shift + bit, shift)
    for which, aim in enumerate(aims):
        there = (member + which >= 1) & (member + which <= GROUP)
        lane = slots[which] & (TILE - 1)
        block = shifts[which] * CHUNKS + (slots[which] >> 7)
        lanes = [wide(lane[c : c + 1]) for c in range(CHUNKS)]
        blocks = [wide(block[c : c + 1]) for c in range(CHUNKS)]
        found = [jnp.zeros((FIELDS, TILE), jnp.float32)] * CHUNKS
        for x in range(GROUP):
            for h in range(CHUNKS):
                table = raw[aim ^ x, pl.ds(FIELDS * h, FIELDS), :]
                for c in range(CHUNKS):
                    here = blocks[c] == x * CHUNKS + h
                    found[c] = jnp.where(here, take(table, lanes[c]), found[c])
        for c in range(CHUNKS):
            own[which, pl.ds(FIELDS * c, FIELDS), :] = jnp.where(there, found[c], 0.0)
        own[which, pl.ds(RIM_AT, 1), :] = jnp.where(there, raw[aim, pl.ds(RIM_AT, 1), :], 0.0)

def join_kernel(stride, states, fixed, paired, across, own, *sends):
    me = lax.axis_index("parts")
    member, kind = me // stride, me % stride
    odd = member % 2 == 1
    for which in range(3):
        own[which, pl.ds(0, FIRST_AT), :] = states[which]
        there = (member + which >= 1) & (member + which <= GROUP)
        for at in range(0, FIXED, FIELDS):
            rows = pl.ds(at, FIELDS)
            if which == 1:
                rest = fixed[rows, :]
            else:
                by_pair = odd if which == 0 else jnp.logical_not(odd)
                rest = jnp.where(by_pair, paired[rows, :], across[rows, :])
            absent = 1.0 if at == DIAG_AT - FIRST_AT else 0.0
            own[which, pl.ds(FIRST_AT + at, FIELDS), :] = jnp.where(there, rest, absent)

    if stride == BLOCK:
        for send, later in zip(sends, (kind % 2 == 0, kind < 2)):
            for k in range(2):
                send[k] = jnp.where(later, own[k + 1], own[k])
    else:
        (send,) = sends

        def fill(to, carry):
            base = jnp.where(kind < to, 1, 0)
            send[to, 0] = own[base]
            send[to, 1] = own[base + 1]
            return carry

        lax.fori_loop(0, stride, fill, 0)


def gather_records(stride, own, sources, records, offsets):
    kind = lax.axis_index("parts") % stride
    even = kind % 2 == 0
    for o in offsets:
        at, later = o + REACH, 1 if o > 0 else 0
        if o % stride == 0:
            records[at] = own[1 + o // stride]
        elif stride != BLOCK:
            records[at] = sources[0][(kind + o + stride) % stride, later]
        elif o % 2 == 0:
            records[at] = sources[2][later]
        else:
            by_chip = even if o in (1, -3) else jnp.logical_not(even)
            records[at] = jnp.where(by_chip, sources[0][later], sources[1][later])


def state_of(record):
    return [record[pl.ds(FIELDS * c, FIELDS), :] for c in range(CHUNKS)]


def ends_of(record):
    first = record[pl.ds(FIRST_AT, FIELDS), :].astype(jnp.int32)
    second = record[pl.ds(SECOND_AT, FIELDS), :].astype(jnp.int32)
    return first, second


def diag_of(record):
    return record[pl.ds(DIAG_AT, FIELDS), :]


def rim_of(record, blocks):
    slots = wide(record[pl.ds(RIM_AT, 1), :].astype(jnp.int32))
    lane, high = slots & (TILE - 1), slots >> 7
    found = take(blocks[0], lane)
    for c in range(1, CHUNKS):
        found = jnp.where(high == c, take(blocks[c], lane), found)
    return found


def difference(local, before, after, field, first, second):
    near = [local[pl.ds(FIELDS * c + field, 1), :] for c in range(CHUNKS)]
    ghosts = [one[pl.ds(field, 1), :] for one in (before, after)]
    return look_up(near, first) - look_up(near + ghosts, second)


def first_lam(record, before, after):
    first, second = ends_of(record)
    normal = [difference(record, before, after, k, first, second) for k in range(3)]
    speed = sum(
        normal[k] * difference(record, before, after, 3 + k, first, second) for k in range(3)
    )
    return normal, jnp.maximum(0.0, -speed / diag_of(record))


def add_up(force, first, second, heads, rows):
    for k in range(3):
        head = force[k].astype(jnp.bfloat16).astype(jnp.float32)
        rows[pl.ds(k, FIELDS, stride=FIELDS), :] = force[k] - head
        rows[pl.ds(3 + k, FIELDS, stride=FIELDS), :] = head
    empty = jnp.zeros((FIELDS, TILE), jnp.float32)
    pad = [empty] * (len(heads) % 2)
    left, right = [], []
    for t in range(FIELDS):
        value = rows[pl.ds(FIELDS * t, FIELDS), :]
        for index, limit, signed in ((first, CHUNKS, value), (second, EXT_CHUNKS, -value)):
            if min(heads) >= limit:
                continue
            row = index[t : t + 1]
            high = wide(row >> 7)
            groups = [jnp.where(high == h, signed, 0.0) if h < limit else empty for h in heads]
            left.append(jnp.concatenate(groups + pad, axis=0))
            right.append(one_hot(row & (TILE - 1)))
    total = 0.0
    for k in range(0, len(left), 2):
        total += lax.dot_general(
            jnp.concatenate(left[k : k + 2], axis=1).astype(jnp.bfloat16),
            jnp.concatenate(right[k : k + 2], axis=1),
            NT,
            preferred_element_type=jnp.float32,
        )
    blocks = [total[FIELDS * k : FIELDS * (k + 1)] for k in range(len(heads))]
    return {h: block + pltpu.roll(block, 3, 0) for h, block in zip(heads, blocks)}


def moved(was, here, incoming, back_row):
    place = wide(back_row)
    extra = jnp.where(place > 0, take(incoming, jnp.maximum(place - 1, 0)), 0.0)
    field = rows_iota((FIELDS, TILE))
    gain = wide(was[6:7]) * (here + extra)
    return was + jnp.where((field >= 3) & (field < 6), gain, 0.0)


def near_kernel(stride, sources, *refs):
    own, came = refs[0], refs[1 : 1 + sources]
    tiles, coupled, records, rims = refs[1 + sources :]
    gather_records(stride, own, came, records, (-1, 0, 1))
    before, here, after = [records.at[o + REACH] for o in (-1, 0, 1)]
    for k, record in ((0, before), (1, after)):
        rims[k] = rim_of(record, state_of(record))
    lam = first_lam(here, rims.at[0], rims.at[1])[1]
    head = lam.astype(jnp.bfloat16).astype(jnp.float32)
    both = jnp.concatenate([head, lam - head], axis=0).astype(jnp.bfloat16)
    total = jnp.zeros((FIELDS, TILE), jnp.float32)
    for t in range(tiles.shape[0]):
        tile = tiles[t]
        tile_head = tile.astype(jnp.bfloat16)
        tile_tail = (tile - tile_head.astype(jnp.float32)).astype(jnp.bfloat16)
        main = lax.dot_general(both, tile_head, NT, preferred_element_type=jnp.float32)
        rest = lax.dot_general(both, tile_tail, NT, preferred_element_type=jnp.float32)
        whole = main[:FIELDS] + main[FIELDS:] + rest[:FIELDS]
        total = jnp.where(rows_iota((FIELDS, TILE)) == t, whole, total)
    coupled[...] = total


def middle_kernel(stride, sources, *refs):
    own, came = refs[0], refs[1 : 1 + sources]
    stage, back_here, fixed_out, gathered, rims, rows, state_next, rims_next = refs[1 + sources :]
    offsets = range(-REACH, REACH + 1)
    gather_records(stride, own, came, gathered, offsets)
    records = {o: gathered.at[o + REACH] for o in offsets}
    for o, record in records.items():
        rims[o + REACH] = rim_of(record, state_of(record))
    sums, contacts = {}, {}
    for o in range(1 - REACH, REACH):
        record = records[o]
        contacts[o] = first_lam(record, rims.at[o + REACH - 1], rims.at[o + REACH + 1])
    for o in range(1 - REACH, REACH):
        normal, lam = contacts[o]
        first, second = ends_of(records[o])
        heads = list(range(CHUNKS)) if abs(o) < REACH - 1 else []
        heads += [CHUNKS] if o > 1 - REACH + 1 else []
        heads += [CHUNKS + 1] if o < REACH - 1 - 1 else []
        force = [one * lam for one in normal]
        sums[o] = add_up(force, first, second, heads, rows.at[o + REACH - 1])
    for o in range(2 - REACH, REACH - 1):
        incoming = sums[o - 1][CHUNKS + 1] + sums[o + 1][CHUNKS]
        back = inverse([records[o][pl.ds(RIM_AT, 1), :]])
        if o == 0:
            back_here[...] = back
        blocks = [
            moved(was, sums[o][c], incoming, back[c : c + 1])
            for c, was in enumerate(state_of(records[o]))
        ]
        rims_next[o + REACH] = rim_of(records[o], blocks)
        if abs(o) < 2:
            for c in range(CHUNKS):
                state_next[o + 1, pl.ds(FIELDS * c, FIELDS), :] = blocks[c]
    for o in (-1, 0, 1):
        normal, lam = contacts[o]
        first, second = ends_of(records[o])
        before, after = rims_next.at[o + REACH - 1], rims_next.at[o + REACH + 1]
        state = state_next.at[o + 1]
        speed = sum(
            normal[k] * difference(state, before, after, 3 + k, first, second) for k in range(3)
        )
        for k in range(3):
            stage[o + 1, k] = normal[k]
        stage[o + 1, 3] = lam
        stage[o + 1, 4] = speed
        fixed_out[o + 1] = records[o][pl.ds(FIRST_AT, FIXED), :]


def last_kernel(
    parts, own, stage, back, here, chip, other, mid, fixed, velocity, impulse, rows
):
    me = lax.axis_index("parts")
    odd = me % 2 == 1
    central = (me == parts // 2) | (me == parts // 2 - 1)
    across = jnp.where(central, mid[...], other[...])
    across = jnp.where((me > 0) & (me < parts - 1), across, 0.0)
    coupled = {
        -1: jnp.where(odd, chip[...], across),
        0: here[...],
        1: jnp.where(odd, across, chip[...]),
    }
    sums = {}
    for o, heads in ((-1, [CHUNKS + 1]), (0, list(range(CHUNKS))), (1, [CHUNKS])):
        record = fixed.at[o + 1]
        lam = stage[o + 1, 3]
        diag = record[pl.ds(DIAG_AT - FIRST_AT, FIELDS), :]
        lam = jnp.maximum(0.0, lam - (coupled[o] + stage[o + 1, 4]) / diag)
        if o == 0:
            impulse[...] = lam
        first = record[pl.ds(0, FIELDS), :].astype(jnp.int32)
        second = record[pl.ds(SECOND_AT - FIRST_AT, FIELDS), :].astype(jnp.int32)
        force = [stage[o + 1, k] * lam for k in range(3)]
        sums[o] = add_up(force, first, second, heads, rows.at[o + 1])
    incoming = sums[-1][CHUNKS + 1] + sums[1][CHUNKS]
    for c, was in enumerate(state_of(own.at[1])):
        block = moved(was, sums[0][c], incoming, back[pl.ds(c, 1), :])
        velocity[:, pl.ds(c * TILE, TILE)] = block[3:6]


def call(kernel, out_shape, inputs, name, space=pltpu.VMEM, scratch=()):
    many = isinstance(out_shape, (tuple, list))
    vmem = pl.BlockSpec(memory_space=pltpu.VMEM)
    return pl.pallas_call(
        kernel,
        out_shape=out_shape,
        in_specs=[pl.BlockSpec(memory_space=space)] * len(inputs),
        out_specs=[vmem] * len(out_shape) if many else vmem,
        scratch_shapes=list(scratch),
        compiler_params=FROM_HBM if space == pltpu.HBM else PARAMS,
        name=name,
    )(*inputs)


def block_borders(parts, stride):
    to = {i: i ^ 1 for i in range(parts)}
    for i in range(stride, parts - stride):
        to[i] = i + stride if i // stride % 2 == 1 else i - stride
    return list(to.items())


def next_pairs(parts):
    half = parts // 2
    most = {i: i + 1 if i % 2 else i - 1 for i in range(parts)}
    most.update({0: half - 1, half - 1: 0, half: parts - 1, parts - 1: half})
    middle = {i: i ^ 1 for i in range(parts)}
    middle.update({half - 1: half, half: half - 1, half - 2: half + 1, half + 1: half - 2})
    return list(most.items()), list(middle.items())


def body(positions, velocity, inv_mass, swap_lists, rim_list, contact_pair, delassus):
    parts = lax.axis_size("parts")
    stride = parts // GROUP
    grains = positions.shape[1]
    contacts = contact_pair.shape[1]
    tiles = delassus.shape[0]
    reach = 2 * REACH + 1
    float32 = functools.partial(jax.ShapeDtypeStruct, dtype=jnp.float32)
    vmem = lambda *shape: pltpu.VMEM(shape, jnp.float32)
    send = functools.partial(lax.ppermute, axis_name="parts")
    inputs = (
        positions,
        velocity,
        inv_mass.reshape(CHUNKS, TILE),
        swap_lists,
        rim_list.reshape(1, TILE),
    )
    packed = call(
        pack_kernel,
        float32((GROUP, RAW, TILE)),
        inputs,
        "pack",
        pltpu.HBM,
        [pltpu.VMEM(one.shape, one.dtype) for one in inputs] + [pltpu.SemaphoreType.DMA((5,))],
    )
    classes = [[r + stride * k for k in range(GROUP)] for r in range(stride)]
    raw = lax.all_to_all(packed, "parts", 0, 0, axis_index_groups=classes)

    fixed = call(fixed_kernel, float32((FIXED, TILE)), (contact_pair, delassus), "fixed")
    paired = send(fixed, perm=[(i, i ^ stride) for i in range(parts)])
    across = send(fixed, perm=block_borders(parts, stride))

    record = (2, RECORD, TILE)
    sends = [float32(record)] * 2 if stride == BLOCK else [float32((stride, *record))]
    states = call(
        functools.partial(compose_kernel, stride),
        float32((3, FIRST_AT, TILE)),
        (raw,),
        "compose",
    )
    own, *sends = call(
        functools.partial(join_kernel, stride),
        (float32((3, RECORD, TILE)), *sends),
        (states, fixed, paired, across),
        "join",
    )
    within = [(i, i ^ 1) for i in range(parts)]
    opposite = [(i, i ^ 3) for i in range(parts)]
    if stride == BLOCK:
        from_far = send(sends[1], perm=opposite)
        from_side = send(sends[1], perm=[(i, i ^ 2) for i in range(parts)])
        near = (send(sends[0], perm=within), from_far)
        came = (*near, from_side)
    else:
        blocks = [[stride * k + r for r in range(stride)] for k in range(GROUP)]
        near = came = (lax.all_to_all(sends[0], "parts", 0, 0, axis_index_groups=blocks),)

    here = call(
        functools.partial(near_kernel, stride, len(near)),
        float32((tiles, TILE)),
        (own, *near, delassus),
        "near",
        scratch=[vmem(reach, RECORD, TILE), vmem(2, FIELDS, TILE)],
    )
    most, middle = next_pairs(parts)
    other = send(here, perm=most)
    chip = send(here, perm=within)
    mid = send(here, perm=middle)
    stage, back, contact_rows = call(
        functools.partial(middle_kernel, stride, len(came)),
        (
            float32((3, 5, FIELDS, TILE)),
            jax.ShapeDtypeStruct((FIELDS, TILE), jnp.int32),
            float32((3, FIXED, TILE)),
        ),
        (own, *came),
        "middle",
        scratch=[
            vmem(reach, RECORD, TILE),
            vmem(reach, FIELDS, TILE),
            vmem(reach - 2, FIELDS * FIELDS, TILE),
            vmem(3, CHUNKS * FIELDS, TILE),
            vmem(reach, FIELDS, TILE),
        ],
    )
    new_velocity, impulse = call(
        functools.partial(last_kernel, parts),
        (float32((3, grains)), float32((tiles, TILE))),
        (own, stage, back, here, chip, other, mid, contact_rows),
        "last",
        scratch=[vmem(3, FIELDS * FIELDS, TILE)],
    )
    return (new_velocity, impulse.reshape(contacts))


def solution(mesh):
    in_specs = (
        P(None, "parts"),
        P(None, "parts"),
        P("parts"),
        P(None, "parts"),
        P("parts"),
        P(None, "parts"),
        P("parts", None, None),
    )
    out_specs = (P(None, "parts"), P("parts"))
    return jax.shard_map(body, mesh=mesh, in_specs=in_specs, out_specs=out_specs, check_vma=False)
```

```python
import functools

import jax
import jax.numpy as jnp
from jax import lax
from jax.experimental import pallas as pl
from jax.experimental.pallas import tpu as pltpu
from jax.sharding import PartitionSpec as P

TILE = 128
LEVELS = 3
GROUP = 2**LEVELS
REACH = 2
FIELDS = 8
CHUNKS = 4
EXT_CHUNKS = 6
RIM_AT = 7
FIRST_AT = 32
SECOND_AT = 40
DIAG_AT = 48
RECORD = 56
LISTS_AT = 32
RAW = 40
FIXED = RECORD - FIRST_AT
BLOCK = 4
EDGE = 8
PARAMS = pltpu.CompilerParams(vmem_limit_bytes=32 * 2**20)
FROM_HBM = pltpu.CompilerParams(vmem_limit_bytes=63 * 2**20)
NT = (((1,), (1,)), ((), ()))


def rows_iota(shape):
    return lax.broadcasted_iota(jnp.int32, shape, 0)


def lanes_iota(shape):
    return lax.broadcasted_iota(jnp.int32, shape, 1)


def wide(row):
    return jnp.broadcast_to(row, (FIELDS, TILE))


def take(table, lane):
    return jnp.take_along_axis(table, lane, axis=1, mode="promise_in_bounds")


def look_up(rows, index):
    lane, high = index & (TILE - 1), index >> 7
    found = take(wide(rows[0]), lane)
    for h in range(1, len(rows)):
        found = jnp.where(high == h, take(wide(rows[h]), lane), found)
    return found


def one_hot(low_row):
    return (rows_iota((TILE, TILE)) == low_row).astype(jnp.float32).astype(jnp.bfloat16)


def inverse(slot_rows):
    left, right = [], []
    for at, row in enumerate(slot_rows):
        slots = row.astype(jnp.int32)
        place = (lanes_iota((FIELDS, TILE)) + (at * TILE + 1)).astype(jnp.float32)
        heads = jnp.where(wide(slots >> 7) == rows_iota((FIELDS, TILE)), place, 0.0)
        left.append(heads.astype(jnp.bfloat16))
        right.append(one_hot(slots & (TILE - 1)))
    total = lax.dot_general(
        jnp.concatenate(left, axis=1),
        jnp.concatenate(right, axis=1),
        NT,
        preferred_element_type=jnp.float32,
    )
    return total.astype(jnp.int32)


def pack_kernel(*refs):
    sources, out, held, sems = refs[:5], refs[5], refs[6:11], refs[11]
    copies = [
        pltpu.make_async_copy(source, target, sems.at[k])
        for k, (source, target) in enumerate(zip(sources, held))
    ]
    for copy in copies:
        copy.start()
    pos, vel, mass, lists, rim = held
    for copy in copies:
        copy.wait()
    first = out.at[0]
    for c in range(CHUNKS):
        lanes = pl.ds(c * TILE, TILE)
        first[pl.ds(FIELDS * c, 3), :] = pos[:, lanes]
        first[pl.ds(FIELDS * c + 3, 3), :] = vel[:, lanes]
        first[pl.ds(FIELDS * c + 6, 1), :] = mass[pl.ds(c, 1), :]
        spare = rim[...].astype(jnp.float32) if c == 0 else jnp.zeros((1, TILE), jnp.float32)
        first[pl.ds(FIELDS * c + 7, 1), :] = spare
    for level in range(LEVELS):
        for h in range(2):
            row = lists[pl.ds(level, 1), pl.ds(h * TILE, TILE)]
            first[pl.ds(LISTS_AT + 2 * level + h, 1), :] = row.astype(jnp.float32)
    first[pl.ds(LISTS_AT + 2 * LEVELS, 2), :] = jnp.zeros((2, TILE), jnp.float32)
    whole = first[...]
    for m in range(1, GROUP):
        out[m] = whole


def fixed_kernel(pair, tiles, out, heads, tails):
    eye = rows_iota((TILE, TILE)) == lanes_iota((TILE, TILE))
    for t in range(tiles.shape[0]):
        lanes = pl.ds(t * TILE, TILE)
        out[pl.ds(t, 1), :] = pair[pl.ds(0, 1), lanes].astype(jnp.float32)
        out[pl.ds(FIELDS + t, 1), :] = pair[pl.ds(1, 1), lanes].astype(jnp.float32)
        tile = tiles[t]
        head = tile.astype(jnp.bfloat16)
        heads[t] = head
        tails[t] = (tile - head.astype(jnp.float32)).astype(jnp.bfloat16)
        diag = jnp.sum(jnp.where(eye, tile, 0.0), axis=0, keepdims=True)
        out[pl.ds(2 * FIELDS + t, 1), :] = diag


def second_part(stride):
    me = lax.axis_index("parts")
    member, kind = me // stride, me % stride
    step = jnp.where(kind < stride // 2, 1, -1)
    return step, (member + step >= 0) & (member + step < GROUP)


def swapped(lists, other_lists, own, other, out):
    back = inverse(lists)
    place = jnp.maximum(back - 1, 0)
    slot = look_up(other_lists, place).astype(jnp.int32)
    lane = slot & (TILE - 1)
    block = jnp.where(back > 0, slot >> 7, -1)
    tables = [other[pl.ds(FIELDS * h, FIELDS), :] for h in range(CHUNKS)]
    for c in range(CHUNKS):
        rows = pl.ds(FIELDS * c, FIELDS)
        lane_c, block_c = wide(lane[c : c + 1]), wide(block[c : c + 1])
        found = own[rows, :]
        for h, table in enumerate(tables):
            found = jnp.where(block_c == h, take(table, lane_c), found)
        out[rows, :] = found


def compose_kernel(stride, raw, own, once, twice):
    member = lax.axis_index("parts") // stride
    step, exists = second_part(stride)

    def came_from(part):
        return raw.at[GROUP - 1 - part]

    def list_rows(part, level):
        rows = came_from(part)
        return [rows[pl.ds(LISTS_AT + 2 * level + h, 1), :] for h in range(2)]

    def level_step(level, part, apart, own_state, other_state, out):
        lists, others = list_rows(part, level), list_rows(part ^ apart, level)
        swapped(lists, others, own_state, other_state, out)

    for r in range(GROUP):
        level_step(0, r, 4, came_from(r), came_from(r ^ 4), once.at[r])
    second = (member + step + GROUP) % GROUP
    for i, part in enumerate((member, member ^ 1, second, second ^ 1)):
        level_step(1, part, 2, once.at[part], once.at[part ^ 2], twice.at[i])
    for i, part in enumerate((member, second)):
        level_step(2, part, 1, twice.at[2 * i], twice.at[2 * i + 1], own.at[i])
        own[i, pl.ds(RIM_AT, 1), :] = came_from(part)[pl.ds(RIM_AT, 1), :]
    for c in range(CHUNKS):
        rows = pl.ds(FIELDS * c, FIELDS)
        own[1, rows, :] = jnp.where(exists, own[1, rows, :], 0.0)


def join_kernel(stride, states, fixed, given, mine, far, low, high):
    kind = lax.axis_index("parts") % stride
    exists = second_part(stride)[1]
    early, outer = kind < stride // 2, (kind == 0) | (kind == stride - 1)
    for at in range(0, RECORD, FIELDS):
        rows = pl.ds(at, FIELDS)
        if at < FIRST_AT:
            one, two = states[0, rows, :], states[1, rows, :]
        else:
            part = pl.ds(at - FIRST_AT, FIELDS)
            absent = 1.0 if at == DIAG_AT else 0.0
            one, two = fixed[part, :], jnp.where(exists, given[part, :], absent)
        mine[rows, :] = one
        far[rows, :] = jnp.where(outer, two, one)
        low[rows, :] = jnp.where(early, one, two)
        high[rows, :] = jnp.where(early, two, one)


def gather_records(stride, parts, came, records):
    me = lax.axis_index("parts")
    swap = (stride == BLOCK) & (me % 2 == 0)
    mine, one, two, *side = came
    for at in range(0, RECORD, FIELDS):
        rows = pl.ds(at, FIELDS)
        blocks = {
            0: mine[rows, :],
            -1: jnp.where(swap, two[rows, :], one[rows, :]),
            1: jnp.where(swap, one[rows, :], two[rows, :]),
        }
        if side:
            blocks[-2], blocks[2] = side[0][rows, :], side[1][rows, :]
        for o, block in blocks.items():
            absent = 1.0 if at == DIAG_AT else 0.0
            there = (me + o >= 0) & (me + o < parts)
            records[o + REACH, rows, :] = jnp.where(there, block, absent) if o else block


def state_of(record):
    return [record[pl.ds(FIELDS * c, FIELDS), :] for c in range(CHUNKS)]


def ends_of(record):
    first = record[pl.ds(FIRST_AT, FIELDS), :].astype(jnp.int32)
    second = record[pl.ds(SECOND_AT, FIELDS), :].astype(jnp.int32)
    return first, second


def diag_of(record):
    return record[pl.ds(DIAG_AT, FIELDS), :]


def rim_of(record, blocks):
    slots = wide(record[pl.ds(RIM_AT, 1), :].astype(jnp.int32))
    lane, high = slots & (TILE - 1), slots >> 7
    found = take(blocks[0], lane)
    for c in range(1, CHUNKS):
        found = jnp.where(high == c, take(blocks[c], lane), found)
    return found


def difference(local, ghosts, field, first, second):
    near = [local[pl.ds(FIELDS * c + field, 1), :] for c in range(CHUNKS)]
    far = [one[pl.ds(field, 1), :] for one in ghosts]
    return look_up(near, first) - look_up(near + far if len(far) > 1 else far, second)


def first_lam(record, ghosts):
    first, second = ends_of(record)
    normal = [difference(record, ghosts, k, first, second) for k in range(3)]
    speed = sum(normal[k] * difference(record, ghosts, 3 + k, first, second) for k in range(3))
    return normal, jnp.maximum(0.0, -speed / diag_of(record))


def add_up(force, first, second, heads, rows):
    for k in range(3):
        head = force[k].astype(jnp.bfloat16).astype(jnp.float32)
        rows[pl.ds(k, FIELDS, stride=FIELDS), :] = force[k] - head
        rows[pl.ds(3 + k, FIELDS, stride=FIELDS), :] = head
    empty = jnp.zeros((FIELDS, TILE), jnp.float32)
    pad = [empty] * (len(heads) % 2)
    left, right = [], []
    for t in range(FIELDS):
        value = rows[pl.ds(FIELDS * t, FIELDS), :]
        for index, limit, signed in ((first, CHUNKS, value), (second, EXT_CHUNKS, -value)):
            if min(heads) >= limit:
                continue
            row = index[t : t + 1]
            high = wide(row >> 7)
            groups = [jnp.where(high == h, signed, 0.0) if h < limit else empty for h in heads]
            left.append(jnp.concatenate(groups + pad, axis=0))
            right.append(one_hot(row & (TILE - 1)))
    total = 0.0
    for k in range(0, len(left), 2):
        total += lax.dot_general(
            jnp.concatenate(left[k : k + 2], axis=1).astype(jnp.bfloat16),
            jnp.concatenate(right[k : k + 2], axis=1),
            NT,
            preferred_element_type=jnp.float32,
        )
    blocks = [total[FIELDS * k : FIELDS * (k + 1)] for k in range(len(heads))]
    return {h: block + pltpu.roll(block, 3, 0) for h, block in zip(heads, blocks)}


def moved(was, here, incoming, back_row):
    place = wide(back_row)
    extra = jnp.where(place > 0, take(incoming, jnp.maximum(place - 1, 0)), 0.0)
    field = rows_iota((FIELDS, TILE))
    gain = wide(was[6:7]) * (here + extra)
    return was + jnp.where((field >= 3) & (field < 6), gain, 0.0)


def near_kernel(stride, parts, *refs):
    came, (heads, tails, coupled, contacts, records, rims) = refs[:3], refs[3:]
    gather_records(stride, parts, came, records)
    for k in (-1, 1):
        record = records.at[REACH + k]
        rims[REACH + k] = rim_of(record, state_of(record))
    normal, lam = first_lam(records.at[REACH], (rims.at[REACH - 1], rims.at[REACH + 1]))
    for k, one in enumerate((*normal, lam)):
        contacts[k] = one
    head = lam.astype(jnp.bfloat16).astype(jnp.float32)
    both = jnp.concatenate([head, lam - head], axis=0).astype(jnp.bfloat16)
    total = jnp.zeros((FIELDS, TILE), jnp.float32)
    for t in range(heads.shape[0]):
        main = lax.dot_general(both, heads[t], NT, preferred_element_type=jnp.float32)
        rest = lax.dot_general(both, tails[t], NT, preferred_element_type=jnp.float32)
        whole = main[:FIELDS] + main[FIELDS:] + rest[:FIELDS]
        total = jnp.where(rows_iota((FIELDS, TILE)) == t, whole, total)
    coupled[...] = total


def middle_kernel(stride, parts, count, *refs):
    came, known = refs[:count], refs[count]
    stage, back_here, fixed_out, gathered, rims, rows, state_next, rims_next = refs[count + 1 :]
    gather_records(stride, parts, came, gathered)
    records = {o: gathered.at[o + REACH] for o in range(-REACH, REACH + 1)}
    rim = {o: rims.at[o + REACH] for o in records}
    rim_next = {o: rims_next.at[o + 1] for o in (-1, 0, 1)}
    left, right = CHUNKS, CHUNKS + 1
    local = list(range(CHUNKS))
    for o, record in records.items():
        rim[o][...] = rim_of(record, state_of(record))
    heads = {-2: [right], -1: local + [right], 0: local + [left, right], 1: local + [left], 2: [left]}
    ghosts = {o: (rim[o - 1], rim[o + 1]) for o in (-1, 1)}
    ghosts.update({-2: (rim[-1],), 2: (rim[1],)})
    sums, contacts = {}, {}
    for o, record in records.items():
        contacts[o] = first_lam(record, ghosts[o]) if o else ([known[k] for k in range(3)], known[3])
    for o, record in records.items():
        normal, lam = contacts[o]
        first, second = ends_of(record)
        force = [one * lam for one in normal]
        sums[o] = add_up(force, first, second, heads[o], rows.at[o + REACH])
    for o in (-1, 0, 1):
        incoming = sums[o - 1][right] + sums[o + 1][left]
        back = inverse([records[o][pl.ds(RIM_AT, 1), :]])
        if o == 0:
            back_here[...] = back
        blocks = [
            moved(was, sums[o][c], incoming, back[c : c + 1])
            for c, was in enumerate(state_of(records[o]))
        ]
        rim_next[o][...] = rim_of(records[o], blocks)
        for c in range(CHUNKS):
            state_next[o + 1, pl.ds(FIELDS * c, FIELDS), :] = blocks[c]
    ghosts = {-1: (rim_next[0],), 0: (rim_next[-1], rim_next[1]), 1: (rim_next[0],)}
    for o in (-1, 0, 1):
        normal, lam = contacts[o]
        first, second = ends_of(records[o])
        state = state_next.at[o + 1]
        speed = sum(
            normal[k] * difference(state, ghosts[o], 3 + k, first, second) for k in range(3)
        )
        for k in range(3):
            stage[o + 1, k] = normal[k]
        stage[o + 1, 3] = lam
        stage[o + 1, 4] = speed
        fixed_out[o + 1] = records[o][pl.ds(FIRST_AT, FIXED), :]


def last_kernel(
    parts, mine, stage, back, here, chip, mid, other, fixed, velocity, impulse, rows
):
    me = lax.axis_index("parts")
    odd = me % 2 == 1
    late = parts - EDGE
    apart = (me == EDGE) | (me == EDGE - 1) | (me == late) | (me == late - 1)
    across = jnp.where(apart, mid[...], other[...])
    across = jnp.where((me > 0) & (me < parts - 1), across, 0.0)
    coupled = {
        -1: jnp.where(odd, chip[...], across),
        0: here[...],
        1: jnp.where(odd, across, chip[...]),
    }
    sums = {}
    for o, heads in ((-1, [CHUNKS + 1]), (0, list(range(CHUNKS))), (1, [CHUNKS])):
        record = fixed.at[o + 1]
        lam = stage[o + 1, 3]
        diag = record[pl.ds(DIAG_AT - FIRST_AT, FIELDS), :]
        lam = jnp.maximum(0.0, lam - (coupled[o] + stage[o + 1, 4]) / diag)
        if o == 0:
            impulse[...] = lam
        first = record[pl.ds(0, FIELDS), :].astype(jnp.int32)
        second = record[pl.ds(SECOND_AT - FIRST_AT, FIELDS), :].astype(jnp.int32)
        force = [stage[o + 1, k] * lam for k in range(3)]
        sums[o] = add_up(force, first, second, heads, rows.at[o + 1])
    incoming = sums[-1][CHUNKS + 1] + sums[1][CHUNKS]
    for c, was in enumerate(state_of(mine)):
        block = moved(was, sums[0][c], incoming, back[pl.ds(c, 1), :])
        velocity[:, pl.ds(c * TILE, TILE)] = block[3:6]


def call(kernel, out_shape, inputs, name, space=pltpu.VMEM, scratch=()):
    many = isinstance(out_shape, (tuple, list))
    vmem = pl.BlockSpec(memory_space=pltpu.VMEM)
    return pl.pallas_call(
        kernel,
        out_shape=out_shape,
        in_specs=[pl.BlockSpec(memory_space=space)] * len(inputs),
        out_specs=[vmem] * len(out_shape) if many else vmem,
        scratch_shapes=list(scratch),
        compiler_params=FROM_HBM if space == pltpu.HBM else PARAMS,
        name=name,
    )(*inputs)


def second_parts(parts, stride):
    pairs = []
    for i in range(parts):
        step = -stride if i % stride < stride // 2 else stride
        to = i + step
        if not 0 <= to < parts:
            to = i + (stride // 2 if step < 0 else -(stride // 2))
        pairs.append((i, to))
    return pairs


def next_pairs(parts):
    late = parts - EDGE
    most = {i: i + 1 if i % 2 else i - 1 for i in range(parts)}
    edge = {i: i ^ 1 for i in range(parts)}
    for i, j in ((0, EDGE), (EDGE - 1, late - 1), (late, parts - 1)):
        most[i], most[j] = j, i
    for at in (EDGE, late):
        for i, j in ((at - 1, at), (at - 2, at + 2), (at + 1, at + 3)):
            edge[i], edge[j] = j, i
    return list(most.items()), list(edge.items())


def body(positions, velocity, inv_mass, swap_lists, rim_list, contact_pair, delassus):
    parts = lax.axis_size("parts")
    stride = parts // GROUP
    grains = positions.shape[1]
    contacts = contact_pair.shape[1]
    tiles = delassus.shape[0]
    reach = 2 * REACH + 1
    float32 = functools.partial(jax.ShapeDtypeStruct, dtype=jnp.float32)
    vmem = lambda *shape: pltpu.VMEM(shape, jnp.float32)
    send = functools.partial(lax.ppermute, axis_name="parts")
    inputs = (
        positions,
        velocity,
        inv_mass.reshape(CHUNKS, TILE),
        swap_lists,
        rim_list.reshape(1, TILE),
    )
    packed = call(
        pack_kernel,
        float32((GROUP, RAW, TILE)),
        inputs,
        "pack",
        pltpu.HBM,
        [pltpu.VMEM(one.shape, one.dtype) for one in inputs]
        + [pltpu.SemaphoreType.DMA((5,))],
    )
    classes = [[r + stride * (GROUP - 1 - k) for k in range(GROUP)] for r in range(stride)]
    raw = lax.all_to_all(packed, "parts", 0, 0, axis_index_groups=classes)

    half = jax.ShapeDtypeStruct(delassus.shape, jnp.bfloat16)
    fixed, heads, tails = call(
        fixed_kernel, (float32((FIXED, TILE)), half, half), (contact_pair, delassus), "fixed"
    )
    given = send(fixed, perm=second_parts(parts, stride))

    states = call(
        functools.partial(compose_kernel, stride),
        float32((2, FIRST_AT, TILE)),
        (raw,),
        "compose",
        scratch=[vmem(GROUP, FIRST_AT, TILE), vmem(4, FIRST_AT, TILE)],
    )
    record = (RECORD, TILE)
    mine, far, low, high = call(
        functools.partial(join_kernel, stride),
        [float32(record)] * 4,
        (states, fixed, given),
        "join",
    )
    within = [(i, i ^ 1) for i in range(parts)]
    if stride == BLOCK:
        from_far = send(far, perm=[(i, i ^ 3) for i in range(parts)])
        near = (mine, send(mine, perm=within), from_far)
        beyond = [(i, i ^ 2) for i in range(parts)]
        came = (*near, send(low, perm=beyond), send(high, perm=beyond))
    else:
        shifts = [[(i, (i + by) % parts) for i in range(parts)] for by in (1, -1, 2, -2)]
        came = (mine, *[send(mine, perm=shift) for shift in shifts])
        near = came[:3]

    here, known = call(
        functools.partial(near_kernel, stride, parts),
        (float32((tiles, TILE)), float32((4, tiles, TILE))),
        (*near, heads, tails),
        "near",
        scratch=[vmem(reach, *record), vmem(reach, FIELDS, TILE)],
    )
    most, edge = next_pairs(parts)
    other = send(here, perm=most)
    chip = send(here, perm=within)
    mid = send(here, perm=edge)
    stage, back, contact_rows = call(
        functools.partial(middle_kernel, stride, parts, len(came)),
        (
            float32((3, 5, FIELDS, TILE)),
            jax.ShapeDtypeStruct((FIELDS, TILE), jnp.int32),
            float32((3, FIXED, TILE)),
        ),
        (*came, known),
        "middle",
        scratch=[
            vmem(reach, *record),
            vmem(reach, FIELDS, TILE),
            vmem(reach, FIELDS * FIELDS, TILE),
            vmem(3, CHUNKS * FIELDS, TILE),
            vmem(3, FIELDS, TILE),
        ],
    )
    new_velocity, impulse = call(
        functools.partial(last_kernel, parts),
        (float32((3, grains)), float32((tiles, TILE))),
        (mine, stage, back, here, chip, mid, other, contact_rows),
        "last",
        scratch=[vmem(3, FIELDS * FIELDS, TILE)],
    )
    return (new_velocity, impulse.reshape(contacts))


def solution(mesh):
    in_specs = (
        P(None, "parts"),
        P(None, "parts"),
        P("parts"),
        P(None, "parts"),
        P("parts"),
        P(None, "parts"),
        P("parts", None, None),
    )
    out_specs = (P(None, "parts"), P("parts"))
    return jax.shard_map(body, mesh=mesh, in_specs=in_specs, out_specs=out_specs, check_vma=False)
```

```python
import functools

import jax
import jax.numpy as jnp
from jax import lax
from jax.experimental import pallas as pl
from jax.experimental.pallas import tpu as pltpu
from jax.sharding import PartitionSpec as P

TILE = 128
LEVELS = 3
GROUP = 2**LEVELS
REACH = 2
FIELDS = 8
CHUNKS = 4
EXT_CHUNKS = 6
RIM_AT = 7
FIRST_AT = 32
SECOND_AT = 40
DIAG_AT = 48
RECORD = 56
LISTS_AT = 32
RAW = 40
FIXED = RECORD - FIRST_AT
BLOCK = 4
PARAMS = pltpu.CompilerParams(vmem_limit_bytes=32 * 2**20)
FROM_HBM = pltpu.CompilerParams(vmem_limit_bytes=63 * 2**20)
NT = (((1,), (1,)), ((), ()))


def rows_iota(shape):
    return lax.broadcasted_iota(jnp.int32, shape, 0)


def lanes_iota(shape):
    return lax.broadcasted_iota(jnp.int32, shape, 1)


def wide(row):
    return jnp.broadcast_to(row, (FIELDS, TILE))


def take(table, lane):
    return jnp.take_along_axis(table, lane, axis=1, mode="promise_in_bounds")


def look_up(rows, index):
    lane, high = index & (TILE - 1), index >> 7
    found = take(wide(rows[0]), lane)
    for h in range(1, len(rows)):
        found = jnp.where(high == h, take(wide(rows[h]), lane), found)
    return found


def one_hot(low_row):
    row = jnp.broadcast_to(low_row.astype(jnp.float32).astype(jnp.bfloat16), (TILE, TILE))
    column = rows_iota((TILE, TILE)).astype(jnp.float32).astype(jnp.bfloat16)
    return jnp.where(row == column, jnp.bfloat16(1), jnp.bfloat16(0))


def inverse(slot_rows):
    left, right = [], []
    for at, row in enumerate(slot_rows):
        slots = row.astype(jnp.int32)
        place = (lanes_iota((FIELDS, TILE)) + (at * TILE + 1)).astype(jnp.float32)
        heads = jnp.where(wide(slots >> 7) == rows_iota((FIELDS, TILE)), place, 0.0)
        left.append(heads.astype(jnp.bfloat16))
        right.append(one_hot(slots & (TILE - 1)))
    total = lax.dot_general(
        jnp.concatenate(left, axis=1),
        jnp.concatenate(right, axis=1),
        NT,
        preferred_element_type=jnp.float32,
    )
    return total.astype(jnp.int32)


def pack_kernel(*refs):
    sources, out, held, sems = refs[:5], refs[5], refs[6:11], refs[11]
    copies = [
        pltpu.make_async_copy(source, target, sems.at[k])
        for k, (source, target) in enumerate(zip(sources, held))
    ]
    for copy in copies:
        copy.start()
    pos, vel, mass, lists, rim = held
    for copy in copies:
        copy.wait()
    first = out.at[0]
    for c in range(CHUNKS):
        lanes = pl.ds(c * TILE, TILE)
        first[pl.ds(FIELDS * c, 3), :] = pos[:, lanes]
        first[pl.ds(FIELDS * c + 3, 3), :] = vel[:, lanes]
        first[pl.ds(FIELDS * c + 6, 1), :] = mass[pl.ds(c, 1), :]
        spare = rim[...].astype(jnp.float32) if c == 0 else jnp.zeros((1, TILE), jnp.float32)
        first[pl.ds(FIELDS * c + 7, 1), :] = spare
    for level in range(LEVELS):
        for h in range(2):
            row = lists[pl.ds(level, 1), pl.ds(h * TILE, TILE)]
            first[pl.ds(LISTS_AT + 2 * level + h, 1), :] = row.astype(jnp.float32)
    first[pl.ds(LISTS_AT + 2 * LEVELS, 2), :] = jnp.zeros((2, TILE), jnp.float32)
    whole = first[...]
    for m in range(1, GROUP):
        out[m] = whole


def fixed_kernel(pair, tiles, out, heads, tails):
    eye = rows_iota((TILE, TILE)) == lanes_iota((TILE, TILE))
    for t in range(tiles.shape[0]):
        lanes = pl.ds(t * TILE, TILE)
        out[pl.ds(t, 1), :] = pair[pl.ds(0, 1), lanes].astype(jnp.float32)
        out[pl.ds(FIELDS + t, 1), :] = pair[pl.ds(1, 1), lanes].astype(jnp.float32)
        tile = tiles[t]
        turned = tile.T
        head = turned.astype(jnp.bfloat16)
        heads[t] = head
        tails[t] = (turned - head.astype(jnp.float32)).astype(jnp.bfloat16)
        diag = jnp.sum(jnp.where(eye, tile, 0.0), axis=0, keepdims=True)
        out[pl.ds(2 * FIELDS + t, 1), :] = diag


def second_part(stride):
    me = lax.axis_index("parts")
    member, kind = me // stride, me % stride
    step = jnp.where(kind < stride // 2, 1, -1)
    return step, (member + step >= 0) & (member + step < GROUP)


def swapped(lists, other_lists, own, other, out):
    back = inverse(lists)
    place = jnp.maximum(back - 1, 0)
    slot = look_up(other_lists, place).astype(jnp.int32)
    lane = slot & (TILE - 1)
    block = jnp.where(back > 0, slot >> 7, -1)
    tables = [other[pl.ds(FIELDS * h, FIELDS), :] for h in range(CHUNKS)]
    for c in range(CHUNKS):
        rows = pl.ds(FIELDS * c, FIELDS)
        lane_c, block_c = wide(lane[c : c + 1]), wide(block[c : c + 1])
        found = own[rows, :]
        for h, table in enumerate(tables):
            found = jnp.where(block_c == h, take(table, lane_c), found)
        out[rows, :] = found


def compose_kernel(stride, raw, own, once, twice):
    member = lax.axis_index("parts") // stride
    step, exists = second_part(stride)

    def came_from(part):
        return raw.at[GROUP - 1 - part]

    def list_rows(part, level):
        rows = came_from(part)
        return [rows[pl.ds(LISTS_AT + 2 * level + h, 1), :] for h in range(2)]

    def level_step(level, part, apart, own_state, other_state, out):
        lists, others = list_rows(part, level), list_rows(part ^ apart, level)
        swapped(lists, others, own_state, other_state, out)

    for r in range(GROUP):
        level_step(0, r, 4, came_from(r), came_from(r ^ 4), once.at[r])
    second = (member + step + GROUP) % GROUP
    for i, part in enumerate((member, member ^ 1, second, second ^ 1)):
        level_step(1, part, 2, once.at[part], once.at[part ^ 2], twice.at[i])
    for i, part in enumerate((member, second)):
        level_step(2, part, 1, twice.at[2 * i], twice.at[2 * i + 1], own.at[i])
        own[i, pl.ds(RIM_AT, 1), :] = came_from(part)[pl.ds(RIM_AT, 1), :]
    for c in range(CHUNKS):
        rows = pl.ds(FIELDS * c, FIELDS)
        own[1, rows, :] = jnp.where(exists, own[1, rows, :], 0.0)


def join_kernel(stride, states, fixed, given, mine, far, low, high):
    kind = lax.axis_index("parts") % stride
    exists = second_part(stride)[1]
    early, outer = kind < stride // 2, (kind == 0) | (kind == stride - 1)
    for at in range(0, RECORD, FIELDS):
        rows = pl.ds(at, FIELDS)
        if at < FIRST_AT:
            one, two = states[0, rows, :], states[1, rows, :]
        else:
            part = pl.ds(at - FIRST_AT, FIELDS)
            absent = 1.0 if at == DIAG_AT else 0.0
            one, two = fixed[part, :], jnp.where(exists, given[part, :], absent)
        mine[rows, :] = one
        far[rows, :] = jnp.where(outer, two, one)
        low[rows, :] = jnp.where(early, one, two)
        high[rows, :] = jnp.where(early, two, one)


def gather_records(stride, parts, came, records):
    me = lax.axis_index("parts")
    swap = (stride == BLOCK) & (me % 2 == 0)
    mine, one, two, *side = came
    for at in range(0, RECORD, FIELDS):
        rows = pl.ds(at, FIELDS)
        blocks = {
            0: mine[rows, :],
            -1: jnp.where(swap, two[rows, :], one[rows, :]),
            1: jnp.where(swap, one[rows, :], two[rows, :]),
        }
        if side:
            blocks[-2], blocks[2] = side[0][rows, :], side[1][rows, :]
        for o, block in blocks.items():
            absent = 1.0 if at == DIAG_AT else 0.0
            there = (me + o >= 0) & (me + o < parts)
            records[o + REACH, rows, :] = jnp.where(there, block, absent) if o else block


def state_of(record):
    return [record[pl.ds(FIELDS * c, FIELDS), :] for c in range(CHUNKS)]


def ends_of(record):
    first = record[pl.ds(FIRST_AT, FIELDS), :].astype(jnp.int32)
    second = record[pl.ds(SECOND_AT, FIELDS), :].astype(jnp.int32)
    return first, second


def diag_of(record):
    return record[pl.ds(DIAG_AT, FIELDS), :]


def rim_of(record, blocks):
    slots = wide(record[pl.ds(RIM_AT, 1), :].astype(jnp.int32))
    lane, high = slots & (TILE - 1), slots >> 7
    found = take(blocks[0], lane)
    for c in range(1, CHUNKS):
        found = jnp.where(high == c, take(blocks[c], lane), found)
    return found


def difference(local, ghosts, field, first, second):
    near = [local[pl.ds(FIELDS * c + field, 1), :] for c in range(CHUNKS)]
    far = [one[pl.ds(field, 1), :] for one in ghosts]
    return look_up(near, first) - look_up(near + far if len(far) > 1 else far, second)


def first_lam(record, ghosts):
    first, second = ends_of(record)
    normal = [difference(record, ghosts, k, first, second) for k in range(3)]
    speed = sum(normal[k] * difference(record, ghosts, 3 + k, first, second) for k in range(3))
    return normal, jnp.maximum(0.0, -speed / diag_of(record))


def add_up(force, first, second, heads, rows):
    for k in range(3):
        head = force[k].astype(jnp.bfloat16).astype(jnp.float32)
        rows[pl.ds(k, FIELDS, stride=FIELDS), :] = force[k] - head
        rows[pl.ds(3 + k, FIELDS, stride=FIELDS), :] = head
    empty = jnp.zeros((FIELDS, TILE), jnp.float32)
    pad = [empty] * (len(heads) % 2)
    left, right = [], []
    for t in range(FIELDS):
        value = rows[pl.ds(FIELDS * t, FIELDS), :]
        for index, limit, signed in ((first, CHUNKS, value), (second, EXT_CHUNKS, -value)):
            if min(heads) >= limit:
                continue
            row = index[t : t + 1]
            high = wide(row >> 7)
            groups = [jnp.where(high == h, signed, 0.0) if h < limit else empty for h in heads]
            left.append(jnp.concatenate(groups + pad, axis=0))
            right.append(one_hot(row & (TILE - 1)))
    total = 0.0
    for k in range(0, len(left), 2):
        total += lax.dot_general(
            jnp.concatenate(left[k : k + 2], axis=1).astype(jnp.bfloat16),
            jnp.concatenate(right[k : k + 2], axis=1),
            NT,
            preferred_element_type=jnp.float32,
        )
    blocks = [total[FIELDS * k : FIELDS * (k + 1)] for k in range(len(heads))]
    return {h: block + pltpu.roll(block, 3, 0) for h, block in zip(heads, blocks)}


def moved(was, here, incoming, back_row):
    place = wide(back_row)
    extra = jnp.where(place > 0, take(incoming, jnp.maximum(place - 1, 0)), 0.0)
    field = rows_iota((FIELDS, TILE))
    gain = wide(was[6:7]) * (here + extra)
    return was + jnp.where((field >= 3) & (field < 6), gain, 0.0)


def near_kernel(stride, parts, *refs):
    came, (heads, tails, coupled, contacts, records, rims) = refs[:3], refs[3:]
    gather_records(stride, parts, came, records)
    for k in (-1, 1):
        record = records.at[REACH + k]
        rims[REACH + k] = rim_of(record, state_of(record))
    normal, lam = first_lam(records.at[REACH], (rims.at[REACH - 1], rims.at[REACH + 1]))
    for k, one in enumerate((*normal, lam)):
        contacts[k] = one
    head = lam.astype(jnp.bfloat16).astype(jnp.float32)
    both = jnp.concatenate([head, lam - head], axis=0).astype(jnp.bfloat16)
    total = jnp.zeros((FIELDS, TILE), jnp.float32)
    for t in range(heads.shape[0]):
        main = jnp.dot(both, heads[t], preferred_element_type=jnp.float32)
        rest = jnp.dot(both, tails[t], preferred_element_type=jnp.float32)
        whole = main[:FIELDS] + main[FIELDS:] + rest[:FIELDS]
        total = jnp.where(rows_iota((FIELDS, TILE)) == t, whole, total)
    coupled[...] = total


def middle_kernel(stride, parts, count, *refs):
    came, known = refs[:count], refs[count]
    stage, back_here, fixed_out, gathered, rims, rows, state_next, rims_next = refs[count + 1 :]
    gather_records(stride, parts, came, gathered)
    records = {o: gathered.at[o + REACH] for o in range(-REACH, REACH + 1)}
    rim = {o: rims.at[o + REACH] for o in records}
    rim_next = {o: rims_next.at[o + 1] for o in (-1, 0, 1)}
    left, right = CHUNKS, CHUNKS + 1
    local = list(range(CHUNKS))
    for o, record in records.items():
        rim[o][...] = rim_of(record, state_of(record))
    heads = {-2: [right], -1: local + [right], 0: local + [left, right], 1: local + [left], 2: [left]}
    ghosts = {o: (rim[o - 1], rim[o + 1]) for o in (-1, 1)}
    ghosts.update({-2: (rim[-1],), 2: (rim[1],)})
    sums, contacts = {}, {}
    for o, record in records.items():
        contacts[o] = first_lam(record, ghosts[o]) if o else ([known[k] for k in range(3)], known[3])
    for o, record in records.items():
        normal, lam = contacts[o]
        first, second = ends_of(record)
        force = [one * lam for one in normal]
        sums[o] = add_up(force, first, second, heads[o], rows.at[o + REACH])
    for o in (-1, 0, 1):
        incoming = sums[o - 1][right] + sums[o + 1][left]
        back = inverse([records[o][pl.ds(RIM_AT, 1), :]])
        if o == 0:
            back_here[...] = back
        blocks = [
            moved(was, sums[o][c], incoming, back[c : c + 1])
            for c, was in enumerate(state_of(records[o]))
        ]
        rim_next[o][...] = rim_of(records[o], blocks)
        for c in range(CHUNKS):
            state_next[o + 1, pl.ds(FIELDS * c, FIELDS), :] = blocks[c]
    ghosts = {-1: (rim_next[0],), 0: (rim_next[-1], rim_next[1]), 1: (rim_next[0],)}
    for o in (-1, 0, 1):
        normal, lam = contacts[o]
        first, second = ends_of(records[o])
        state = state_next.at[o + 1]
        speed = sum(
            normal[k] * difference(state, ghosts[o], 3 + k, first, second) for k in range(3)
        )
        for k in range(3):
            stage[o + 1, k] = normal[k]
        stage[o + 1, 3] = lam
        stage[o + 1, 4] = speed
        fixed_out[o + 1] = records[o][pl.ds(FIRST_AT, FIXED), :]


def last_kernel(
    parts, mine, stage, back, here, chip, mid, other, fixed, velocity, impulse, rows
):
    me = lax.axis_index("parts")
    odd = me % 2 == 1
    apart = (me % (2 * BLOCK) == BLOCK) | (me % (2 * BLOCK) == BLOCK - 1)
    across = jnp.where(apart, mid[...], other[...])
    across = jnp.where((me > 0) & (me < parts - 1), across, 0.0)
    coupled = {
        -1: jnp.where(odd, chip[...], across),
        0: here[...],
        1: jnp.where(odd, across, chip[...]),
    }
    sums = {}
    for o, heads in ((-1, [CHUNKS + 1]), (0, list(range(CHUNKS))), (1, [CHUNKS])):
        record = fixed.at[o + 1]
        lam = stage[o + 1, 3]
        diag = record[pl.ds(DIAG_AT - FIRST_AT, FIELDS), :]
        lam = jnp.maximum(0.0, lam - (coupled[o] + stage[o + 1, 4]) / diag)
        if o == 0:
            impulse[...] = lam
        first = record[pl.ds(0, FIELDS), :].astype(jnp.int32)
        second = record[pl.ds(SECOND_AT - FIRST_AT, FIELDS), :].astype(jnp.int32)
        force = [stage[o + 1, k] * lam for k in range(3)]
        sums[o] = add_up(force, first, second, heads, rows.at[o + 1])
    incoming = sums[-1][CHUNKS + 1] + sums[1][CHUNKS]
    for c, was in enumerate(state_of(mine)):
        block = moved(was, sums[0][c], incoming, back[pl.ds(c, 1), :])
        velocity[:, pl.ds(c * TILE, TILE)] = block[3:6]


def call(kernel, out_shape, inputs, name, space=pltpu.VMEM, scratch=()):
    many = isinstance(out_shape, (tuple, list))
    vmem = pl.BlockSpec(memory_space=pltpu.VMEM)
    return pl.pallas_call(
        kernel,
        out_shape=out_shape,
        in_specs=[pl.BlockSpec(memory_space=space)] * len(inputs),
        out_specs=[vmem] * len(out_shape) if many else vmem,
        scratch_shapes=list(scratch),
        compiler_params=FROM_HBM if space == pltpu.HBM else PARAMS,
        name=name,
    )(*inputs)


def second_parts(parts, stride):
    pairs = []
    for i in range(parts):
        step = -stride if i % stride < stride // 2 else stride
        to = i + step
        if not 0 <= to < parts:
            to = i + (stride // 2 if step < 0 else -(stride // 2))
        pairs.append((i, to))
    return pairs


def edges(parts):
    return range(BLOCK, parts, 2 * BLOCK)


def next_pairs(parts):
    most = {i: i + 1 if i % 2 else i - 1 for i in range(parts)}
    edge = {i: i ^ 1 for i in range(parts)}
    ends = [0]
    for at in edges(parts):
        ends += [at - 1, at]
        for i, j in ((at - 1, at), (at - 2, at + 2), (at + 1, at + 3)):
            edge[i], edge[j] = j, i
    ends.append(parts - 1)
    closings = [(0, BLOCK), (ends[-2], parts - 1)]
    for k in range(1, len(ends) - 4, 2):
        closings.append((ends[k], ends[k + 2]) if k % 4 == 1 else (ends[k + 1], ends[k + 3]))
    for i, j in closings:
        most[i], most[j] = j, i
    return list(most.items()), list(edge.items())


def body(positions, velocity, inv_mass, swap_lists, rim_list, contact_pair, delassus):
    parts = lax.axis_size("parts")
    stride = parts // GROUP
    grains = positions.shape[1]
    contacts = contact_pair.shape[1]
    tiles = delassus.shape[0]
    reach = 2 * REACH + 1
    float32 = functools.partial(jax.ShapeDtypeStruct, dtype=jnp.float32)
    vmem = lambda *shape: pltpu.VMEM(shape, jnp.float32)
    send = functools.partial(lax.ppermute, axis_name="parts")
    inputs = (
        positions,
        velocity,
        inv_mass.reshape(CHUNKS, TILE),
        swap_lists,
        rim_list.reshape(1, TILE),
    )
    packed = call(
        pack_kernel,
        float32((GROUP, RAW, TILE)),
        inputs,
        "pack",
        pltpu.HBM,
        [pltpu.VMEM(one.shape, one.dtype) for one in inputs]
        + [pltpu.SemaphoreType.DMA((5,))],
    )
    classes = [[r + stride * (GROUP - 1 - k) for k in range(GROUP)] for r in range(stride)]
    raw = lax.all_to_all(packed, "parts", 0, 0, axis_index_groups=classes)

    half = jax.ShapeDtypeStruct(delassus.shape, jnp.bfloat16)
    fixed, heads, tails = call(
        fixed_kernel, (float32((FIXED, TILE)), half, half), (contact_pair, delassus), "fixed"
    )
    given = send(fixed, perm=second_parts(parts, stride))

    states = call(
        functools.partial(compose_kernel, stride),
        float32((2, FIRST_AT, TILE)),
        (raw,),
        "compose",
        scratch=[vmem(GROUP, FIRST_AT, TILE), vmem(4, FIRST_AT, TILE)],
    )
    record = (RECORD, TILE)
    mine, far, low, high = call(
        functools.partial(join_kernel, stride),
        [float32(record)] * 4,
        (states, fixed, given),
        "join",
    )
    within = [(i, i ^ 1) for i in range(parts)]
    if stride == BLOCK:
        from_far = send(far, perm=[(i, i ^ 3) for i in range(parts)])
        near = (mine, send(mine, perm=within), from_far)
        beyond = [(i, i ^ 2) for i in range(parts)]
        came = (*near, send(low, perm=beyond), send(high, perm=beyond))
    else:
        shifts = [[(i, (i + by) % parts) for i in range(parts)] for by in (1, -1, 2, -2)]
        came = (mine, *[send(mine, perm=shift) for shift in shifts])
        near = came[:3]

    here, known = call(
        functools.partial(near_kernel, stride, parts),
        (float32((tiles, TILE)), float32((4, tiles, TILE))),
        (*near, heads, tails),
        "near",
        scratch=[vmem(reach, *record), vmem(reach, FIELDS, TILE)],
    )
    most, edge = next_pairs(parts)
    other = send(here, perm=most)
    chip = send(here, perm=within)
    mid = send(here, perm=edge)
    stage, back, contact_rows = call(
        functools.partial(middle_kernel, stride, parts, len(came)),
        (
            float32((3, 5, FIELDS, TILE)),
            jax.ShapeDtypeStruct((FIELDS, TILE), jnp.int32),
            float32((3, FIXED, TILE)),
        ),
        (*came, known),
        "middle",
        scratch=[
            vmem(reach, *record),
            vmem(reach, FIELDS, TILE),
            vmem(reach, FIELDS * FIELDS, TILE),
            vmem(3, CHUNKS * FIELDS, TILE),
            vmem(3, FIELDS, TILE),
        ],
    )
    new_velocity, impulse = call(
        functools.partial(last_kernel, parts),
        (float32((3, grains)), float32((tiles, TILE))),
        (mine, stage, back, here, chip, mid, other, contact_rows),
        "last",
        scratch=[vmem(3, FIELDS * FIELDS, TILE)],
    )
    return (new_velocity, impulse.reshape(contacts))


def solution(mesh):
    in_specs = (
        P(None, "parts"),
        P(None, "parts"),
        P("parts"),
        P(None, "parts"),
        P("parts"),
        P(None, "parts"),
        P("parts", None, None),
    )
    out_specs = (P(None, "parts"), P("parts"))
    return jax.shard_map(body, mesh=mesh, in_specs=in_specs, out_specs=out_specs, check_vma=False)
```

```python
import functools

import jax
import jax.numpy as jnp
from jax import lax
from jax.experimental import pallas as pl
from jax.experimental.pallas import tpu as pltpu
from jax.sharding import PartitionSpec as P

TILE = 128
LEVELS = 3
GROUP = 2**LEVELS
REACH = 2
FIELDS = 8
CHUNKS = 4
EXT_CHUNKS = 6
RIM_AT = 7
FIRST_AT = 32
SECOND_AT = 40
DIAG_AT = 48
RECORD = 56
LISTS_AT = 32
RAW = 40
FIXED = RECORD - FIRST_AT
BLOCK = 4
PARAMS = pltpu.CompilerParams(vmem_limit_bytes=32 * 2**20)
FROM_HBM = pltpu.CompilerParams(vmem_limit_bytes=63 * 2**20)
NT = (((1,), (1,)), ((), ()))


def rows_iota(shape):
    return lax.broadcasted_iota(jnp.int32, shape, 0)


def lanes_iota(shape):
    return lax.broadcasted_iota(jnp.int32, shape, 1)


def wide(row):
    return jnp.broadcast_to(row, (FIELDS, TILE))


def take(table, lane):
    return jnp.take_along_axis(table, lane, axis=1, mode="promise_in_bounds")


def look_up(rows, index):
    lane, high = index & (TILE - 1), index >> 7
    found = take(wide(rows[0]), lane)
    for h in range(1, len(rows)):
        found = jnp.where(high == h, take(wide(rows[h]), lane), found)
    return found


def one_hot(low_row):
    row = jnp.broadcast_to(low_row.astype(jnp.float32).astype(jnp.bfloat16), (TILE, TILE))
    column = rows_iota((TILE, TILE)).astype(jnp.float32).astype(jnp.bfloat16)
    return jnp.where(row == column, jnp.bfloat16(1), jnp.bfloat16(0))


def inverse(slot_rows):
    left, right = [], []
    for at, row in enumerate(slot_rows):
        slots = row.astype(jnp.int32)
        place = (lanes_iota((FIELDS, TILE)) + (at * TILE + 1)).astype(jnp.float32)
        heads = jnp.where(wide(slots >> 7) == rows_iota((FIELDS, TILE)), place, 0.0)
        left.append(heads.astype(jnp.bfloat16))
        right.append(one_hot(slots & (TILE - 1)))
    total = lax.dot_general(
        jnp.concatenate(left, axis=1),
        jnp.concatenate(right, axis=1),
        NT,
        preferred_element_type=jnp.float32,
    )
    return total.astype(jnp.int32)


def pack_kernel(*refs):
    sources, out, held, sems = refs[:5], refs[5], refs[6:11], refs[11]
    copies = [
        pltpu.make_async_copy(source, target, sems.at[k])
        for k, (source, target) in enumerate(zip(sources, held))
    ]
    for copy in copies:
        copy.start()
    pos, vel, mass, lists, rim = held
    for copy in copies:
        copy.wait()
    first = out.at[0]
    for c in range(CHUNKS):
        lanes = pl.ds(c * TILE, TILE)
        first[pl.ds(FIELDS * c, 3), :] = pos[:, lanes]
        first[pl.ds(FIELDS * c + 3, 3), :] = vel[:, lanes]
        first[pl.ds(FIELDS * c + 6, 1), :] = mass[pl.ds(c, 1), :]
        spare = rim[...].astype(jnp.float32) if c == 0 else jnp.zeros((1, TILE), jnp.float32)
        first[pl.ds(FIELDS * c + 7, 1), :] = spare
    for level in range(LEVELS):
        for h in range(2):
            row = lists[pl.ds(level, 1), pl.ds(h * TILE, TILE)]
            first[pl.ds(LISTS_AT + 2 * level + h, 1), :] = row.astype(jnp.float32)
    first[pl.ds(LISTS_AT + 2 * LEVELS, 2), :] = jnp.zeros((2, TILE), jnp.float32)
    whole = first[...]
    for m in range(1, GROUP):
        out[m] = whole


def fixed_kernel(pair, tiles, out, heads, tails):
    eye = rows_iota((TILE, TILE)) == lanes_iota((TILE, TILE))
    for t in range(tiles.shape[0]):
        lanes = pl.ds(t * TILE, TILE)
        out[pl.ds(t, 1), :] = pair[pl.ds(0, 1), lanes].astype(jnp.float32)
        out[pl.ds(FIELDS + t, 1), :] = pair[pl.ds(1, 1), lanes].astype(jnp.float32)
        tile = tiles[t]
        turned = tile.T
        head = turned.astype(jnp.bfloat16)
        heads[t] = head
        tails[t] = (turned - head.astype(jnp.float32)).astype(jnp.bfloat16)
        diag = jnp.sum(jnp.where(eye, tile, 0.0), axis=0, keepdims=True)
        out[pl.ds(2 * FIELDS + t, 1), :] = diag


def second_part(stride):
    me = lax.axis_index("parts")
    member, kind = me // stride, me % stride
    step = jnp.where(kind < stride // 2, 1, -1)
    return step, (member + step >= 0) & (member + step < GROUP)


def swapped(lists, other_lists, own, other, out):
    back = inverse(lists)
    place = jnp.maximum(back - 1, 0)
    slot = look_up(other_lists, place).astype(jnp.int32)
    lane = slot & (TILE - 1)
    block = jnp.where(back > 0, slot >> 7, -1)
    tables = [other[pl.ds(FIELDS * h, FIELDS), :] for h in range(CHUNKS)]
    for c in range(CHUNKS):
        rows = pl.ds(FIELDS * c, FIELDS)
        lane_c, block_c = wide(lane[c : c + 1]), wide(block[c : c + 1])
        found = own[rows, :]
        for h, table in enumerate(tables):
            found = jnp.where(block_c == h, take(table, lane_c), found)
        out[rows, :] = found


def compose_kernel(stride, raw, own, once, twice):
    member = lax.axis_index("parts") // stride
    step, exists = second_part(stride)

    def came_from(part):
        return raw.at[(part + 2) % GROUP]

    def list_rows(part, level):
        rows = came_from(part)
        return [rows[pl.ds(LISTS_AT + 2 * level + h, 1), :] for h in range(2)]

    def level_step(level, part, apart, own_state, other_state, out):
        lists, others = list_rows(part, level), list_rows(part ^ apart, level)
        swapped(lists, others, own_state, other_state, out)

    for r in range(GROUP):
        level_step(0, r, 4, came_from(r), came_from(r ^ 4), once.at[r])
    second = (member + step + GROUP) % GROUP
    for i, part in enumerate((member, member ^ 1, second, second ^ 1)):
        level_step(1, part, 2, once.at[part], once.at[part ^ 2], twice.at[i])
    for i, part in enumerate((member, second)):
        level_step(2, part, 1, twice.at[2 * i], twice.at[2 * i + 1], own.at[i])
        own[i, pl.ds(RIM_AT, 1), :] = came_from(part)[pl.ds(RIM_AT, 1), :]
    for c in range(CHUNKS):
        rows = pl.ds(FIELDS * c, FIELDS)
        own[1, rows, :] = jnp.where(exists, own[1, rows, :], 0.0)


def join_kernel(stride, states, fixed, given, mine, far, low, high):
    kind = lax.axis_index("parts") % stride
    exists = second_part(stride)[1]
    early, outer = kind < stride // 2, (kind == 0) | (kind == stride - 1)
    for at in range(0, RECORD, FIELDS):
        rows = pl.ds(at, FIELDS)
        if at < FIRST_AT:
            one, two = states[0, rows, :], states[1, rows, :]
        else:
            part = pl.ds(at - FIRST_AT, FIELDS)
            absent = 1.0 if at == DIAG_AT else 0.0
            one, two = fixed[part, :], jnp.where(exists, given[part, :], absent)
        mine[rows, :] = one
        far[rows, :] = jnp.where(outer, two, one)
        low[rows, :] = jnp.where(early, one, two)
        high[rows, :] = jnp.where(early, two, one)


def gather_records(stride, parts, came, records):
    me = lax.axis_index("parts")
    swap = (stride == BLOCK) & (me % 2 == 0)
    mine, one, two, *side = came
    for at in range(0, RECORD, FIELDS):
        rows = pl.ds(at, FIELDS)
        blocks = {
            0: mine[rows, :],
            -1: jnp.where(swap, two[rows, :], one[rows, :]),
            1: jnp.where(swap, one[rows, :], two[rows, :]),
        }
        if side:
            blocks[-2], blocks[2] = side[0][rows, :], side[1][rows, :]
        for o, block in blocks.items():
            absent = 1.0 if at == DIAG_AT else 0.0
            there = (me + o >= 0) & (me + o < parts)
            records[o + REACH, rows, :] = jnp.where(there, block, absent) if o else block


def state_of(record):
    return [record[pl.ds(FIELDS * c, FIELDS), :] for c in range(CHUNKS)]


def ends_of(record):
    first = record[pl.ds(FIRST_AT, FIELDS), :].astype(jnp.int32)
    second = record[pl.ds(SECOND_AT, FIELDS), :].astype(jnp.int32)
    return first, second


def diag_of(record):
    return record[pl.ds(DIAG_AT, FIELDS), :]


def rim_of(record, blocks):
    slots = wide(record[pl.ds(RIM_AT, 1), :].astype(jnp.int32))
    lane, high = slots & (TILE - 1), slots >> 7
    found = take(blocks[0], lane)
    for c in range(1, CHUNKS):
        found = jnp.where(high == c, take(blocks[c], lane), found)
    return found


def difference(local, ghosts, field, first, second):
    near = [local[pl.ds(FIELDS * c + field, 1), :] for c in range(CHUNKS)]
    far = [one[pl.ds(field, 1), :] for one in ghosts]
    return look_up(near, first) - look_up(near + far if len(far) > 1 else far, second)


def first_lam(record, ghosts):
    first, second = ends_of(record)
    normal = [difference(record, ghosts, k, first, second) for k in range(3)]
    speed = sum(normal[k] * difference(record, ghosts, 3 + k, first, second) for k in range(3))
    return normal, jnp.maximum(0.0, -speed / diag_of(record))


def add_up(force, first, second, heads, rows):
    for k in range(3):
        head = force[k].astype(jnp.bfloat16).astype(jnp.float32)
        rows[pl.ds(k, FIELDS, stride=FIELDS), :] = force[k] - head
        rows[pl.ds(3 + k, FIELDS, stride=FIELDS), :] = head
    empty = jnp.zeros((FIELDS, TILE), jnp.float32)
    pad = [empty] * (len(heads) % 2)
    left, right = [], []
    for t in range(FIELDS):
        value = rows[pl.ds(FIELDS * t, FIELDS), :]
        for index, limit, signed in ((first, CHUNKS, value), (second, EXT_CHUNKS, -value)):
            if min(heads) >= limit:
                continue
            row = index[t : t + 1]
            high = wide(row >> 7)
            groups = [jnp.where(high == h, signed, 0.0) if h < limit else empty for h in heads]
            left.append(jnp.concatenate(groups + pad, axis=0))
            right.append(one_hot(row & (TILE - 1)))
    total = 0.0
    for k in range(0, len(left), 2):
        total += lax.dot_general(
            jnp.concatenate(left[k : k + 2], axis=1).astype(jnp.bfloat16),
            jnp.concatenate(right[k : k + 2], axis=1),
            NT,
            preferred_element_type=jnp.float32,
        )
    blocks = [total[FIELDS * k : FIELDS * (k + 1)] for k in range(len(heads))]
    return {h: block + pltpu.roll(block, 3, 0) for h, block in zip(heads, blocks)}


def moved(was, here, incoming, back_row):
    place = wide(back_row)
    extra = jnp.where(place > 0, take(incoming, jnp.maximum(place - 1, 0)), 0.0)
    field = rows_iota((FIELDS, TILE))
    gain = wide(was[6:7]) * (here + extra)
    return was + jnp.where((field >= 3) & (field < 6), gain, 0.0)


def near_kernel(stride, parts, *refs):
    came, (heads, tails, coupled, contacts, records, rims) = refs[:3], refs[3:]
    gather_records(stride, parts, came, records)
    for k in (-1, 1):
        record = records.at[REACH + k]
        rims[REACH + k] = rim_of(record, state_of(record))
    normal, lam = first_lam(records.at[REACH], (rims.at[REACH - 1], rims.at[REACH + 1]))
    for k, one in enumerate((*normal, lam)):
        contacts[k] = one
    head = lam.astype(jnp.bfloat16).astype(jnp.float32)
    both = jnp.concatenate([head, lam - head], axis=0).astype(jnp.bfloat16)
    total = jnp.zeros((FIELDS, TILE), jnp.float32)
    for t in range(heads.shape[0]):
        main = jnp.dot(both, heads[t], preferred_element_type=jnp.float32)
        rest = jnp.dot(both, tails[t], preferred_element_type=jnp.float32)
        whole = main[:FIELDS] + main[FIELDS:] + rest[:FIELDS]
        total = jnp.where(rows_iota((FIELDS, TILE)) == t, whole, total)
    coupled[...] = total


def middle_kernel(stride, parts, count, *refs):
    came, known, here = refs[:count], refs[count], refs[count + 1]
    stage, impulse, base, gathered, rims, rows, state_next, rims_next = refs[count + 2 :]
    gather_records(stride, parts, came, gathered)
    records = {o: gathered.at[o + REACH] for o in range(-REACH, REACH + 1)}
    rim = {o: rims.at[o + REACH] for o in records}
    rim_next = {o: rims_next.at[o + 1] for o in (-1, 0, 1)}
    left, right = CHUNKS, CHUNKS + 1
    local = list(range(CHUNKS))
    for o, record in records.items():
        rim[o][...] = rim_of(record, state_of(record))
    heads = {-2: [right], -1: local + [right], 0: local + [left, right], 1: local + [left], 2: [left]}
    ghosts = {o: (rim[o - 1], rim[o + 1]) for o in (-1, 1)}
    ghosts.update({-2: (rim[-1],), 2: (rim[1],)})
    sums, contacts = {}, {}
    for o, record in records.items():
        contacts[o] = first_lam(record, ghosts[o]) if o else ([known[k] for k in range(3)], known[3])
    for o, record in records.items():
        normal, lam = contacts[o]
        first, second = ends_of(record)
        force = [one * lam for one in normal]
        sums[o] = add_up(force, first, second, heads[o], rows.at[o + REACH])
    for o in (-1, 0, 1):
        incoming = sums[o - 1][right] + sums[o + 1][left]
        back = inverse([records[o][pl.ds(RIM_AT, 1), :]])
        if o == 0:
            base[pl.ds(CHUNKS * FIELDS, FIELDS), :] = back.astype(jnp.float32)
        blocks = [
            moved(was, sums[o][c], incoming, back[c : c + 1])
            for c, was in enumerate(state_of(records[o]))
        ]
        rim_next[o][...] = rim_of(records[o], blocks)
        for c in range(CHUNKS):
            state_next[o + 1, pl.ds(FIELDS * c, FIELDS), :] = blocks[c]
    ghosts = {-1: (rim_next[0],), 0: (rim_next[-1], rim_next[1]), 1: (rim_next[0],)}
    for o in (-1, 0, 1):
        normal, lam = contacts[o]
        first, second = ends_of(records[o])
        state = state_next.at[o + 1]
        speed = sum(
            normal[k] * difference(state, ghosts[o], 3 + k, first, second) for k in range(3)
        )
        diag = diag_of(records[o])
        if o == 0:
            lam = jnp.maximum(0.0, lam - (here[...] + speed) / diag)
            impulse[...] = lam
            force = [one * lam for one in normal]
            total = add_up(force, first, second, local, rows.at[2 * REACH + 1])
            for c in local:
                base[pl.ds(FIELDS * c, FIELDS), :] = total[c]
            continue
        side = stage.at[(o + 1) // 2]
        for k, one in enumerate((*normal, lam, speed, diag)):
            side[k] = one
        side[6] = records[o][pl.ds(SECOND_AT, FIELDS), :]


def last_kernel(parts, mine, stage, base, chip, mid, other, velocity, rows):
    me = lax.axis_index("parts")
    odd = me % 2 == 1
    apart = (me % (2 * BLOCK) == BLOCK) | (me % (2 * BLOCK) == BLOCK - 1)
    across = jnp.where(apart, mid[...], other[...])
    across = jnp.where((me > 0) & (me < parts - 1), across, 0.0)
    products = (jnp.where(odd, chip[...], across), jnp.where(odd, across, chip[...]))
    incoming = 0.0
    for k, head in ((0, CHUNKS + 1), (1, CHUNKS)):
        lam = jnp.maximum(0.0, stage[k, 3] - (products[k] + stage[k, 4]) / stage[k, 5])
        second = stage[k, 6].astype(jnp.int32)
        force = [stage[k, d] * lam for d in range(3)]
        incoming += add_up(force, None, second, [head], rows.at[k])[head]
    back = base[pl.ds(CHUNKS * FIELDS, FIELDS), :].astype(jnp.int32)
    for c, was in enumerate(state_of(mine)):
        here = base[pl.ds(FIELDS * c, FIELDS), :]
        block = moved(was, here, incoming, back[c : c + 1])
        velocity[:, pl.ds(c * TILE, TILE)] = block[3:6]


def call(kernel, out_shape, inputs, name, space=pltpu.VMEM, scratch=()):
    many = isinstance(out_shape, (tuple, list))
    vmem = pl.BlockSpec(memory_space=pltpu.VMEM)
    return pl.pallas_call(
        kernel,
        out_shape=out_shape,
        in_specs=[pl.BlockSpec(memory_space=space)] * len(inputs),
        out_specs=[vmem] * len(out_shape) if many else vmem,
        scratch_shapes=list(scratch),
        compiler_params=FROM_HBM if space == pltpu.HBM else PARAMS,
        name=name,
    )(*inputs)


def second_parts(parts, stride):
    pairs = []
    for i in range(parts):
        step = -stride if i % stride < stride // 2 else stride
        to = i + step
        if not 0 <= to < parts:
            to = i + (stride // 2 if step < 0 else -(stride // 2))
        pairs.append((i, to))
    return pairs


def edges(parts):
    return range(BLOCK, parts, 2 * BLOCK)


def next_pairs(parts):
    most = {i: i + 1 if i % 2 else i - 1 for i in range(parts)}
    edge = {i: i ^ 1 for i in range(parts)}
    ends = [0]
    for at in edges(parts):
        ends += [at - 1, at]
        for i, j in ((at - 1, at), (at - 2, at + 2), (at + 1, at + 3)):
            edge[i], edge[j] = j, i
    ends.append(parts - 1)
    closings = [(0, BLOCK), (ends[-2], parts - 1)]
    for k in range(1, len(ends) - 4, 2):
        closings.append((ends[k], ends[k + 2]) if k % 4 == 1 else (ends[k + 1], ends[k + 3]))
    for i, j in closings:
        most[i], most[j] = j, i
    return list(most.items()), list(edge.items())


def body(positions, velocity, inv_mass, swap_lists, rim_list, contact_pair, delassus):
    parts = lax.axis_size("parts")
    stride = parts // GROUP
    grains = positions.shape[1]
    contacts = contact_pair.shape[1]
    tiles = delassus.shape[0]
    reach = 2 * REACH + 1
    float32 = functools.partial(jax.ShapeDtypeStruct, dtype=jnp.float32)
    vmem = lambda *shape: pltpu.VMEM(shape, jnp.float32)
    send = functools.partial(lax.ppermute, axis_name="parts")
    inputs = (
        positions,
        velocity,
        inv_mass.reshape(CHUNKS, TILE),
        swap_lists,
        rim_list.reshape(1, TILE),
    )
    packed = call(
        pack_kernel,
        float32((GROUP, RAW, TILE)),
        inputs,
        "pack",
        pltpu.HBM,
        [pltpu.VMEM(one.shape, one.dtype) for one in inputs]
        + [pltpu.SemaphoreType.DMA((5,))],
    )
    classes = [[r + stride * ((k - 2) % GROUP) for k in range(GROUP)] for r in range(stride)]
    raw = lax.all_to_all(packed, "parts", 0, 0, axis_index_groups=classes)

    half = jax.ShapeDtypeStruct(delassus.shape, jnp.bfloat16)
    fixed, heads, tails = call(
        fixed_kernel, (float32((FIXED, TILE)), half, half), (contact_pair, delassus), "fixed"
    )
    given = send(fixed, perm=second_parts(parts, stride))

    states = call(
        functools.partial(compose_kernel, stride),
        float32((2, FIRST_AT, TILE)),
        (raw,),
        "compose",
        scratch=[vmem(GROUP, FIRST_AT, TILE), vmem(4, FIRST_AT, TILE)],
    )
    record = (RECORD, TILE)
    mine, far, low, high = call(
        functools.partial(join_kernel, stride),
        [float32(record)] * 4,
        (states, fixed, given),
        "join",
    )
    within = [(i, i ^ 1) for i in range(parts)]
    if stride == BLOCK:
        from_far = send(far, perm=[(i, i ^ 3) for i in range(parts)])
        near = (mine, send(mine, perm=within), from_far)
        beyond = [(i, i ^ 2) for i in range(parts)]
        came = (*near, send(low, perm=beyond), send(high, perm=beyond))
    else:
        shifts = [[(i, (i + by) % parts) for i in range(parts)] for by in (1, -1, 2, -2)]
        came = (mine, *[send(mine, perm=shift) for shift in shifts])
        near = came[:3]

    here, known = call(
        functools.partial(near_kernel, stride, parts),
        (float32((tiles, TILE)), float32((4, tiles, TILE))),
        (*near, heads, tails),
        "near",
        scratch=[vmem(reach, *record), vmem(reach, FIELDS, TILE)],
    )
    most, edge = next_pairs(parts)
    other = send(here, perm=most)
    chip = send(here, perm=within)
    mid = send(here, perm=edge)
    stage, impulse, base = call(
        functools.partial(middle_kernel, stride, parts, len(came)),
        (
            float32((2, 7, FIELDS, TILE)),
            float32((tiles, TILE)),
            float32(((CHUNKS + 1) * FIELDS, TILE)),
        ),
        (*came, known, here),
        "middle",
        scratch=[
            vmem(reach, *record),
            vmem(reach, FIELDS, TILE),
            vmem(reach + 1, FIELDS * FIELDS, TILE),
            vmem(3, CHUNKS * FIELDS, TILE),
            vmem(3, FIELDS, TILE),
        ],
    )
    new_velocity = call(
        functools.partial(last_kernel, parts),
        float32((3, grains)),
        (mine, stage, base, chip, mid, other),
        "last",
        scratch=[vmem(2, FIELDS * FIELDS, TILE)],
    )
    return (new_velocity, impulse.reshape(contacts))


def solution(mesh):
    in_specs = (
        P(None, "parts"),
        P(None, "parts"),
        P("parts"),
        P(None, "parts"),
        P("parts"),
        P(None, "parts"),
        P("parts", None, None),
    )
    out_specs = (P(None, "parts"), P("parts"))
    return jax.shard_map(body, mesh=mesh, in_specs=in_specs, out_specs=out_specs, check_vma=False)
```

```python
import functools

import jax
import jax.numpy as jnp
from jax import lax
from jax.experimental import pallas as pl
from jax.experimental.pallas import tpu as pltpu
from jax.sharding import PartitionSpec as P

TILE = 128
LEVELS = 3
GROUP = 2**LEVELS
REACH = 2
FIELDS = 8
CHUNKS = 4
EXT_CHUNKS = 6
RIM_AT = 7
FIRST_AT = 32
SECOND_AT = 40
DIAG_AT = 48
RECORD = 56
LISTS_AT = 32
RAW = 40
FIXED = RECORD - FIRST_AT
BLOCK = 4
PARAMS = pltpu.CompilerParams(vmem_limit_bytes=32 * 2**20)
FROM_HBM = pltpu.CompilerParams(vmem_limit_bytes=63 * 2**20)
NT = (((1,), (1,)), ((), ()))


def rows_iota(shape):
    return lax.broadcasted_iota(jnp.int32, shape, 0)


def lanes_iota(shape):
    return lax.broadcasted_iota(jnp.int32, shape, 1)


def wide(row):
    return jnp.broadcast_to(row, (FIELDS, TILE))


def take(table, lane):
    return jnp.take_along_axis(table, lane, axis=1, mode="promise_in_bounds")


def look_up(rows, index):
    lane, high = index & (TILE - 1), index >> 7
    found = take(wide(rows[0]), lane)
    for h in range(1, len(rows)):
        found = jnp.where(high == h, take(wide(rows[h]), lane), found)
    return found


def one_hot(low_row):
    row = jnp.broadcast_to(low_row.astype(jnp.float32).astype(jnp.bfloat16), (TILE, TILE))
    column = rows_iota((TILE, TILE)).astype(jnp.float32).astype(jnp.bfloat16)
    return jnp.where(row == column, jnp.bfloat16(1), jnp.bfloat16(0))


def inverse(slot_rows):
    left, right = [], []
    for at, row in enumerate(slot_rows):
        slots = row.astype(jnp.int32)
        place = (lanes_iota((FIELDS, TILE)) + (at * TILE + 1)).astype(jnp.float32)
        heads = jnp.where(wide(slots >> 7) == rows_iota((FIELDS, TILE)), place, 0.0)
        left.append(heads.astype(jnp.bfloat16))
        right.append(one_hot(slots & (TILE - 1)))
    total = lax.dot_general(
        jnp.concatenate(left, axis=1),
        jnp.concatenate(right, axis=1),
        NT,
        preferred_element_type=jnp.float32,
    )
    return total.astype(jnp.int32)


def pack_kernel(*refs):
    sources, out, held, sems = refs[:5], refs[5], refs[6:11], refs[11]
    copies = [
        pltpu.make_async_copy(source, target, sems.at[k])
        for k, (source, target) in enumerate(zip(sources, held))
    ]
    for copy in copies:
        copy.start()
    pos, vel, mass, lists, rim = held
    for copy in copies:
        copy.wait()
    first = out.at[0]
    for c in range(CHUNKS):
        lanes = pl.ds(c * TILE, TILE)
        first[pl.ds(FIELDS * c, 3), :] = pos[:, lanes]
        first[pl.ds(FIELDS * c + 3, 3), :] = vel[:, lanes]
        first[pl.ds(FIELDS * c + 6, 1), :] = mass[pl.ds(c, 1), :]
        spare = rim[...].astype(jnp.float32) if c == 0 else jnp.zeros((1, TILE), jnp.float32)
        first[pl.ds(FIELDS * c + 7, 1), :] = spare
    for level in range(LEVELS):
        for h in range(2):
            row = lists[pl.ds(level, 1), pl.ds(h * TILE, TILE)]
            first[pl.ds(LISTS_AT + 2 * level + h, 1), :] = row.astype(jnp.float32)
    first[pl.ds(LISTS_AT + 2 * LEVELS, 2), :] = jnp.zeros((2, TILE), jnp.float32)
    whole = first[...]
    for m in range(1, GROUP):
        out[m] = whole


def fixed_kernel(pair, tiles, out, heads, tails):
    eye = rows_iota((TILE, TILE)) == lanes_iota((TILE, TILE))
    for t in range(tiles.shape[0]):
        lanes = pl.ds(t * TILE, TILE)
        out[pl.ds(t, 1), :] = pair[pl.ds(0, 1), lanes].astype(jnp.float32)
        out[pl.ds(FIELDS + t, 1), :] = pair[pl.ds(1, 1), lanes].astype(jnp.float32)
        tile = tiles[t]
        turned = tile.T
        head = turned.astype(jnp.bfloat16)
        heads[t] = head
        tails[t] = (turned - head.astype(jnp.float32)).astype(jnp.bfloat16)
        diag = jnp.sum(jnp.where(eye, tile, 0.0), axis=0, keepdims=True)
        out[pl.ds(2 * FIELDS + t, 1), :] = diag


def second_part(stride):
    me = lax.axis_index("parts")
    member, kind = me // stride, me % stride
    step = jnp.where(kind < stride // 2, 1, -1)
    return step, (member + step >= 0) & (member + step < GROUP)


def swapped(lists, other_lists, own, other, out):
    back = inverse(lists)
    place = jnp.maximum(back - 1, 0)
    slot = look_up(other_lists, place).astype(jnp.int32)
    lane = slot & (TILE - 1)
    block = jnp.where(back > 0, slot >> 7, -1)
    tables = [other[pl.ds(FIELDS * h, FIELDS), :] for h in range(CHUNKS)]
    for c in range(CHUNKS):
        rows = pl.ds(FIELDS * c, FIELDS)
        lane_c, block_c = wide(lane[c : c + 1]), wide(block[c : c + 1])
        found = own[rows, :]
        for h, table in enumerate(tables):
            found = jnp.where(block_c == h, take(table, lane_c), found)
        out[rows, :] = found


def compose_kernel(stride, raw, own, once, twice):
    member = lax.axis_index("parts") // stride
    step, exists = second_part(stride)

    def came_from(part):
        return raw.at[(part + 2) % GROUP]

    def list_rows(part, level):
        rows = came_from(part)
        return [rows[pl.ds(LISTS_AT + 2 * level + h, 1), :] for h in range(2)]

    def level_step(level, part, apart, own_state, other_state, out):
        lists, others = list_rows(part, level), list_rows(part ^ apart, level)
        swapped(lists, others, own_state, other_state, out)

    for r in range(GROUP):
        level_step(0, r, 4, came_from(r), came_from(r ^ 4), once.at[r])
    second = (member + step + GROUP) % GROUP
    for i, part in enumerate((member, member ^ 1, second, second ^ 1)):
        level_step(1, part, 2, once.at[part], once.at[part ^ 2], twice.at[i])
    for i, part in enumerate((member, second)):
        level_step(2, part, 1, twice.at[2 * i], twice.at[2 * i + 1], own.at[i])
        own[i, pl.ds(RIM_AT, 1), :] = came_from(part)[pl.ds(RIM_AT, 1), :]
    for c in range(CHUNKS):
        rows = pl.ds(FIELDS * c, FIELDS)
        own[1, rows, :] = jnp.where(exists, own[1, rows, :], 0.0)


def join_kernel(stride, states, fixed, given, mine, far, low, high):
    kind = lax.axis_index("parts") % stride
    exists = second_part(stride)[1]
    early, outer = kind < stride // 2, (kind == 0) | (kind == stride - 1)
    for at in range(0, RECORD, FIELDS):
        rows = pl.ds(at, FIELDS)
        if at < FIRST_AT:
            one, two = states[0, rows, :], states[1, rows, :]
        else:
            part = pl.ds(at - FIRST_AT, FIELDS)
            absent = 1.0 if at == DIAG_AT else 0.0
            one, two = fixed[part, :], jnp.where(exists, given[part, :], absent)
        mine[rows, :] = one
        far[rows, :] = jnp.where(outer, two, one)
        low[rows, :] = jnp.where(early, one, two)
        high[rows, :] = jnp.where(early, two, one)


def gather_records(stride, parts, came, records):
    me = lax.axis_index("parts")
    swap = (stride == BLOCK) & (me % 2 == 0)
    mine, one, two, *side = came
    for at in range(0, RECORD, FIELDS):
        rows = pl.ds(at, FIELDS)
        blocks = {
            0: mine[rows, :],
            -1: jnp.where(swap, two[rows, :], one[rows, :]),
            1: jnp.where(swap, one[rows, :], two[rows, :]),
        }
        if side:
            blocks[-2], blocks[2] = side[0][rows, :], side[1][rows, :]
        for o, block in blocks.items():
            absent = 1.0 if at == DIAG_AT else 0.0
            there = (me + o >= 0) & (me + o < parts)
            records[o + REACH, rows, :] = jnp.where(there, block, absent) if o else block


def state_of(record):
    return [record[pl.ds(FIELDS * c, FIELDS), :] for c in range(CHUNKS)]


def ends_of(record):
    first = record[pl.ds(FIRST_AT, FIELDS), :].astype(jnp.int32)
    second = record[pl.ds(SECOND_AT, FIELDS), :].astype(jnp.int32)
    return first, second


def diag_of(record):
    return record[pl.ds(DIAG_AT, FIELDS), :]


def rim_of(record, blocks):
    slots = wide(record[pl.ds(RIM_AT, 1), :].astype(jnp.int32))
    lane, high = slots & (TILE - 1), slots >> 7
    found = take(blocks[0], lane)
    for c in range(1, CHUNKS):
        found = jnp.where(high == c, take(blocks[c], lane), found)
    return found


def difference(local, ghosts, field, first, second):
    near = [local[pl.ds(FIELDS * c + field, 1), :] for c in range(CHUNKS)]
    far = [one[pl.ds(field, 1), :] for one in ghosts]
    return look_up(near, first) - look_up(near + far if len(far) > 1 else far, second)


def first_lam(record, ghosts):
    first, second = ends_of(record)
    normal = [difference(record, ghosts, k, first, second) for k in range(3)]
    speed = sum(normal[k] * difference(record, ghosts, 3 + k, first, second) for k in range(3))
    return normal, jnp.maximum(0.0, -speed / diag_of(record))


def add_up(force, first, second, heads, rows):
    for k in range(3):
        head = force[k].astype(jnp.bfloat16).astype(jnp.float32)
        rows[pl.ds(k, FIELDS, stride=FIELDS), :] = force[k] - head
        rows[pl.ds(3 + k, FIELDS, stride=FIELDS), :] = head
    empty = jnp.zeros((FIELDS, TILE), jnp.float32)
    pad = [empty] * (len(heads) % 2)
    left, right = [], []
    for t in range(FIELDS):
        value = rows[pl.ds(FIELDS * t, FIELDS), :]
        for index, limit, signed in ((first, CHUNKS, value), (second, EXT_CHUNKS, -value)):
            if min(heads) >= limit:
                continue
            row = index[t : t + 1]
            high = wide(row >> 7)
            groups = [jnp.where(high == h, signed, 0.0) if h < limit else empty for h in heads]
            left.append(jnp.concatenate(groups + pad, axis=0))
            right.append(one_hot(row & (TILE - 1)))
    total = 0.0
    for k in range(0, len(left), 2):
        total += lax.dot_general(
            jnp.concatenate(right[k : k + 2], axis=1),
            jnp.concatenate(left[k : k + 2], axis=1).astype(jnp.bfloat16),
            NT,
            preferred_element_type=jnp.float32,
        )
    total = total.T
    blocks = [total[FIELDS * k : FIELDS * (k + 1)] for k in range(len(heads))]
    return {h: block + pltpu.roll(block, 3, 0) for h, block in zip(heads, blocks)}


def moved(was, here, incoming, back_row):
    place = wide(back_row)
    extra = jnp.where(place > 0, take(incoming, jnp.maximum(place - 1, 0)), 0.0)
    field = rows_iota((FIELDS, TILE))
    gain = wide(was[6:7]) * (here + extra)
    return was + jnp.where((field >= 3) & (field < 6), gain, 0.0)


def near_kernel(stride, parts, *refs):
    came, (heads, tails, coupled, contacts, records, rims) = refs[:3], refs[3:]
    gather_records(stride, parts, came, records)
    for k in (-1, 1):
        record = records.at[REACH + k]
        rims[REACH + k] = rim_of(record, state_of(record))
    normal, lam = first_lam(records.at[REACH], (rims.at[REACH - 1], rims.at[REACH + 1]))
    for k, one in enumerate((*normal, lam)):
        contacts[k] = one
    head = lam.astype(jnp.bfloat16).astype(jnp.float32)
    both = jnp.concatenate([head, lam - head], axis=0).astype(jnp.bfloat16)
    total = jnp.zeros((FIELDS, TILE), jnp.float32)
    for t in range(heads.shape[0]):
        main = jnp.dot(both, heads[t], preferred_element_type=jnp.float32)
        rest = jnp.dot(both, tails[t], preferred_element_type=jnp.float32)
        whole = main[:FIELDS] + main[FIELDS:] + rest[:FIELDS]
        total = jnp.where(rows_iota((FIELDS, TILE)) == t, whole, total)
    coupled[...] = total


def middle_kernel(stride, parts, count, *refs):
    came, known = refs[:count], refs[count]
    stage, back_here, fixed_out, gathered, rims, rows, state_next, rims_next = refs[count + 1 :]
    gather_records(stride, parts, came, gathered)
    records = {o: gathered.at[o + REACH] for o in range(-REACH, REACH + 1)}
    rim = {o: rims.at[o + REACH] for o in records}
    rim_next = {o: rims_next.at[o + 1] for o in (-1, 0, 1)}
    left, right = CHUNKS, CHUNKS + 1
    local = list(range(CHUNKS))
    for o, record in records.items():
        rim[o][...] = rim_of(record, state_of(record))
    heads = {-2: [right], -1: local + [right], 0: local + [left, right], 1: local + [left], 2: [left]}
    ghosts = {o: (rim[o - 1], rim[o + 1]) for o in (-1, 1)}
    ghosts.update({-2: (rim[-1],), 2: (rim[1],)})
    sums, contacts = {}, {}
    for o, record in records.items():
        contacts[o] = first_lam(record, ghosts[o]) if o else ([known[k] for k in range(3)], known[3])
    for o, record in records.items():
        normal, lam = contacts[o]
        first, second = ends_of(record)
        force = [one * lam for one in normal]
        sums[o] = add_up(force, first, second, heads[o], rows.at[o + REACH])
    for o in (-1, 0, 1):
        incoming = sums[o - 1][right] + sums[o + 1][left]
        back = inverse([records[o][pl.ds(RIM_AT, 1), :]])
        if o == 0:
            back_here[...] = back
        blocks = [
            moved(was, sums[o][c], incoming, back[c : c + 1])
            for c, was in enumerate(state_of(records[o]))
        ]
        rim_next[o][...] = rim_of(records[o], blocks)
        for c in range(CHUNKS):
            state_next[o + 1, pl.ds(FIELDS * c, FIELDS), :] = blocks[c]
    ghosts = {-1: (rim_next[0],), 0: (rim_next[-1], rim_next[1]), 1: (rim_next[0],)}
    for o in (-1, 0, 1):
        normal, lam = contacts[o]
        first, second = ends_of(records[o])
        state = state_next.at[o + 1]
        speed = sum(
            normal[k] * difference(state, ghosts[o], 3 + k, first, second) for k in range(3)
        )
        for k in range(3):
            stage[o + 1, k] = normal[k]
        stage[o + 1, 3] = lam
        stage[o + 1, 4] = speed
        fixed_out[o + 1] = records[o][pl.ds(FIRST_AT, FIXED), :]


def last_kernel(
    parts, mine, stage, back, here, chip, mid, other, fixed, velocity, impulse, rows
):
    me = lax.axis_index("parts")
    odd = me % 2 == 1
    apart = (me % (2 * BLOCK) == BLOCK) | (me % (2 * BLOCK) == BLOCK - 1)
    across = jnp.where(apart, mid[...], other[...])
    across = jnp.where((me > 0) & (me < parts - 1), across, 0.0)
    coupled = {
        -1: jnp.where(odd, chip[...], across),
        0: here[...],
        1: jnp.where(odd, across, chip[...]),
    }
    sums = {}
    for o, heads in ((-1, [CHUNKS + 1]), (0, list(range(CHUNKS))), (1, [CHUNKS])):
        record = fixed.at[o + 1]
        lam = stage[o + 1, 3]
        diag = record[pl.ds(DIAG_AT - FIRST_AT, FIELDS), :]
        lam = jnp.maximum(0.0, lam - (coupled[o] + stage[o + 1, 4]) / diag)
        if o == 0:
            impulse[...] = lam
        first = record[pl.ds(0, FIELDS), :].astype(jnp.int32)
        second = record[pl.ds(SECOND_AT - FIRST_AT, FIELDS), :].astype(jnp.int32)
        force = [stage[o + 1, k] * lam for k in range(3)]
        sums[o] = add_up(force, first, second, heads, rows.at[o + 1])
    incoming = sums[-1][CHUNKS + 1] + sums[1][CHUNKS]
    for c, was in enumerate(state_of(mine)):
        block = moved(was, sums[0][c], incoming, back[pl.ds(c, 1), :])
        velocity[:, pl.ds(c * TILE, TILE)] = block[3:6]


def call(kernel, out_shape, inputs, name, space=pltpu.VMEM, scratch=()):
    many = isinstance(out_shape, (tuple, list))
    vmem = pl.BlockSpec(memory_space=pltpu.VMEM)
    return pl.pallas_call(
        kernel,
        out_shape=out_shape,
        in_specs=[pl.BlockSpec(memory_space=space)] * len(inputs),
        out_specs=[vmem] * len(out_shape) if many else vmem,
        scratch_shapes=list(scratch),
        compiler_params=FROM_HBM if space == pltpu.HBM else PARAMS,
        name=name,
    )(*inputs)


def second_parts(parts, stride):
    pairs = []
    for i in range(parts):
        step = -stride if i % stride < stride // 2 else stride
        to = i + step
        if not 0 <= to < parts:
            to = i + (stride // 2 if step < 0 else -(stride // 2))
        pairs.append((i, to))
    return pairs


def edges(parts):
    return range(BLOCK, parts, 2 * BLOCK)


def next_pairs(parts):
    most = {i: i + 1 if i % 2 else i - 1 for i in range(parts)}
    edge = {i: i ^ 1 for i in range(parts)}
    ends = [0]
    for at in edges(parts):
        ends += [at - 1, at]
        for i, j in ((at - 1, at), (at - 2, at + 2), (at + 1, at + 3)):
            edge[i], edge[j] = j, i
    ends.append(parts - 1)
    closings = [(0, BLOCK), (ends[-2], parts - 1)]
    for k in range(1, len(ends) - 4, 2):
        closings.append((ends[k], ends[k + 2]) if k % 4 == 1 else (ends[k + 1], ends[k + 3]))
    for i, j in closings:
        most[i], most[j] = j, i
    return list(most.items()), list(edge.items())


def body(positions, velocity, inv_mass, swap_lists, rim_list, contact_pair, delassus):
    parts = lax.axis_size("parts")
    stride = parts // GROUP
    grains = positions.shape[1]
    contacts = contact_pair.shape[1]
    tiles = delassus.shape[0]
    reach = 2 * REACH + 1
    float32 = functools.partial(jax.ShapeDtypeStruct, dtype=jnp.float32)
    vmem = lambda *shape: pltpu.VMEM(shape, jnp.float32)
    send = functools.partial(lax.ppermute, axis_name="parts")
    inputs = (
        positions,
        velocity,
        inv_mass.reshape(CHUNKS, TILE),
        swap_lists,
        rim_list.reshape(1, TILE),
    )
    packed = call(
        pack_kernel,
        float32((GROUP, RAW, TILE)),
        inputs,
        "pack",
        pltpu.HBM,
        [pltpu.VMEM(one.shape, one.dtype) for one in inputs]
        + [pltpu.SemaphoreType.DMA((5,))],
    )
    classes = [[r + stride * ((k - 2) % GROUP) for k in range(GROUP)] for r in range(stride)]
    raw = lax.all_to_all(packed, "parts", 0, 0, axis_index_groups=classes)

    half = jax.ShapeDtypeStruct(delassus.shape, jnp.bfloat16)
    fixed, heads, tails = call(
        fixed_kernel, (float32((FIXED, TILE)), half, half), (contact_pair, delassus), "fixed"
    )
    given = send(fixed, perm=second_parts(parts, stride))

    states = call(
        functools.partial(compose_kernel, stride),
        float32((2, FIRST_AT, TILE)),
        (raw,),
        "compose",
        scratch=[vmem(GROUP, FIRST_AT, TILE), vmem(4, FIRST_AT, TILE)],
    )
    record = (RECORD, TILE)
    mine, far, low, high = call(
        functools.partial(join_kernel, stride),
        [float32(record)] * 4,
        (states, fixed, given),
        "join",
    )
    within = [(i, i ^ 1) for i in range(parts)]
    if stride == BLOCK:
        from_far = send(far, perm=[(i, i ^ 3) for i in range(parts)])
        near = (mine, send(mine, perm=within), from_far)
        beyond = [(i, i ^ 2) for i in range(parts)]
        came = (*near, send(low, perm=beyond), send(high, perm=beyond))
    else:
        shifts = [[(i, (i + by) % parts) for i in range(parts)] for by in (1, -1, 2, -2)]
        came = (mine, *[send(mine, perm=shift) for shift in shifts])
        near = came[:3]

    here, known = call(
        functools.partial(near_kernel, stride, parts),
        (float32((tiles, TILE)), float32((4, tiles, TILE))),
        (*near, heads, tails),
        "near",
        scratch=[vmem(reach, *record), vmem(reach, FIELDS, TILE)],
    )
    most, edge = next_pairs(parts)
    other = send(here, perm=most)
    chip = send(here, perm=within)
    mid = send(here, perm=edge)
    stage, back, contact_rows = call(
        functools.partial(middle_kernel, stride, parts, len(came)),
        (
            float32((3, 5, FIELDS, TILE)),
            jax.ShapeDtypeStruct((FIELDS, TILE), jnp.int32),
            float32((3, FIXED, TILE)),
        ),
        (*came, known),
        "middle",
        scratch=[
            vmem(reach, *record),
            vmem(reach, FIELDS, TILE),
            vmem(reach, FIELDS * FIELDS, TILE),
            vmem(3, CHUNKS * FIELDS, TILE),
            vmem(3, FIELDS, TILE),
        ],
    )
    new_velocity, impulse = call(
        functools.partial(last_kernel, parts),
        (float32((3, grains)), float32((tiles, TILE))),
        (mine, stage, back, here, chip, mid, other, contact_rows),
        "last",
        scratch=[vmem(3, FIELDS * FIELDS, TILE)],
    )
    return (new_velocity, impulse.reshape(contacts))


def solution(mesh):
    in_specs = (
        P(None, "parts"),
        P(None, "parts"),
        P("parts"),
        P(None, "parts"),
        P("parts"),
        P(None, "parts"),
        P("parts", None, None),
    )
    out_specs = (P(None, "parts"), P("parts"))
    return jax.shard_map(body, mesh=mesh, in_specs=in_specs, out_specs=out_specs, check_vma=False)
```

```python
import functools

import jax
import jax.numpy as jnp
from jax import lax
from jax.experimental import pallas as pl
from jax.experimental.pallas import tpu as pltpu
from jax.sharding import PartitionSpec as P

TILE = 128
LEVELS = 3
GROUP = 2**LEVELS
REACH = 2
FIELDS = 8
CHUNKS = 4
EXT_CHUNKS = 6
RIM_AT = 7
FIRST_AT = 32
SECOND_AT = 40
DIAG_AT = 48
RECORD = 56
LISTS_AT = 32
RAW = 40
FIXED = RECORD - FIRST_AT
BLOCK = 4
PARAMS = pltpu.CompilerParams(vmem_limit_bytes=32 * 2**20)
FROM_HBM = pltpu.CompilerParams(vmem_limit_bytes=63 * 2**20)
NT = (((1,), (1,)), ((), ()))


def rows_iota(shape):
    return lax.broadcasted_iota(jnp.int32, shape, 0)


def lanes_iota(shape):
    return lax.broadcasted_iota(jnp.int32, shape, 1)


def wide(row):
    return jnp.broadcast_to(row, (FIELDS, TILE))


def take(table, lane):
    return jnp.take_along_axis(table, lane, axis=1, mode="promise_in_bounds")


def look_up(rows, index):
    lane, high = index & (TILE - 1), index >> 7
    found = take(wide(rows[0]), lane)
    for h in range(1, len(rows)):
        found = jnp.where(high == h, take(wide(rows[h]), lane), found)
    return found


def one_hot(low_row):
    row = jnp.broadcast_to(low_row.astype(jnp.float32).astype(jnp.bfloat16), (TILE, TILE))
    column = rows_iota((TILE, TILE)).astype(jnp.float32).astype(jnp.bfloat16)
    return jnp.where(row == column, jnp.bfloat16(1), jnp.bfloat16(0))


def inverse(slot_rows):
    left, right = [], []
    for at, row in enumerate(slot_rows):
        slots = row.astype(jnp.int32)
        place = (lanes_iota((FIELDS, TILE)) + (at * TILE + 1)).astype(jnp.float32)
        heads = jnp.where(wide(slots >> 7) == rows_iota((FIELDS, TILE)), place, 0.0)
        left.append(heads.astype(jnp.bfloat16))
        right.append(one_hot(slots & (TILE - 1)))
    total = lax.dot_general(
        jnp.concatenate(left, axis=1),
        jnp.concatenate(right, axis=1),
        NT,
        preferred_element_type=jnp.float32,
    )
    return total.astype(jnp.int32)


def pack_kernel(*refs):
    sources, out, held, sems = refs[:5], refs[5], refs[6:11], refs[11]
    copies = [
        pltpu.make_async_copy(source, target, sems.at[k])
        for k, (source, target) in enumerate(zip(sources, held))
    ]
    for copy in copies:
        copy.start()
    pos, vel, mass, lists, rim = held
    for copy in copies:
        copy.wait()
    first = out.at[0]
    for c in range(CHUNKS):
        lanes = pl.ds(c * TILE, TILE)
        first[pl.ds(FIELDS * c, 3), :] = pos[:, lanes]
        first[pl.ds(FIELDS * c + 3, 3), :] = vel[:, lanes]
        first[pl.ds(FIELDS * c + 6, 1), :] = mass[pl.ds(c, 1), :]
        spare = rim[...].astype(jnp.float32) if c == 0 else jnp.zeros((1, TILE), jnp.float32)
        first[pl.ds(FIELDS * c + 7, 1), :] = spare
    for level in range(LEVELS):
        for h in range(2):
            row = lists[pl.ds(level, 1), pl.ds(h * TILE, TILE)]
            first[pl.ds(LISTS_AT + 2 * level + h, 1), :] = row.astype(jnp.float32)
    first[pl.ds(LISTS_AT + 2 * LEVELS, 2), :] = jnp.zeros((2, TILE), jnp.float32)
    whole = first[...]
    for m in range(1, GROUP):
        out[m] = whole


def fixed_kernel(pair, tiles, out, heads, tails):
    eye = rows_iota((TILE, TILE)) == lanes_iota((TILE, TILE))
    for t in range(tiles.shape[0]):
        lanes = pl.ds(t * TILE, TILE)
        out[pl.ds(t, 1), :] = pair[pl.ds(0, 1), lanes].astype(jnp.float32)
        out[pl.ds(FIELDS + t, 1), :] = pair[pl.ds(1, 1), lanes].astype(jnp.float32)
        tile = tiles[t]
        turned = tile.T
        head = turned.astype(jnp.bfloat16)
        heads[t] = head
        tails[t] = (turned - head.astype(jnp.float32)).astype(jnp.bfloat16)
        diag = jnp.sum(jnp.where(eye, tile, 0.0), axis=0, keepdims=True)
        out[pl.ds(2 * FIELDS + t, 1), :] = diag


def second_part(stride):
    me = lax.axis_index("parts")
    member, kind = me // stride, me % stride
    step = jnp.where(kind < stride // 2, 1, -1)
    return step, (member + step >= 0) & (member + step < GROUP)


def swapped(lists, other_lists, own, other, out):
    back = inverse(lists)
    place = jnp.maximum(back - 1, 0)
    slot = look_up(other_lists, place).astype(jnp.int32)
    lane = slot & (TILE - 1)
    block = jnp.where(back > 0, slot >> 7, -1)
    tables = [other[pl.ds(FIELDS * h, FIELDS), :] for h in range(CHUNKS)]
    for c in range(CHUNKS):
        rows = pl.ds(FIELDS * c, FIELDS)
        lane_c, block_c = wide(lane[c : c + 1]), wide(block[c : c + 1])
        found = own[rows, :]
        for h, table in enumerate(tables):
            found = jnp.where(block_c == h, take(table, lane_c), found)
        out[rows, :] = found


def compose_kernel(stride, raw, own, once, twice):
    member = lax.axis_index("parts") // stride
    step, exists = second_part(stride)

    def came_from(part):
        return raw.at[(part + 2) % GROUP]

    def list_rows(part, level):
        rows = came_from(part)
        return [rows[pl.ds(LISTS_AT + 2 * level + h, 1), :] for h in range(2)]

    def level_step(level, part, apart, own_state, other_state, out):
        lists, others = list_rows(part, level), list_rows(part ^ apart, level)
        swapped(lists, others, own_state, other_state, out)

    second = (member + step + GROUP) % GROUP

    def first_swap(half):
        for i in range(GROUP // 2):
            r = half + i
            level_step(0, r, 4, came_from(r), came_from(r ^ 4), once.at[r])

    near_half = member // 4 * 4
    first_swap(near_half)

    @pl.when(second // 4 * 4 != near_half)
    def _():
        first_swap(4 - near_half)

    for i, part in enumerate((member, member ^ 1, second, second ^ 1)):
        level_step(1, part, 2, once.at[part], once.at[part ^ 2], twice.at[i])
    for i, part in enumerate((member, second)):
        level_step(2, part, 1, twice.at[2 * i], twice.at[2 * i + 1], own.at[i])
        own[i, pl.ds(RIM_AT, 1), :] = came_from(part)[pl.ds(RIM_AT, 1), :]
    for c in range(CHUNKS):
        rows = pl.ds(FIELDS * c, FIELDS)
        own[1, rows, :] = jnp.where(exists, own[1, rows, :], 0.0)


def join_kernel(stride, states, fixed, given, mine, far, low, high):
    kind = lax.axis_index("parts") % stride
    exists = second_part(stride)[1]
    early, outer = kind < stride // 2, (kind == 0) | (kind == stride - 1)
    for at in range(0, RECORD, FIELDS):
        rows = pl.ds(at, FIELDS)
        if at < FIRST_AT:
            one, two = states[0, rows, :], states[1, rows, :]
        else:
            part = pl.ds(at - FIRST_AT, FIELDS)
            absent = 1.0 if at == DIAG_AT else 0.0
            one, two = fixed[part, :], jnp.where(exists, given[part, :], absent)
        mine[rows, :] = one
        far[rows, :] = jnp.where(outer, two, one)
        low[rows, :] = jnp.where(early, one, two)
        high[rows, :] = jnp.where(early, two, one)


def gather_records(stride, parts, came, records):
    me = lax.axis_index("parts")
    swap = (stride == BLOCK) & (me % 2 == 0)
    mine, one, two, *side = came
    for at in range(0, RECORD, FIELDS):
        rows = pl.ds(at, FIELDS)
        blocks = {
            0: mine[rows, :],
            -1: jnp.where(swap, two[rows, :], one[rows, :]),
            1: jnp.where(swap, one[rows, :], two[rows, :]),
        }
        if side:
            blocks[-2], blocks[2] = side[0][rows, :], side[1][rows, :]
        for o, block in blocks.items():
            absent = 1.0 if at == DIAG_AT else 0.0
            there = (me + o >= 0) & (me + o < parts)
            records[o + REACH, rows, :] = jnp.where(there, block, absent) if o else block


def state_of(record):
    return [record[pl.ds(FIELDS * c, FIELDS), :] for c in range(CHUNKS)]


def ends_of(record):
    first = record[pl.ds(FIRST_AT, FIELDS), :].astype(jnp.int32)
    second = record[pl.ds(SECOND_AT, FIELDS), :].astype(jnp.int32)
    return first, second


def diag_of(record):
    return record[pl.ds(DIAG_AT, FIELDS), :]


def rim_of(record, blocks):
    slots = wide(record[pl.ds(RIM_AT, 1), :].astype(jnp.int32))
    lane, high = slots & (TILE - 1), slots >> 7
    found = take(blocks[0], lane)
    for c in range(1, CHUNKS):
        found = jnp.where(high == c, take(blocks[c], lane), found)
    return found


def difference(local, ghosts, field, first, second):
    near = [local[pl.ds(FIELDS * c + field, 1), :] for c in range(CHUNKS)]
    far = [one[pl.ds(field, 1), :] for one in ghosts]
    return look_up(near, first) - look_up(near + far if len(far) > 1 else far, second)


def first_lam(record, ghosts):
    first, second = ends_of(record)
    normal = [difference(record, ghosts, k, first, second) for k in range(3)]
    speed = sum(normal[k] * difference(record, ghosts, 3 + k, first, second) for k in range(3))
    return normal, jnp.maximum(0.0, -speed / diag_of(record))


def add_up(force, first, second, heads, rows):
    for k in range(3):
        head = force[k].astype(jnp.bfloat16).astype(jnp.float32)
        rows[pl.ds(k, FIELDS, stride=FIELDS), :] = force[k] - head
        rows[pl.ds(3 + k, FIELDS, stride=FIELDS), :] = head
    empty = jnp.zeros((FIELDS, TILE), jnp.float32)
    pad = [empty] * (len(heads) % 2)
    left, right = [], []
    for t in range(FIELDS):
        value = rows[pl.ds(FIELDS * t, FIELDS), :]
        for index, limit, signed in ((first, CHUNKS, value), (second, EXT_CHUNKS, -value)):
            if min(heads) >= limit:
                continue
            row = index[t : t + 1]
            high = wide(row >> 7)
            groups = [jnp.where(high == h, signed, 0.0) if h < limit else empty for h in heads]
            left.append(jnp.concatenate(groups + pad, axis=0))
            right.append(one_hot(row & (TILE - 1)))
    total = lax.dot_general(
        jnp.concatenate(left, axis=1).astype(jnp.bfloat16),
        jnp.concatenate(right, axis=1),
        NT,
        preferred_element_type=jnp.float32,
    )
    blocks = [total[FIELDS * k : FIELDS * (k + 1)] for k in range(len(heads))]
    return {h: block + pltpu.roll(block, 3, 0) for h, block in zip(heads, blocks)}


def moved(was, here, incoming, back_row):
    place = wide(back_row)
    extra = jnp.where(place > 0, take(incoming, jnp.maximum(place - 1, 0)), 0.0)
    field = rows_iota((FIELDS, TILE))
    gain = wide(was[6:7]) * (here + extra)
    return was + jnp.where((field >= 3) & (field < 6), gain, 0.0)


def near_kernel(stride, parts, *refs):
    came, (heads, tails, coupled, contacts, records, rims) = refs[:3], refs[3:]
    gather_records(stride, parts, came, records)
    for k in (-1, 1):
        record = records.at[REACH + k]
        rims[REACH + k] = rim_of(record, state_of(record))
    normal, lam = first_lam(records.at[REACH], (rims.at[REACH - 1], rims.at[REACH + 1]))
    for k, one in enumerate((*normal, lam)):
        contacts[k] = one
    head = lam.astype(jnp.bfloat16).astype(jnp.float32)
    both = jnp.concatenate([head, lam - head], axis=0).astype(jnp.bfloat16)
    total = jnp.zeros((FIELDS, TILE), jnp.float32)
    for t in range(heads.shape[0]):
        main = jnp.dot(both, heads[t], preferred_element_type=jnp.float32)
        rest = jnp.dot(both, tails[t], preferred_element_type=jnp.float32)
        whole = main[:FIELDS] + main[FIELDS:] + rest[:FIELDS]
        total = jnp.where(rows_iota((FIELDS, TILE)) == t, whole, total)
    coupled[...] = total


def middle_kernel(stride, parts, count, *refs):
    came, known = refs[:count], refs[count]
    stage, back_here, fixed_out, gathered, rims, rows, state_next, rims_next = refs[count + 1 :]
    gather_records(stride, parts, came, gathered)
    records = {o: gathered.at[o + REACH] for o in range(-REACH, REACH + 1)}
    rim = {o: rims.at[o + REACH] for o in records}
    rim_next = {o: rims_next.at[o + 1] for o in (-1, 0, 1)}
    left, right = CHUNKS, CHUNKS + 1
    local = list(range(CHUNKS))
    for o, record in records.items():
        rim[o][...] = rim_of(record, state_of(record))
    heads = {-2: [right], -1: local + [right], 0: local + [left, right], 1: local + [left], 2: [left]}
    ghosts = {o: (rim[o - 1], rim[o + 1]) for o in (-1, 1)}
    ghosts.update({-2: (rim[-1],), 2: (rim[1],)})
    sums, contacts = {}, {}
    for o, record in records.items():
        contacts[o] = first_lam(record, ghosts[o]) if o else ([known[k] for k in range(3)], known[3])
    for o, record in records.items():
        normal, lam = contacts[o]
        first, second = ends_of(record)
        force = [one * lam for one in normal]
        sums[o] = add_up(force, first, second, heads[o], rows.at[o + REACH])
    for o in (-1, 0, 1):
        incoming = sums[o - 1][right] + sums[o + 1][left]
        back = inverse([records[o][pl.ds(RIM_AT, 1), :]])
        if o == 0:
            back_here[...] = back
        blocks = [
            moved(was, sums[o][c], incoming, back[c : c + 1])
            for c, was in enumerate(state_of(records[o]))
        ]
        rim_next[o][...] = rim_of(records[o], blocks)
        for c in range(CHUNKS):
            state_next[o + 1, pl.ds(FIELDS * c, FIELDS), :] = blocks[c]
    ghosts = {-1: (rim_next[0],), 0: (rim_next[-1], rim_next[1]), 1: (rim_next[0],)}
    for o in (-1, 0, 1):
        normal, lam = contacts[o]
        first, second = ends_of(records[o])
        state = state_next.at[o + 1]
        speed = sum(
            normal[k] * difference(state, ghosts[o], 3 + k, first, second) for k in range(3)
        )
        for k in range(3):
            stage[o + 1, k] = normal[k]
        stage[o + 1, 3] = lam
        stage[o + 1, 4] = speed
        fixed_out[o + 1] = records[o][pl.ds(FIRST_AT, FIXED), :]


def last_kernel(
    parts, mine, stage, back, here, chip, mid, other, fixed, velocity, impulse, rows
):
    me = lax.axis_index("parts")
    odd = me % 2 == 1
    apart = (me % (2 * BLOCK) == BLOCK) | (me % (2 * BLOCK) == BLOCK - 1)
    across = jnp.where(apart, mid[...], other[...])
    across = jnp.where((me > 0) & (me < parts - 1), across, 0.0)
    coupled = {
        -1: jnp.where(odd, chip[...], across),
        0: here[...],
        1: jnp.where(odd, across, chip[...]),
    }
    sums = {}
    for o, heads in ((-1, [CHUNKS + 1]), (0, list(range(CHUNKS))), (1, [CHUNKS])):
        record = fixed.at[o + 1]
        lam = stage[o + 1, 3]
        diag = record[pl.ds(DIAG_AT - FIRST_AT, FIELDS), :]
        lam = jnp.maximum(0.0, lam - (coupled[o] + stage[o + 1, 4]) / diag)
        if o == 0:
            impulse[...] = lam
        first = record[pl.ds(0, FIELDS), :].astype(jnp.int32)
        second = record[pl.ds(SECOND_AT - FIRST_AT, FIELDS), :].astype(jnp.int32)
        force = [stage[o + 1, k] * lam for k in range(3)]
        sums[o] = add_up(force, first, second, heads, rows.at[o + 1])
    incoming = sums[-1][CHUNKS + 1] + sums[1][CHUNKS]
    for c, was in enumerate(state_of(mine)):
        block = moved(was, sums[0][c], incoming, back[pl.ds(c, 1), :])
        velocity[:, pl.ds(c * TILE, TILE)] = block[3:6]


def call(kernel, out_shape, inputs, name, space=pltpu.VMEM, scratch=()):
    many = isinstance(out_shape, (tuple, list))
    vmem = pl.BlockSpec(memory_space=pltpu.VMEM)
    return pl.pallas_call(
        kernel,
        out_shape=out_shape,
        in_specs=[pl.BlockSpec(memory_space=space)] * len(inputs),
        out_specs=[vmem] * len(out_shape) if many else vmem,
        scratch_shapes=list(scratch),
        compiler_params=FROM_HBM if space == pltpu.HBM else PARAMS,
        name=name,
    )(*inputs)


def second_parts(parts, stride):
    pairs = []
    for i in range(parts):
        step = -stride if i % stride < stride // 2 else stride
        to = i + step
        if not 0 <= to < parts:
            to = i + (stride // 2 if step < 0 else -(stride // 2))
        pairs.append((i, to))
    return pairs


def edges(parts):
    return range(BLOCK, parts, 2 * BLOCK)


def next_pairs(parts):
    most = {i: i + 1 if i % 2 else i - 1 for i in range(parts)}
    edge = {i: i ^ 1 for i in range(parts)}
    ends = [0]
    for at in edges(parts):
        ends += [at - 1, at]
        for i, j in ((at - 1, at), (at - 2, at + 2), (at + 1, at + 3)):
            edge[i], edge[j] = j, i
    ends.append(parts - 1)
    closings = [(0, BLOCK), (ends[-2], parts - 1)]
    for k in range(1, len(ends) - 4, 2):
        closings.append((ends[k], ends[k + 2]) if k % 4 == 1 else (ends[k + 1], ends[k + 3]))
    for i, j in closings:
        most[i], most[j] = j, i
    return list(most.items()), list(edge.items())


def body(positions, velocity, inv_mass, swap_lists, rim_list, contact_pair, delassus):
    parts = lax.axis_size("parts")
    stride = parts // GROUP
    grains = positions.shape[1]
    contacts = contact_pair.shape[1]
    tiles = delassus.shape[0]
    reach = 2 * REACH + 1
    float32 = functools.partial(jax.ShapeDtypeStruct, dtype=jnp.float32)
    vmem = lambda *shape: pltpu.VMEM(shape, jnp.float32)
    send = functools.partial(lax.ppermute, axis_name="parts")
    inputs = (
        positions,
        velocity,
        inv_mass.reshape(CHUNKS, TILE),
        swap_lists,
        rim_list.reshape(1, TILE),
    )
    packed = call(
        pack_kernel,
        float32((GROUP, RAW, TILE)),
        inputs,
        "pack",
        pltpu.HBM,
        [pltpu.VMEM(one.shape, one.dtype) for one in inputs]
        + [pltpu.SemaphoreType.DMA((5,))],
    )
    classes = [[r + stride * ((k - 2) % GROUP) for k in range(GROUP)] for r in range(stride)]
    raw = lax.all_to_all(packed, "parts", 0, 0, axis_index_groups=classes)

    half = jax.ShapeDtypeStruct(delassus.shape, jnp.bfloat16)
    fixed, heads, tails = call(
        fixed_kernel, (float32((FIXED, TILE)), half, half), (contact_pair, delassus), "fixed"
    )
    given = send(fixed, perm=second_parts(parts, stride))

    states = call(
        functools.partial(compose_kernel, stride),
        float32((2, FIRST_AT, TILE)),
        (raw,),
        "compose",
        scratch=[vmem(GROUP, FIRST_AT, TILE), vmem(4, FIRST_AT, TILE)],
    )
    record = (RECORD, TILE)
    mine, far, low, high = call(
        functools.partial(join_kernel, stride),
        [float32(record)] * 4,
        (states, fixed, given),
        "join",
    )
    within = [(i, i ^ 1) for i in range(parts)]
    if stride == BLOCK:
        from_far = send(far, perm=[(i, i ^ 3) for i in range(parts)])
        near = (mine, send(mine, perm=within), from_far)
        beyond = [(i, i ^ 2) for i in range(parts)]
        came = (*near, send(low, perm=beyond), send(high, perm=beyond))
    else:
        shifts = [[(i, (i + by) % parts) for i in range(parts)] for by in (1, -1, 2, -2)]
        came = (mine, *[send(mine, perm=shift) for shift in shifts])
        near = came[:3]

    here, known = call(
        functools.partial(near_kernel, stride, parts),
        (float32((tiles, TILE)), float32((4, tiles, TILE))),
        (*near, heads, tails),
        "near",
        scratch=[vmem(reach, *record), vmem(reach, FIELDS, TILE)],
    )
    most, edge = next_pairs(parts)
    other = send(here, perm=most)
    chip = send(here, perm=within)
    mid = send(here, perm=edge)
    stage, back, contact_rows = call(
        functools.partial(middle_kernel, stride, parts, len(came)),
        (
            float32((3, 5, FIELDS, TILE)),
            jax.ShapeDtypeStruct((FIELDS, TILE), jnp.int32),
            float32((3, FIXED, TILE)),
        ),
        (*came, known),
        "middle",
        scratch=[
            vmem(reach, *record),
            vmem(reach, FIELDS, TILE),
            vmem(reach, FIELDS * FIELDS, TILE),
            vmem(3, CHUNKS * FIELDS, TILE),
            vmem(3, FIELDS, TILE),
        ],
    )
    new_velocity, impulse = call(
        functools.partial(last_kernel, parts),
        (float32((3, grains)), float32((tiles, TILE))),
        (mine, stage, back, here, chip, mid, other, contact_rows),
        "last",
        scratch=[vmem(3, FIELDS * FIELDS, TILE)],
    )
    return (new_velocity, impulse.reshape(contacts))


def solution(mesh):
    in_specs = (
        P(None, "parts"),
        P(None, "parts"),
        P("parts"),
        P(None, "parts"),
        P("parts"),
        P(None, "parts"),
        P("parts", None, None),
    )
    out_specs = (P(None, "parts"), P("parts"))
    return jax.shard_map(body, mesh=mesh, in_specs=in_specs, out_specs=out_specs, check_vma=False)
```

```python
import functools

import jax
import jax.numpy as jnp
from jax import lax
from jax.experimental import pallas as pl
from jax.experimental.pallas import tpu as pltpu
from jax.sharding import PartitionSpec as P

TILE = 128
LEVELS = 3
GROUP = 2**LEVELS
REACH = 2
FIELDS = 8
CHUNKS = 4
EXT_CHUNKS = 6
RIM_AT = 7
FIRST_AT = 32
SECOND_AT = 40
DIAG_AT = 48
RECORD = 56
LISTS_AT = 32
RAW = 40
FIXED = RECORD - FIRST_AT
BLOCK = 4
LISTED = (7, 0, 6, 1, 2, 3, 4, 5)
PARAMS = pltpu.CompilerParams(vmem_limit_bytes=32 * 2**20)
FROM_HBM = pltpu.CompilerParams(vmem_limit_bytes=63 * 2**20)
NT = (((1,), (1,)), ((), ()))


def rows_iota(shape):
    return lax.broadcasted_iota(jnp.int32, shape, 0)


def lanes_iota(shape):
    return lax.broadcasted_iota(jnp.int32, shape, 1)


def wide(row):
    return jnp.broadcast_to(row, (FIELDS, TILE))


def take(table, lane):
    return jnp.take_along_axis(table, lane, axis=1, mode="promise_in_bounds")


def look_up(rows, index):
    lane, high = index & (TILE - 1), index >> 7
    found = take(wide(rows[0]), lane)
    for h in range(1, len(rows)):
        found = jnp.where(high == h, take(wide(rows[h]), lane), found)
    return found


def one_hot(low_row):
    row = jnp.broadcast_to(low_row.astype(jnp.float32).astype(jnp.bfloat16), (TILE, TILE))
    column = rows_iota((TILE, TILE)).astype(jnp.float32).astype(jnp.bfloat16)
    return jnp.where(row == column, jnp.bfloat16(1), jnp.bfloat16(0))


def inverse(slot_rows):
    left, right = [], []
    for at, row in enumerate(slot_rows):
        slots = row.astype(jnp.int32)
        place = (lanes_iota((FIELDS, TILE)) + (at * TILE + 1)).astype(jnp.float32)
        heads = jnp.where(wide(slots >> 7) == rows_iota((FIELDS, TILE)), place, 0.0)
        left.append(heads.astype(jnp.bfloat16))
        right.append(one_hot(slots & (TILE - 1)))
    total = lax.dot_general(
        jnp.concatenate(left, axis=1),
        jnp.concatenate(right, axis=1),
        NT,
        preferred_element_type=jnp.float32,
    )
    return total.astype(jnp.int32)


def pack_kernel(*refs):
    sources, out, held, sems = refs[:5], refs[5], refs[6:11], refs[11]
    copies = [
        pltpu.make_async_copy(source, target, sems.at[k])
        for k, (source, target) in enumerate(zip(sources, held))
    ]
    for copy in copies:
        copy.start()
    pos, vel, mass, lists, rim = held
    for copy in copies:
        copy.wait()
    first = out.at[0]
    for c in range(CHUNKS):
        lanes = pl.ds(c * TILE, TILE)
        first[pl.ds(FIELDS * c, 3), :] = pos[:, lanes]
        first[pl.ds(FIELDS * c + 3, 3), :] = vel[:, lanes]
        first[pl.ds(FIELDS * c + 6, 1), :] = mass[pl.ds(c, 1), :]
        spare = rim[...].astype(jnp.float32) if c == 0 else jnp.zeros((1, TILE), jnp.float32)
        first[pl.ds(FIELDS * c + 7, 1), :] = spare
    for level in range(LEVELS):
        for h in range(2):
            row = lists[pl.ds(level, 1), pl.ds(h * TILE, TILE)]
            first[pl.ds(LISTS_AT + 2 * level + h, 1), :] = row.astype(jnp.float32)
    first[pl.ds(LISTS_AT + 2 * LEVELS, 2), :] = jnp.zeros((2, TILE), jnp.float32)
    whole = first[...]
    for m in range(1, GROUP):
        out[m] = whole


def fixed_kernel(pair, tiles, out, heads, tails):
    eye = rows_iota((TILE, TILE)) == lanes_iota((TILE, TILE))
    for t in range(tiles.shape[0]):
        lanes = pl.ds(t * TILE, TILE)
        out[pl.ds(t, 1), :] = pair[pl.ds(0, 1), lanes].astype(jnp.float32)
        out[pl.ds(FIELDS + t, 1), :] = pair[pl.ds(1, 1), lanes].astype(jnp.float32)
        tile = tiles[t]
        turned = tile.T
        head = turned.astype(jnp.bfloat16)
        heads[t] = head
        tails[t] = (turned - head.astype(jnp.float32)).astype(jnp.bfloat16)
        diag = jnp.sum(jnp.where(eye, tile, 0.0), axis=0, keepdims=True)
        out[pl.ds(2 * FIELDS + t, 1), :] = diag


def place_of(block):
    if isinstance(block, int):
        return LISTED.index(block)
    return sum(jnp.where(block == one, at, 0) for at, one in enumerate(LISTED))


def second_part(stride):
    me = lax.axis_index("parts")
    member, kind = me // stride, me % stride
    step = jnp.where(kind < stride // 2, 1, -1)
    return step, (member + step >= 0) & (member + step < GROUP)


def swapped(lists, other_lists, own, other, out):
    back = inverse(lists)
    place = jnp.maximum(back - 1, 0)
    slot = look_up(other_lists, place).astype(jnp.int32)
    lane = slot & (TILE - 1)
    block = jnp.where(back > 0, slot >> 7, -1)
    tables = [other[pl.ds(FIELDS * h, FIELDS), :] for h in range(CHUNKS)]
    for c in range(CHUNKS):
        rows = pl.ds(FIELDS * c, FIELDS)
        lane_c, block_c = wide(lane[c : c + 1]), wide(block[c : c + 1])
        found = own[rows, :]
        for h, table in enumerate(tables):
            found = jnp.where(block_c == h, take(table, lane_c), found)
        out[rows, :] = found


def compose_kernel(stride, raw, own, once, twice):
    member = lax.axis_index("parts") // stride
    step, exists = second_part(stride)

    def came_from(part):
        return raw.at[place_of(part)]

    def list_rows(part, level):
        rows = came_from(part)
        return [rows[pl.ds(LISTS_AT + 2 * level + h, 1), :] for h in range(2)]

    def level_step(level, part, apart, own_state, other_state, out):
        lists, others = list_rows(part, level), list_rows(part ^ apart, level)
        swapped(lists, others, own_state, other_state, out)

    for r in range(GROUP):
        level_step(0, r, 4, came_from(r), came_from(r ^ 4), once.at[r])
    second = (member + step + GROUP) % GROUP
    for i, part in enumerate((member, member ^ 1, second, second ^ 1)):
        level_step(1, part, 2, once.at[part], once.at[part ^ 2], twice.at[i])
    for i, part in enumerate((member, second)):
        level_step(2, part, 1, twice.at[2 * i], twice.at[2 * i + 1], own.at[i])
        own[i, pl.ds(RIM_AT, 1), :] = came_from(part)[pl.ds(RIM_AT, 1), :]
    for c in range(CHUNKS):
        rows = pl.ds(FIELDS * c, FIELDS)
        own[1, rows, :] = jnp.where(exists, own[1, rows, :], 0.0)


def join_kernel(stride, states, fixed, given, mine, far, low, high):
    kind = lax.axis_index("parts") % stride
    exists = second_part(stride)[1]
    early, outer = kind < stride // 2, (kind == 0) | (kind == stride - 1)
    for at in range(0, RECORD, FIELDS):
        rows = pl.ds(at, FIELDS)
        if at < FIRST_AT:
            one, two = states[0, rows, :], states[1, rows, :]
        else:
            part = pl.ds(at - FIRST_AT, FIELDS)
            absent = 1.0 if at == DIAG_AT else 0.0
            one, two = fixed[part, :], jnp.where(exists, given[part, :], absent)
        mine[rows, :] = one
        far[rows, :] = jnp.where(outer, two, one)
        low[rows, :] = jnp.where(early, one, two)
        high[rows, :] = jnp.where(early, two, one)


def gather_records(stride, parts, came, records):
    me = lax.axis_index("parts")
    swap = (stride == BLOCK) & (me % 2 == 0)
    mine, one, two, *side = came
    for at in range(0, RECORD, FIELDS):
        rows = pl.ds(at, FIELDS)
        blocks = {
            0: mine[rows, :],
            -1: jnp.where(swap, two[rows, :], one[rows, :]),
            1: jnp.where(swap, one[rows, :], two[rows, :]),
        }
        if side:
            blocks[-2], blocks[2] = side[0][rows, :], side[1][rows, :]
        for o, block in blocks.items():
            absent = 1.0 if at == DIAG_AT else 0.0
            there = (me + o >= 0) & (me + o < parts)
            records[o + REACH, rows, :] = jnp.where(there, block, absent) if o else block


def state_of(record):
    return [record[pl.ds(FIELDS * c, FIELDS), :] for c in range(CHUNKS)]


def ends_of(record):
    first = record[pl.ds(FIRST_AT, FIELDS), :].astype(jnp.int32)
    second = record[pl.ds(SECOND_AT, FIELDS), :].astype(jnp.int32)
    return first, second


def diag_of(record):
    return record[pl.ds(DIAG_AT, FIELDS), :]


def rim_of(record, blocks):
    slots = wide(record[pl.ds(RIM_AT, 1), :].astype(jnp.int32))
    lane, high = slots & (TILE - 1), slots >> 7
    found = take(blocks[0], lane)
    for c in range(1, CHUNKS):
        found = jnp.where(high == c, take(blocks[c], lane), found)
    return found


def difference(local, ghosts, field, first, second):
    near = [local[pl.ds(FIELDS * c + field, 1), :] for c in range(CHUNKS)]
    far = [one[pl.ds(field, 1), :] for one in ghosts]
    return look_up(near, first) - look_up(near + far if len(far) > 1 else far, second)


def first_lam(record, ghosts):
    first, second = ends_of(record)
    normal = [difference(record, ghosts, k, first, second) for k in range(3)]
    speed = sum(normal[k] * difference(record, ghosts, 3 + k, first, second) for k in range(3))
    return normal, jnp.maximum(0.0, -speed / diag_of(record))


def add_up(force, first, second, heads, rows):
    for k in range(3):
        head = force[k].astype(jnp.bfloat16).astype(jnp.float32)
        rows[pl.ds(k, FIELDS, stride=FIELDS), :] = force[k] - head
        rows[pl.ds(3 + k, FIELDS, stride=FIELDS), :] = head
    empty = jnp.zeros((FIELDS, TILE), jnp.float32)
    pad = [empty] * (len(heads) % 2)
    left, right = [], []
    for t in range(FIELDS):
        value = rows[pl.ds(FIELDS * t, FIELDS), :]
        for index, limit, signed in ((first, CHUNKS, value), (second, EXT_CHUNKS, -value)):
            if min(heads) >= limit:
                continue
            row = index[t : t + 1]
            high = wide(row >> 7)
            groups = [jnp.where(high == h, signed, 0.0) if h < limit else empty for h in heads]
            left.append(jnp.concatenate(groups + pad, axis=0))
            right.append(one_hot(row & (TILE - 1)))
    total = lax.dot_general(
        jnp.concatenate(left, axis=1).astype(jnp.bfloat16),
        jnp.concatenate(right, axis=1),
        NT,
        preferred_element_type=jnp.float32,
    )
    blocks = [total[FIELDS * k : FIELDS * (k + 1)] for k in range(len(heads))]
    return {h: block + pltpu.roll(block, 3, 0) for h, block in zip(heads, blocks)}


def moved(was, here, incoming, back_row):
    place = wide(back_row)
    extra = jnp.where(place > 0, take(incoming, jnp.maximum(place - 1, 0)), 0.0)
    field = rows_iota((FIELDS, TILE))
    gain = wide(was[6:7]) * (here + extra)
    return was + jnp.where((field >= 3) & (field < 6), gain, 0.0)


def near_kernel(stride, parts, *refs):
    came, (heads, tails, coupled, contacts, records, rims) = refs[:3], refs[3:]
    gather_records(stride, parts, came, records)
    for k in (-1, 1):
        record = records.at[REACH + k]
        rims[REACH + k] = rim_of(record, state_of(record))
    normal, lam = first_lam(records.at[REACH], (rims.at[REACH - 1], rims.at[REACH + 1]))
    for k, one in enumerate((*normal, lam)):
        contacts[k] = one
    head = lam.astype(jnp.bfloat16).astype(jnp.float32)
    both = jnp.concatenate([head, lam - head], axis=0).astype(jnp.bfloat16)
    total = jnp.zeros((FIELDS, TILE), jnp.float32)
    for t in range(heads.shape[0]):
        main = jnp.dot(both, heads[t], preferred_element_type=jnp.float32)
        rest = jnp.dot(both, tails[t], preferred_element_type=jnp.float32)
        whole = main[:FIELDS] + main[FIELDS:] + rest[:FIELDS]
        total = jnp.where(rows_iota((FIELDS, TILE)) == t, whole, total)
    coupled[...] = total


def middle_kernel(stride, parts, count, *refs):
    came, known = refs[:count], refs[count]
    stage, back_here, fixed_out, gathered, rims, rows, state_next, rims_next = refs[count + 1 :]
    gather_records(stride, parts, came, gathered)
    records = {o: gathered.at[o + REACH] for o in range(-REACH, REACH + 1)}
    rim = {o: rims.at[o + REACH] for o in records}
    rim_next = {o: rims_next.at[o + 1] for o in (-1, 0, 1)}
    left, right = CHUNKS, CHUNKS + 1
    local = list(range(CHUNKS))
    for o, record in records.items():
        rim[o][...] = rim_of(record, state_of(record))
    heads = {-2: [right], -1: local + [right], 0: local + [left, right], 1: local + [left], 2: [left]}
    ghosts = {o: (rim[o - 1], rim[o + 1]) for o in (-1, 1)}
    ghosts.update({-2: (rim[-1],), 2: (rim[1],)})
    sums, contacts = {}, {}
    for o, record in records.items():
        contacts[o] = first_lam(record, ghosts[o]) if o else ([known[k] for k in range(3)], known[3])
    for o, record in records.items():
        normal, lam = contacts[o]
        first, second = ends_of(record)
        force = [one * lam for one in normal]
        sums[o] = add_up(force, first, second, heads[o], rows.at[o + REACH])
    for o in (-1, 0, 1):
        incoming = sums[o - 1][right] + sums[o + 1][left]
        back = inverse([records[o][pl.ds(RIM_AT, 1), :]])
        if o == 0:
            back_here[...] = back
        blocks = [
            moved(was, sums[o][c], incoming, back[c : c + 1])
            for c, was in enumerate(state_of(records[o]))
        ]
        rim_next[o][...] = rim_of(records[o], blocks)
        for c in range(CHUNKS):
            state_next[o + 1, pl.ds(FIELDS * c, FIELDS), :] = blocks[c]
    ghosts = {-1: (rim_next[0],), 0: (rim_next[-1], rim_next[1]), 1: (rim_next[0],)}
    for o in (-1, 0, 1):
        normal, lam = contacts[o]
        first, second = ends_of(records[o])
        state = state_next.at[o + 1]
        speed = sum(
            normal[k] * difference(state, ghosts[o], 3 + k, first, second) for k in range(3)
        )
        for k in range(3):
            stage[o + 1, k] = normal[k]
        stage[o + 1, 3] = lam
        stage[o + 1, 4] = speed
        fixed_out[o + 1] = records[o][pl.ds(FIRST_AT, FIXED), :]


def last_kernel(
    parts, mine, stage, back, here, chip, mid, other, fixed, velocity, impulse, rows
):
    me = lax.axis_index("parts")
    odd = me % 2 == 1
    apart = (me % (2 * BLOCK) == BLOCK) | (me % (2 * BLOCK) == BLOCK - 1)
    across = jnp.where(apart, mid[...], other[...])
    across = jnp.where((me > 0) & (me < parts - 1), across, 0.0)
    coupled = {
        -1: jnp.where(odd, chip[...], across),
        0: here[...],
        1: jnp.where(odd, across, chip[...]),
    }
    sums = {}
    for o, heads in ((-1, [CHUNKS + 1]), (0, list(range(CHUNKS))), (1, [CHUNKS])):
        record = fixed.at[o + 1]
        lam = stage[o + 1, 3]
        diag = record[pl.ds(DIAG_AT - FIRST_AT, FIELDS), :]
        lam = jnp.maximum(0.0, lam - (coupled[o] + stage[o + 1, 4]) / diag)
        if o == 0:
            impulse[...] = lam
        first = record[pl.ds(0, FIELDS), :].astype(jnp.int32)
        second = record[pl.ds(SECOND_AT - FIRST_AT, FIELDS), :].astype(jnp.int32)
        force = [stage[o + 1, k] * lam for k in range(3)]
        sums[o] = add_up(force, first, second, heads, rows.at[o + 1])
    incoming = sums[-1][CHUNKS + 1] + sums[1][CHUNKS]
    for c, was in enumerate(state_of(mine)):
        block = moved(was, sums[0][c], incoming, back[pl.ds(c, 1), :])
        velocity[:, pl.ds(c * TILE, TILE)] = block[3:6]


def call(kernel, out_shape, inputs, name, space=pltpu.VMEM, scratch=()):
    many = isinstance(out_shape, (tuple, list))
    vmem = pl.BlockSpec(memory_space=pltpu.VMEM)
    return pl.pallas_call(
        kernel,
        out_shape=out_shape,
        in_specs=[pl.BlockSpec(memory_space=space)] * len(inputs),
        out_specs=[vmem] * len(out_shape) if many else vmem,
        scratch_shapes=list(scratch),
        compiler_params=FROM_HBM if space == pltpu.HBM else PARAMS,
        name=name,
    )(*inputs)


def second_parts(parts, stride):
    pairs = []
    for i in range(parts):
        step = -stride if i % stride < stride // 2 else stride
        to = i + step
        if not 0 <= to < parts:
            to = i + (stride // 2 if step < 0 else -(stride // 2))
        pairs.append((i, to))
    return pairs


def edges(parts):
    return range(BLOCK, parts, 2 * BLOCK)


def next_pairs(parts):
    most = {i: i + 1 if i % 2 else i - 1 for i in range(parts)}
    edge = {i: i ^ 1 for i in range(parts)}
    ends = [0]
    for at in edges(parts):
        ends += [at - 1, at]
        for i, j in ((at - 1, at), (at - 2, at + 2), (at + 1, at + 3)):
            edge[i], edge[j] = j, i
    ends.append(parts - 1)
    closings = [(0, BLOCK), (ends[-2], parts - 1)]
    for k in range(1, len(ends) - 4, 2):
        closings.append((ends[k], ends[k + 2]) if k % 4 == 1 else (ends[k + 1], ends[k + 3]))
    for i, j in closings:
        most[i], most[j] = j, i
    return list(most.items()), list(edge.items())


def body(positions, velocity, inv_mass, swap_lists, rim_list, contact_pair, delassus):
    parts = lax.axis_size("parts")
    stride = parts // GROUP
    grains = positions.shape[1]
    contacts = contact_pair.shape[1]
    tiles = delassus.shape[0]
    reach = 2 * REACH + 1
    float32 = functools.partial(jax.ShapeDtypeStruct, dtype=jnp.float32)
    vmem = lambda *shape: pltpu.VMEM(shape, jnp.float32)
    send = functools.partial(lax.ppermute, axis_name="parts")
    inputs = (
        positions,
        velocity,
        inv_mass.reshape(CHUNKS, TILE),
        swap_lists,
        rim_list.reshape(1, TILE),
    )
    packed = call(
        pack_kernel,
        float32((GROUP, RAW, TILE)),
        inputs,
        "pack",
        pltpu.HBM,
        [pltpu.VMEM(one.shape, one.dtype) for one in inputs]
        + [pltpu.SemaphoreType.DMA((5,))],
    )
    classes = [[r + stride * k for k in LISTED] for r in range(stride)]
    raw = lax.all_to_all(packed, "parts", 0, 0, axis_index_groups=classes)

    half = jax.ShapeDtypeStruct(delassus.shape, jnp.bfloat16)
    fixed, heads, tails = call(
        fixed_kernel, (float32((FIXED, TILE)), half, half), (contact_pair, delassus), "fixed"
    )
    given = send(fixed, perm=second_parts(parts, stride))

    states = call(
        functools.partial(compose_kernel, stride),
        float32((2, FIRST_AT, TILE)),
        (raw,),
        "compose",
        scratch=[vmem(GROUP, FIRST_AT, TILE), vmem(4, FIRST_AT, TILE)],
    )
    record = (RECORD, TILE)
    mine, far, low, high = call(
        functools.partial(join_kernel, stride),
        [float32(record)] * 4,
        (states, fixed, given),
        "join",
    )
    within = [(i, i ^ 1) for i in range(parts)]
    if stride == BLOCK:
        from_far = send(far, perm=[(i, i ^ 3) for i in range(parts)])
        near = (mine, send(mine, perm=within), from_far)
        beyond = [(i, i ^ 2) for i in range(parts)]
        came = (*near, send(low, perm=beyond), send(high, perm=beyond))
    else:
        shifts = [[(i, (i + by) % parts) for i in range(parts)] for by in (1, -1, 2, -2)]
        came = (mine, *[send(mine, perm=shift) for shift in shifts])
        near = came[:3]

    here, known = call(
        functools.partial(near_kernel, stride, parts),
        (float32((tiles, TILE)), float32((4, tiles, TILE))),
        (*near, heads, tails),
        "near",
        scratch=[vmem(reach, *record), vmem(reach, FIELDS, TILE)],
    )
    most, edge = next_pairs(parts)
    other = send(here, perm=most)
    chip = send(here, perm=within)
    mid = send(here, perm=edge)
    stage, back, contact_rows = call(
        functools.partial(middle_kernel, stride, parts, len(came)),
        (
            float32((3, 5, FIELDS, TILE)),
            jax.ShapeDtypeStruct((FIELDS, TILE), jnp.int32),
            float32((3, FIXED, TILE)),
        ),
        (*came, known),
        "middle",
        scratch=[
            vmem(reach, *record),
            vmem(reach, FIELDS, TILE),
            vmem(reach, FIELDS * FIELDS, TILE),
            vmem(3, CHUNKS * FIELDS, TILE),
            vmem(3, FIELDS, TILE),
        ],
    )
    new_velocity, impulse = call(
        functools.partial(last_kernel, parts),
        (float32((3, grains)), float32((tiles, TILE))),
        (mine, stage, back, here, chip, mid, other, contact_rows),
        "last",
        scratch=[vmem(3, FIELDS * FIELDS, TILE)],
    )
    return (new_velocity, impulse.reshape(contacts))


def solution(mesh):
    in_specs = (
        P(None, "parts"),
        P(None, "parts"),
        P("parts"),
        P(None, "parts"),
        P("parts"),
        P(None, "parts"),
        P("parts", None, None),
    )
    out_specs = (P(None, "parts"), P("parts"))
    return jax.shard_map(body, mesh=mesh, in_specs=in_specs, out_specs=out_specs, check_vma=False)
```

```python
import functools

import jax
import jax.numpy as jnp
from jax import lax
from jax.experimental import pallas as pl
from jax.experimental.pallas import tpu as pltpu
from jax.sharding import PartitionSpec as P

TILE = 128
LEVELS = 3
GROUP = 2**LEVELS
REACH = 2
FIELDS = 8
CHUNKS = 4
EXT_CHUNKS = 6
RIM_AT = 7
FIRST_AT = 32
SECOND_AT = 40
DIAG_AT = 48
RECORD = 56
LISTS_AT = 32
RAW = 40
FIXED = RECORD - FIRST_AT
BLOCK = 4
LISTED = (2, 0, 1, 3, 4, 5, 6, 7)
PARAMS = pltpu.CompilerParams(vmem_limit_bytes=32 * 2**20)
FROM_HBM = pltpu.CompilerParams(vmem_limit_bytes=63 * 2**20)
NT = (((1,), (1,)), ((), ()))


def rows_iota(shape):
    return lax.broadcasted_iota(jnp.int32, shape, 0)


def lanes_iota(shape):
    return lax.broadcasted_iota(jnp.int32, shape, 1)


def wide(row):
    return jnp.broadcast_to(row, (FIELDS, TILE))


def take(table, lane):
    return jnp.take_along_axis(table, lane, axis=1, mode="promise_in_bounds")


def look_up(rows, index):
    lane, high = index & (TILE - 1), index >> 7
    found = take(wide(rows[0]), lane)
    for h in range(1, len(rows)):
        found = jnp.where(high == h, take(wide(rows[h]), lane), found)
    return found


def one_hot(low_row):
    row = jnp.broadcast_to(low_row.astype(jnp.float32).astype(jnp.bfloat16), (TILE, TILE))
    column = rows_iota((TILE, TILE)).astype(jnp.float32).astype(jnp.bfloat16)
    return jnp.where(row == column, jnp.bfloat16(1), jnp.bfloat16(0))


def inverse(slot_rows):
    left, right = [], []
    for at, row in enumerate(slot_rows):
        slots = row.astype(jnp.int32)
        place = (lanes_iota((FIELDS, TILE)) + (at * TILE + 1)).astype(jnp.float32)
        heads = jnp.where(wide(slots >> 7) == rows_iota((FIELDS, TILE)), place, 0.0)
        left.append(heads.astype(jnp.bfloat16))
        right.append(one_hot(slots & (TILE - 1)))
    total = lax.dot_general(
        jnp.concatenate(left, axis=1),
        jnp.concatenate(right, axis=1),
        NT,
        preferred_element_type=jnp.float32,
    )
    return total.astype(jnp.int32)


def pack_kernel(*refs):
    sources, out, held, sems = refs[:5], refs[5], refs[6:11], refs[11]
    copies = [
        pltpu.make_async_copy(source, target, sems.at[k])
        for k, (source, target) in enumerate(zip(sources, held))
    ]
    for copy in copies:
        copy.start()
    pos, vel, mass, lists, rim = held
    for copy in copies:
        copy.wait()
    first = out.at[0]
    for c in range(CHUNKS):
        lanes = pl.ds(c * TILE, TILE)
        first[pl.ds(FIELDS * c, 3), :] = pos[:, lanes]
        first[pl.ds(FIELDS * c + 3, 3), :] = vel[:, lanes]
        first[pl.ds(FIELDS * c + 6, 1), :] = mass[pl.ds(c, 1), :]
        spare = rim[...].astype(jnp.float32) if c == 0 else jnp.zeros((1, TILE), jnp.float32)
        first[pl.ds(FIELDS * c + 7, 1), :] = spare
    for level in range(LEVELS):
        for h in range(2):
            row = lists[pl.ds(level, 1), pl.ds(h * TILE, TILE)]
            first[pl.ds(LISTS_AT + 2 * level + h, 1), :] = row.astype(jnp.float32)
    first[pl.ds(LISTS_AT + 2 * LEVELS, 2), :] = jnp.zeros((2, TILE), jnp.float32)
    whole = first[...]
    for m in range(1, GROUP):
        out[m] = whole


def fixed_kernel(pair, tiles, out, heads, tails):
    eye = rows_iota((TILE, TILE)) == lanes_iota((TILE, TILE))
    for t in range(tiles.shape[0]):
        lanes = pl.ds(t * TILE, TILE)
        out[pl.ds(t, 1), :] = pair[pl.ds(0, 1), lanes].astype(jnp.float32)
        out[pl.ds(FIELDS + t, 1), :] = pair[pl.ds(1, 1), lanes].astype(jnp.float32)
        tile = tiles[t]
        turned = tile.T
        head = turned.astype(jnp.bfloat16)
        heads[t] = head
        tails[t] = (turned - head.astype(jnp.float32)).astype(jnp.bfloat16)
        diag = jnp.sum(jnp.where(eye, tile, 0.0), axis=0, keepdims=True)
        out[pl.ds(2 * FIELDS + t, 1), :] = diag


def place_of(block):
    if isinstance(block, int):
        return LISTED.index(block)
    return sum(jnp.where(block == one, at, 0) for at, one in enumerate(LISTED))


def second_part(stride):
    me = lax.axis_index("parts")
    member, kind = me // stride, me % stride
    step = jnp.where(kind < stride // 2, 1, -1)
    return step, (member + step >= 0) & (member + step < GROUP)


def swapped(lists, other_lists, own, other, out):
    back = inverse(lists)
    place = jnp.maximum(back - 1, 0)
    slot = look_up(other_lists, place).astype(jnp.int32)
    lane = slot & (TILE - 1)
    block = jnp.where(back > 0, slot >> 7, -1)
    tables = [other[pl.ds(FIELDS * h, FIELDS), :] for h in range(CHUNKS)]
    for c in range(CHUNKS):
        rows = pl.ds(FIELDS * c, FIELDS)
        lane_c, block_c = wide(lane[c : c + 1]), wide(block[c : c + 1])
        found = own[rows, :]
        for h, table in enumerate(tables):
            found = jnp.where(block_c == h, take(table, lane_c), found)
        out[rows, :] = found


def compose_kernel(stride, raw, own, once, twice):
    member = lax.axis_index("parts") // stride
    step, exists = second_part(stride)

    def came_from(part):
        return raw.at[place_of(part)]

    def list_rows(part, level):
        rows = came_from(part)
        return [rows[pl.ds(LISTS_AT + 2 * level + h, 1), :] for h in range(2)]

    def level_step(level, part, apart, own_state, other_state, out):
        lists, others = list_rows(part, level), list_rows(part ^ apart, level)
        swapped(lists, others, own_state, other_state, out)

    for r in range(GROUP):
        level_step(0, r, 4, came_from(r), came_from(r ^ 4), once.at[r])
    second = (member + step + GROUP) % GROUP
    for i, part in enumerate((member, member ^ 1, second, second ^ 1)):
        level_step(1, part, 2, once.at[part], once.at[part ^ 2], twice.at[i])
    for i, part in enumerate((member, second)):
        level_step(2, part, 1, twice.at[2 * i], twice.at[2 * i + 1], own.at[i])
        own[i, pl.ds(RIM_AT, 1), :] = came_from(part)[pl.ds(RIM_AT, 1), :]
    for c in range(CHUNKS):
        rows = pl.ds(FIELDS * c, FIELDS)
        own[1, rows, :] = jnp.where(exists, own[1, rows, :], 0.0)


def join_kernel(stride, states, fixed, given, mine, far, low, high):
    kind = lax.axis_index("parts") % stride
    exists = second_part(stride)[1]
    early, outer = kind < stride // 2, (kind == 0) | (kind == stride - 1)
    for at in range(0, RECORD, FIELDS):
        rows = pl.ds(at, FIELDS)
        if at < FIRST_AT:
            one, two = states[0, rows, :], states[1, rows, :]
        else:
            part = pl.ds(at - FIRST_AT, FIELDS)
            absent = 1.0 if at == DIAG_AT else 0.0
            one, two = fixed[part, :], jnp.where(exists, given[part, :], absent)
        mine[rows, :] = one
        far[rows, :] = jnp.where(outer, two, one)
        low[rows, :] = jnp.where(early, one, two)
        high[rows, :] = jnp.where(early, two, one)


def gather_records(stride, parts, came, records):
    me = lax.axis_index("parts")
    swap = (stride == BLOCK) & (me % 2 == 0)
    mine, one, two, *side = came
    for at in range(0, RECORD, FIELDS):
        rows = pl.ds(at, FIELDS)
        blocks = {
            0: mine[rows, :],
            -1: jnp.where(swap, two[rows, :], one[rows, :]),
            1: jnp.where(swap, one[rows, :], two[rows, :]),
        }
        if side:
            blocks[-2], blocks[2] = side[0][rows, :], side[1][rows, :]
        for o, block in blocks.items():
            absent = 1.0 if at == DIAG_AT else 0.0
            there = (me + o >= 0) & (me + o < parts)
            records[o + REACH, rows, :] = jnp.where(there, block, absent) if o else block


def state_of(record):
    return [record[pl.ds(FIELDS * c, FIELDS), :] for c in range(CHUNKS)]


def ends_of(record):
    first = record[pl.ds(FIRST_AT, FIELDS), :].astype(jnp.int32)
    second = record[pl.ds(SECOND_AT, FIELDS), :].astype(jnp.int32)
    return first, second


def diag_of(record):
    return record[pl.ds(DIAG_AT, FIELDS), :]


def rim_of(record, blocks):
    slots = wide(record[pl.ds(RIM_AT, 1), :].astype(jnp.int32))
    lane, high = slots & (TILE - 1), slots >> 7
    found = take(blocks[0], lane)
    for c in range(1, CHUNKS):
        found = jnp.where(high == c, take(blocks[c], lane), found)
    return found


def difference(local, ghosts, field, first, second):
    near = [local[pl.ds(FIELDS * c + field, 1), :] for c in range(CHUNKS)]
    far = [one[pl.ds(field, 1), :] for one in ghosts]
    return look_up(near, first) - look_up(near + far if len(far) > 1 else far, second)


def first_lam(record, ghosts):
    first, second = ends_of(record)
    normal = [difference(record, ghosts, k, first, second) for k in range(3)]
    speed = sum(normal[k] * difference(record, ghosts, 3 + k, first, second) for k in range(3))
    return normal, jnp.maximum(0.0, -speed / diag_of(record))


def add_up(force, first, second, heads, rows):
    for k in range(3):
        head = force[k].astype(jnp.bfloat16).astype(jnp.float32)
        rows[pl.ds(k, FIELDS, stride=FIELDS), :] = force[k] - head
        rows[pl.ds(3 + k, FIELDS, stride=FIELDS), :] = head
    empty = jnp.zeros((FIELDS, TILE), jnp.float32)
    pad = [empty] * (len(heads) % 2)
    left, right = [], []
    for t in range(FIELDS):
        value = rows[pl.ds(FIELDS * t, FIELDS), :]
        for index, limit, signed in ((first, CHUNKS, value), (second, EXT_CHUNKS, -value)):
            if min(heads) >= limit:
                continue
            row = index[t : t + 1]
            high = wide(row >> 7)
            groups = [jnp.where(high == h, signed, 0.0) if h < limit else empty for h in heads]
            left.append(jnp.concatenate(groups + pad, axis=0))
            right.append(one_hot(row & (TILE - 1)))
    total = lax.dot_general(
        jnp.concatenate(left, axis=1).astype(jnp.bfloat16),
        jnp.concatenate(right, axis=1),
        NT,
        preferred_element_type=jnp.float32,
    )
    blocks = [total[FIELDS * k : FIELDS * (k + 1)] for k in range(len(heads))]
    return {h: block + pltpu.roll(block, 3, 0) for h, block in zip(heads, blocks)}


def moved(was, here, incoming, back_row):
    place = wide(back_row)
    extra = jnp.where(place > 0, take(incoming, jnp.maximum(place - 1, 0)), 0.0)
    field = rows_iota((FIELDS, TILE))
    gain = wide(was[6:7]) * (here + extra)
    return was + jnp.where((field >= 3) & (field < 6), gain, 0.0)


def near_kernel(stride, parts, *refs):
    came, (heads, tails, coupled, contacts, records, rims) = refs[:3], refs[3:]
    gather_records(stride, parts, came, records)
    for k in (-1, 1):
        record = records.at[REACH + k]
        rims[REACH + k] = rim_of(record, state_of(record))
    normal, lam = first_lam(records.at[REACH], (rims.at[REACH - 1], rims.at[REACH + 1]))
    for k, one in enumerate((*normal, lam)):
        contacts[k] = one
    head = lam.astype(jnp.bfloat16).astype(jnp.float32)
    both = jnp.concatenate([head, lam - head], axis=0).astype(jnp.bfloat16)
    total = jnp.zeros((FIELDS, TILE), jnp.float32)
    for t in range(heads.shape[0]):
        main = jnp.dot(both, heads[t], preferred_element_type=jnp.float32)
        rest = jnp.dot(both, tails[t], preferred_element_type=jnp.float32)
        whole = main[:FIELDS] + main[FIELDS:] + rest[:FIELDS]
        total = jnp.where(rows_iota((FIELDS, TILE)) == t, whole, total)
    coupled[...] = total


def middle_kernel(stride, parts, count, *refs):
    came, known = refs[:count], refs[count]
    stage, back_here, fixed_out, gathered, rims, rows, state_next, rims_next = refs[count + 1 :]
    gather_records(stride, parts, came, gathered)
    records = {o: gathered.at[o + REACH] for o in range(-REACH, REACH + 1)}
    rim = {o: rims.at[o + REACH] for o in records}
    rim_next = {o: rims_next.at[o + 1] for o in (-1, 0, 1)}
    left, right = CHUNKS, CHUNKS + 1
    local = list(range(CHUNKS))
    for o, record in records.items():
        rim[o][...] = rim_of(record, state_of(record))
    heads = {-2: [right], -1: local + [right], 0: local + [left, right], 1: local + [left], 2: [left]}
    ghosts = {o: (rim[o - 1], rim[o + 1]) for o in (-1, 1)}
    ghosts.update({-2: (rim[-1],), 2: (rim[1],)})
    sums, contacts = {}, {}
    for o, record in records.items():
        contacts[o] = first_lam(record, ghosts[o]) if o else ([known[k] for k in range(3)], known[3])
    for o, record in records.items():
        normal, lam = contacts[o]
        first, second = ends_of(record)
        force = [one * lam for one in normal]
        sums[o] = add_up(force, first, second, heads[o], rows.at[o + REACH])
    for o in (-1, 0, 1):
        incoming = sums[o - 1][right] + sums[o + 1][left]
        back = inverse([records[o][pl.ds(RIM_AT, 1), :]])
        if o == 0:
            back_here[...] = back
        blocks = [
            moved(was, sums[o][c], incoming, back[c : c + 1])
            for c, was in enumerate(state_of(records[o]))
        ]
        rim_next[o][...] = rim_of(records[o], blocks)
        for c in range(CHUNKS):
            state_next[o + 1, pl.ds(FIELDS * c, FIELDS), :] = blocks[c]
    ghosts = {-1: (rim_next[0],), 0: (rim_next[-1], rim_next[1]), 1: (rim_next[0],)}
    for o in (-1, 0, 1):
        normal, lam = contacts[o]
        first, second = ends_of(records[o])
        state = state_next.at[o + 1]
        speed = sum(
            normal[k] * difference(state, ghosts[o], 3 + k, first, second) for k in range(3)
        )
        for k in range(3):
            stage[o + 1, k] = normal[k]
        stage[o + 1, 3] = lam
        stage[o + 1, 4] = speed
        fixed_out[o + 1] = records[o][pl.ds(FIRST_AT, FIXED), :]


def last_kernel(
    parts, mine, stage, back, here, chip, mid, other, fixed, velocity, impulse, rows
):
    me = lax.axis_index("parts")
    odd = me % 2 == 1
    apart = (me % (2 * BLOCK) == BLOCK) | (me % (2 * BLOCK) == BLOCK - 1)
    across = jnp.where(apart, mid[...], other[...])
    across = jnp.where((me > 0) & (me < parts - 1), across, 0.0)
    coupled = {
        -1: jnp.where(odd, chip[...], across),
        0: here[...],
        1: jnp.where(odd, across, chip[...]),
    }
    sums = {}
    for o, heads in ((-1, [CHUNKS + 1]), (0, list(range(CHUNKS))), (1, [CHUNKS])):
        record = fixed.at[o + 1]
        lam = stage[o + 1, 3]
        diag = record[pl.ds(DIAG_AT - FIRST_AT, FIELDS), :]
        lam = jnp.maximum(0.0, lam - (coupled[o] + stage[o + 1, 4]) / diag)
        if o == 0:
            impulse[...] = lam
        first = record[pl.ds(0, FIELDS), :].astype(jnp.int32)
        second = record[pl.ds(SECOND_AT - FIRST_AT, FIELDS), :].astype(jnp.int32)
        force = [stage[o + 1, k] * lam for k in range(3)]
        sums[o] = add_up(force, first, second, heads, rows.at[o + 1])
    incoming = sums[-1][CHUNKS + 1] + sums[1][CHUNKS]
    for c, was in enumerate(state_of(mine)):
        block = moved(was, sums[0][c], incoming, back[pl.ds(c, 1), :])
        velocity[:, pl.ds(c * TILE, TILE)] = block[3:6]


def call(kernel, out_shape, inputs, name, space=pltpu.VMEM, scratch=()):
    many = isinstance(out_shape, (tuple, list))
    vmem = pl.BlockSpec(memory_space=pltpu.VMEM)
    return pl.pallas_call(
        kernel,
        out_shape=out_shape,
        in_specs=[pl.BlockSpec(memory_space=space)] * len(inputs),
        out_specs=[vmem] * len(out_shape) if many else vmem,
        scratch_shapes=list(scratch),
        compiler_params=FROM_HBM if space == pltpu.HBM else PARAMS,
        name=name,
    )(*inputs)


def second_parts(parts, stride):
    pairs = []
    for i in range(parts):
        step = -stride if i % stride < stride // 2 else stride
        to = i + step
        if not 0 <= to < parts:
            to = i + (stride // 2 if step < 0 else -(stride // 2))
        pairs.append((i, to))
    return pairs


def edges(parts):
    return range(BLOCK, parts, 2 * BLOCK)


def next_pairs(parts):
    most = {i: i + 1 if i % 2 else i - 1 for i in range(parts)}
    edge = {i: i ^ 1 for i in range(parts)}
    ends = [0]
    for at in edges(parts):
        ends += [at - 1, at]
        for i, j in ((at - 1, at), (at - 2, at + 2), (at + 1, at + 3)):
            edge[i], edge[j] = j, i
    ends.append(parts - 1)
    closings = [(0, BLOCK), (ends[-2], parts - 1)]
    for k in range(1, len(ends) - 4, 2):
        closings.append((ends[k], ends[k + 2]) if k % 4 == 1 else (ends[k + 1], ends[k + 3]))
    for i, j in closings:
        most[i], most[j] = j, i
    return list(most.items()), list(edge.items())


def body(positions, velocity, inv_mass, swap_lists, rim_list, contact_pair, delassus):
    parts = lax.axis_size("parts")
    stride = parts // GROUP
    grains = positions.shape[1]
    contacts = contact_pair.shape[1]
    tiles = delassus.shape[0]
    reach = 2 * REACH + 1
    float32 = functools.partial(jax.ShapeDtypeStruct, dtype=jnp.float32)
    vmem = lambda *shape: pltpu.VMEM(shape, jnp.float32)
    send = functools.partial(lax.ppermute, axis_name="parts")
    inputs = (
        positions,
        velocity,
        inv_mass.reshape(CHUNKS, TILE),
        swap_lists,
        rim_list.reshape(1, TILE),
    )
    packed = call(
        pack_kernel,
        float32((GROUP, RAW, TILE)),
        inputs,
        "pack",
        pltpu.HBM,
        [pltpu.VMEM(one.shape, one.dtype) for one in inputs]
        + [pltpu.SemaphoreType.DMA((5,))],
    )
    classes = [[r + stride * k for k in LISTED] for r in range(stride)]
    raw = lax.all_to_all(packed, "parts", 0, 0, axis_index_groups=classes)

    half = jax.ShapeDtypeStruct(delassus.shape, jnp.bfloat16)
    fixed, heads, tails = call(
        fixed_kernel, (float32((FIXED, TILE)), half, half), (contact_pair, delassus), "fixed"
    )
    given = send(fixed, perm=second_parts(parts, stride))

    states = call(
        functools.partial(compose_kernel, stride),
        float32((2, FIRST_AT, TILE)),
        (raw,),
        "compose",
        scratch=[vmem(GROUP, FIRST_AT, TILE), vmem(4, FIRST_AT, TILE)],
    )
    record = (RECORD, TILE)
    mine, far, low, high = call(
        functools.partial(join_kernel, stride),
        [float32(record)] * 4,
        (states, fixed, given),
        "join",
    )
    within = [(i, i ^ 1) for i in range(parts)]
    if stride == BLOCK:
        from_far = send(far, perm=[(i, i ^ 3) for i in range(parts)])
        near = (mine, send(mine, perm=within), from_far)
        beyond = [(i, i ^ 2) for i in range(parts)]
        came = (*near, send(low, perm=beyond), send(high, perm=beyond))
    else:
        shifts = [[(i, (i + by) % parts) for i in range(parts)] for by in (1, -1, 2, -2)]
        came = (mine, *[send(mine, perm=shift) for shift in shifts])
        near = came[:3]

    here, known = call(
        functools.partial(near_kernel, stride, parts),
        (float32((tiles, TILE)), float32((4, tiles, TILE))),
        (*near, heads, tails),
        "near",
        scratch=[vmem(reach, *record), vmem(reach, FIELDS, TILE)],
    )
    most, edge = next_pairs(parts)
    other = send(here, perm=most)
    chip = send(here, perm=within)
    mid = send(here, perm=edge)
    stage, back, contact_rows = call(
        functools.partial(middle_kernel, stride, parts, len(came)),
        (
            float32((3, 5, FIELDS, TILE)),
            jax.ShapeDtypeStruct((FIELDS, TILE), jnp.int32),
            float32((3, FIXED, TILE)),
        ),
        (*came, known),
        "middle",
        scratch=[
            vmem(reach, *record),
            vmem(reach, FIELDS, TILE),
            vmem(reach, FIELDS * FIELDS, TILE),
            vmem(3, CHUNKS * FIELDS, TILE),
            vmem(3, FIELDS, TILE),
        ],
    )
    new_velocity, impulse = call(
        functools.partial(last_kernel, parts),
        (float32((3, grains)), float32((tiles, TILE))),
        (mine, stage, back, here, chip, mid, other, contact_rows),
        "last",
        scratch=[vmem(3, FIELDS * FIELDS, TILE)],
    )
    return (new_velocity, impulse.reshape(contacts))


def solution(mesh):
    in_specs = (
        P(None, "parts"),
        P(None, "parts"),
        P("parts"),
        P(None, "parts"),
        P("parts"),
        P(None, "parts"),
        P("parts", None, None),
    )
    out_specs = (P(None, "parts"), P("parts"))
    return jax.shard_map(body, mesh=mesh, in_specs=in_specs, out_specs=out_specs, check_vma=False)
```

```python
import functools

import jax
import jax.numpy as jnp
from jax import lax
from jax.experimental import pallas as pl
from jax.experimental.pallas import tpu as pltpu
from jax.sharding import PartitionSpec as P

TILE = 128
LEVELS = 3
GROUP = 2**LEVELS
REACH = 2
FIELDS = 8
CHUNKS = 4
EXT_CHUNKS = 6
RIM_AT = 7
FIRST_AT = 32
SECOND_AT = 40
DIAG_AT = 48
RECORD = 56
LISTS_AT = 32
RAW = 40
FIXED = RECORD - FIRST_AT
BLOCK = 4
PARAMS = pltpu.CompilerParams(vmem_limit_bytes=32 * 2**20)
FROM_HBM = pltpu.CompilerParams(vmem_limit_bytes=63 * 2**20)
NT = (((1,), (1,)), ((), ()))


def rows_iota(shape):
    return lax.broadcasted_iota(jnp.int32, shape, 0)


def lanes_iota(shape):
    return lax.broadcasted_iota(jnp.int32, shape, 1)


def wide(row):
    return jnp.broadcast_to(row, (FIELDS, TILE))


def take(table, lane):
    return jnp.take_along_axis(table, lane, axis=1, mode="promise_in_bounds")


def look_up(rows, index):
    lane, high = index & (TILE - 1), index >> 7
    found = take(wide(rows[0]), lane)
    for h in range(1, len(rows)):
        found = jnp.where(high == h, take(wide(rows[h]), lane), found)
    return found


def one_hot(low_row):
    row = jnp.broadcast_to(low_row.astype(jnp.float32).astype(jnp.bfloat16), (TILE, TILE))
    column = rows_iota((TILE, TILE)).astype(jnp.float32).astype(jnp.bfloat16)
    return jnp.where(row == column, jnp.bfloat16(1), jnp.bfloat16(0))


def inverse(slot_rows):
    left, right = [], []
    for at, row in enumerate(slot_rows):
        slots = row.astype(jnp.int32)
        place = (lanes_iota((FIELDS, TILE)) + (at * TILE + 1)).astype(jnp.float32)
        heads = jnp.where(wide(slots >> 7) == rows_iota((FIELDS, TILE)), place, 0.0)
        left.append(heads.astype(jnp.bfloat16))
        right.append(one_hot(slots & (TILE - 1)))
    total = lax.dot_general(
        jnp.concatenate(left, axis=1),
        jnp.concatenate(right, axis=1),
        NT,
        preferred_element_type=jnp.float32,
    )
    return total.astype(jnp.int32)


def pack_kernel(*refs):
    sources, out, held, sems = refs[:5], refs[5], refs[6:11], refs[11]
    copies = [
        pltpu.make_async_copy(source, target, sems.at[k])
        for k, (source, target) in enumerate(zip(sources, held))
    ]
    for copy in copies:
        copy.start()
    pos, vel, mass, lists, rim = held
    for copy in copies:
        copy.wait()
    first = out.at[0]
    for c in range(CHUNKS):
        lanes = pl.ds(c * TILE, TILE)
        first[pl.ds(FIELDS * c, 3), :] = pos[:, lanes]
        first[pl.ds(FIELDS * c + 3, 3), :] = vel[:, lanes]
        first[pl.ds(FIELDS * c + 6, 1), :] = mass[pl.ds(c, 1), :]
        spare = rim[...].astype(jnp.float32) if c == 0 else jnp.zeros((1, TILE), jnp.float32)
        first[pl.ds(FIELDS * c + 7, 1), :] = spare
    for level in range(LEVELS):
        for h in range(2):
            row = lists[pl.ds(level, 1), pl.ds(h * TILE, TILE)]
            first[pl.ds(LISTS_AT + 2 * level + h, 1), :] = row.astype(jnp.float32)
    first[pl.ds(LISTS_AT + 2 * LEVELS, 2), :] = jnp.zeros((2, TILE), jnp.float32)
    whole = first[...]
    for m in range(1, GROUP):
        out[m] = whole


def fixed_kernel(pair, tiles, out, heads, tails):
    eye = rows_iota((TILE, TILE)) == lanes_iota((TILE, TILE))
    for t in range(tiles.shape[0]):
        lanes = pl.ds(t * TILE, TILE)
        out[pl.ds(t, 1), :] = pair[pl.ds(0, 1), lanes].astype(jnp.float32)
        out[pl.ds(FIELDS + t, 1), :] = pair[pl.ds(1, 1), lanes].astype(jnp.float32)
        tile = tiles[t]
        turned = tile.T
        head = turned.astype(jnp.bfloat16)
        heads[t] = head
        tails[t] = (turned - head.astype(jnp.float32)).astype(jnp.bfloat16)
        diag = jnp.sum(jnp.where(eye, tile, 0.0), axis=0, keepdims=True)
        out[pl.ds(2 * FIELDS + t, 1), :] = diag


def second_part(stride):
    me = lax.axis_index("parts")
    member, kind = me // stride, me % stride
    step = jnp.where(kind < stride // 2, 1, -1)
    return step, (member + step >= 0) & (member + step < GROUP)


def swapped(lists, other_lists, own, other, out):
    back = inverse(lists)
    place = jnp.maximum(back - 1, 0)
    slot = look_up(other_lists, place).astype(jnp.int32)
    lane = slot & (TILE - 1)
    block = jnp.where(back > 0, slot >> 7, -1)
    tables = [other[pl.ds(FIELDS * h, FIELDS), :] for h in range(CHUNKS)]
    for c in range(CHUNKS):
        rows = pl.ds(FIELDS * c, FIELDS)
        lane_c, block_c = wide(lane[c : c + 1]), wide(block[c : c + 1])
        found = own[rows, :]
        for h, table in enumerate(tables):
            found = jnp.where(block_c == h, take(table, lane_c), found)
        out[rows, :] = found


def compose_kernel(stride, raw, own, once, twice):
    member = lax.axis_index("parts") // stride
    step, exists = second_part(stride)

    def came_from(part):
        return raw.at[(part + 3) % GROUP]

    def list_rows(part, level):
        rows = came_from(part)
        return [rows[pl.ds(LISTS_AT + 2 * level + h, 1), :] for h in range(2)]

    def level_step(level, part, apart, own_state, other_state, out):
        lists, others = list_rows(part, level), list_rows(part ^ apart, level)
        swapped(lists, others, own_state, other_state, out)

    for r in range(GROUP):
        level_step(0, r, 4, came_from(r), came_from(r ^ 4), once.at[r])
    second = (member + step + GROUP) % GROUP
    for i, part in enumerate((member, member ^ 1, second, second ^ 1)):
        level_step(1, part, 2, once.at[part], once.at[part ^ 2], twice.at[i])
    for i, part in enumerate((member, second)):
        level_step(2, part, 1, twice.at[2 * i], twice.at[2 * i + 1], own.at[i])
        own[i, pl.ds(RIM_AT, 1), :] = came_from(part)[pl.ds(RIM_AT, 1), :]
    for c in range(CHUNKS):
        rows = pl.ds(FIELDS * c, FIELDS)
        own[1, rows, :] = jnp.where(exists, own[1, rows, :], 0.0)


def join_kernel(stride, states, fixed, given, mine, far, low, high):
    kind = lax.axis_index("parts") % stride
    exists = second_part(stride)[1]
    early, outer = kind < stride // 2, (kind == 0) | (kind == stride - 1)
    for at in range(0, RECORD, FIELDS):
        rows = pl.ds(at, FIELDS)
        if at < FIRST_AT:
            one, two = states[0, rows, :], states[1, rows, :]
        else:
            part = pl.ds(at - FIRST_AT, FIELDS)
            absent = 1.0 if at == DIAG_AT else 0.0
            one, two = fixed[part, :], jnp.where(exists, given[part, :], absent)
        mine[rows, :] = one
        far[rows, :] = jnp.where(outer, two, one)
        low[rows, :] = jnp.where(early, one, two)
        high[rows, :] = jnp.where(early, two, one)


def gather_records(stride, parts, came, records):
    me = lax.axis_index("parts")
    swap = (stride == BLOCK) & (me % 2 == 0)
    mine, one, two, *side = came
    for at in range(0, RECORD, FIELDS):
        rows = pl.ds(at, FIELDS)
        blocks = {
            0: mine[rows, :],
            -1: jnp.where(swap, two[rows, :], one[rows, :]),
            1: jnp.where(swap, one[rows, :], two[rows, :]),
        }
        if side:
            blocks[-2], blocks[2] = side[0][rows, :], side[1][rows, :]
        for o, block in blocks.items():
            absent = 1.0 if at == DIAG_AT else 0.0
            there = (me + o >= 0) & (me + o < parts)
            records[o + REACH, rows, :] = jnp.where(there, block, absent) if o else block


def state_of(record):
    return [record[pl.ds(FIELDS * c, FIELDS), :] for c in range(CHUNKS)]


def ends_of(record):
    first = record[pl.ds(FIRST_AT, FIELDS), :].astype(jnp.int32)
    second = record[pl.ds(SECOND_AT, FIELDS), :].astype(jnp.int32)
    return first, second


def diag_of(record):
    return record[pl.ds(DIAG_AT, FIELDS), :]


def rim_of(record, blocks):
    slots = wide(record[pl.ds(RIM_AT, 1), :].astype(jnp.int32))
    lane, high = slots & (TILE - 1), slots >> 7
    found = take(blocks[0], lane)
    for c in range(1, CHUNKS):
        found = jnp.where(high == c, take(blocks[c], lane), found)
    return found


def difference(local, ghosts, field, first, second):
    near = [local[pl.ds(FIELDS * c + field, 1), :] for c in range(CHUNKS)]
    far = [one[pl.ds(field, 1), :] for one in ghosts]
    return look_up(near, first) - look_up(near + far if len(far) > 1 else far, second)


def first_lam(record, ghosts):
    first, second = ends_of(record)
    normal = [difference(record, ghosts, k, first, second) for k in range(3)]
    speed = sum(normal[k] * difference(record, ghosts, 3 + k, first, second) for k in range(3))
    return normal, jnp.maximum(0.0, -speed / diag_of(record))


def add_up(force, first, second, heads, rows):
    for k in range(3):
        head = force[k].astype(jnp.bfloat16).astype(jnp.float32)
        rows[pl.ds(k, FIELDS, stride=FIELDS), :] = force[k] - head
        rows[pl.ds(3 + k, FIELDS, stride=FIELDS), :] = head
    empty = jnp.zeros((FIELDS, TILE), jnp.float32)
    pad = [empty] * (len(heads) % 2)
    left, right = [], []
    for t in range(FIELDS):
        value = rows[pl.ds(FIELDS * t, FIELDS), :]
        for index, limit, signed in ((first, CHUNKS, value), (second, EXT_CHUNKS, -value)):
            if min(heads) >= limit:
                continue
            row = index[t : t + 1]
            high = wide(row >> 7)
            groups = [jnp.where(high == h, signed, 0.0) if h < limit else empty for h in heads]
            left.append(jnp.concatenate(groups + pad, axis=0))
            right.append(one_hot(row & (TILE - 1)))
    total = lax.dot_general(
        jnp.concatenate(left, axis=1).astype(jnp.bfloat16),
        jnp.concatenate(right, axis=1),
        NT,
        preferred_element_type=jnp.float32,
    )
    blocks = [total[FIELDS * k : FIELDS * (k + 1)] for k in range(len(heads))]
    return {h: block + pltpu.roll(block, 3, 0) for h, block in zip(heads, blocks)}


def moved(was, here, incoming, back_row):
    place = wide(back_row)
    extra = jnp.where(place > 0, take(incoming, jnp.maximum(place - 1, 0)), 0.0)
    field = rows_iota((FIELDS, TILE))
    gain = wide(was[6:7]) * (here + extra)
    return was + jnp.where((field >= 3) & (field < 6), gain, 0.0)


def near_kernel(stride, parts, *refs):
    came, (heads, tails, coupled, contacts, records, rims) = refs[:3], refs[3:]
    gather_records(stride, parts, came, records)
    for k in (-1, 1):
        record = records.at[REACH + k]
        rims[REACH + k] = rim_of(record, state_of(record))
    normal, lam = first_lam(records.at[REACH], (rims.at[REACH - 1], rims.at[REACH + 1]))
    for k, one in enumerate((*normal, lam)):
        contacts[k] = one
    head = lam.astype(jnp.bfloat16).astype(jnp.float32)
    both = jnp.concatenate([head, lam - head], axis=0).astype(jnp.bfloat16)
    total = jnp.zeros((FIELDS, TILE), jnp.float32)
    for t in range(heads.shape[0]):
        main = jnp.dot(both, heads[t], preferred_element_type=jnp.float32)
        rest = jnp.dot(both, tails[t], preferred_element_type=jnp.float32)
        whole = main[:FIELDS] + main[FIELDS:] + rest[:FIELDS]
        total = jnp.where(rows_iota((FIELDS, TILE)) == t, whole, total)
    coupled[...] = total


def middle_kernel(stride, parts, count, *refs):
    came, known = refs[:count], refs[count]
    stage, back_here, fixed_out, gathered, rims, rows, state_next, rims_next = refs[count + 1 :]
    gather_records(stride, parts, came, gathered)
    records = {o: gathered.at[o + REACH] for o in range(-REACH, REACH + 1)}
    rim = {o: rims.at[o + REACH] for o in records}
    rim_next = {o: rims_next.at[o + 1] for o in (-1, 0, 1)}
    left, right = CHUNKS, CHUNKS + 1
    local = list(range(CHUNKS))
    for o, record in records.items():
        rim[o][...] = rim_of(record, state_of(record))
    heads = {-2: [right], -1: local + [right], 0: local + [left, right], 1: local + [left], 2: [left]}
    ghosts = {o: (rim[o - 1], rim[o + 1]) for o in (-1, 1)}
    ghosts.update({-2: (rim[-1],), 2: (rim[1],)})
    sums, contacts = {}, {}
    for o, record in records.items():
        contacts[o] = first_lam(record, ghosts[o]) if o else ([known[k] for k in range(3)], known[3])
    for o, record in records.items():
        normal, lam = contacts[o]
        first, second = ends_of(record)
        force = [one * lam for one in normal]
        sums[o] = add_up(force, first, second, heads[o], rows.at[o + REACH])
    for o in (-1, 0, 1):
        incoming = sums[o - 1][right] + sums[o + 1][left]
        back = inverse([records[o][pl.ds(RIM_AT, 1), :]])
        if o == 0:
            back_here[...] = back
        blocks = [
            moved(was, sums[o][c], incoming, back[c : c + 1])
            for c, was in enumerate(state_of(records[o]))
        ]
        rim_next[o][...] = rim_of(records[o], blocks)
        for c in range(CHUNKS):
            state_next[o + 1, pl.ds(FIELDS * c, FIELDS), :] = blocks[c]
    ghosts = {-1: (rim_next[0],), 0: (rim_next[-1], rim_next[1]), 1: (rim_next[0],)}
    for o in (-1, 0, 1):
        normal, lam = contacts[o]
        first, second = ends_of(records[o])
        state = state_next.at[o + 1]
        speed = sum(
            normal[k] * difference(state, ghosts[o], 3 + k, first, second) for k in range(3)
        )
        for k in range(3):
            stage[o + 1, k] = normal[k]
        stage[o + 1, 3] = lam
        stage[o + 1, 4] = speed
        fixed_out[o + 1] = records[o][pl.ds(FIRST_AT, FIXED), :]


def last_kernel(
    parts, mine, stage, back, here, chip, mid, other, fixed, velocity, impulse, rows
):
    me = lax.axis_index("parts")
    odd = me % 2 == 1
    apart = (me % (2 * BLOCK) == BLOCK) | (me % (2 * BLOCK) == BLOCK - 1)
    across = jnp.where(apart, mid[...], other[...])
    across = jnp.where((me > 0) & (me < parts - 1), across, 0.0)
    coupled = {
        -1: jnp.where(odd, chip[...], across),
        0: here[...],
        1: jnp.where(odd, across, chip[...]),
    }
    sums = {}
    for o, heads in ((-1, [CHUNKS + 1]), (0, list(range(CHUNKS))), (1, [CHUNKS])):
        record = fixed.at[o + 1]
        lam = stage[o + 1, 3]
        diag = record[pl.ds(DIAG_AT - FIRST_AT, FIELDS), :]
        lam = jnp.maximum(0.0, lam - (coupled[o] + stage[o + 1, 4]) / diag)
        if o == 0:
            impulse[...] = lam
        first = record[pl.ds(0, FIELDS), :].astype(jnp.int32)
        second = record[pl.ds(SECOND_AT - FIRST_AT, FIELDS), :].astype(jnp.int32)
        force = [stage[o + 1, k] * lam for k in range(3)]
        sums[o] = add_up(force, first, second, heads, rows.at[o + 1])
    incoming = sums[-1][CHUNKS + 1] + sums[1][CHUNKS]
    for c, was in enumerate(state_of(mine)):
        block = moved(was, sums[0][c], incoming, back[pl.ds(c, 1), :])
        velocity[:, pl.ds(c * TILE, TILE)] = block[3:6]


def call(kernel, out_shape, inputs, name, space=pltpu.VMEM, scratch=()):
    many = isinstance(out_shape, (tuple, list))
    vmem = pl.BlockSpec(memory_space=pltpu.VMEM)
    return pl.pallas_call(
        kernel,
        out_shape=out_shape,
        in_specs=[pl.BlockSpec(memory_space=space)] * len(inputs),
        out_specs=[vmem] * len(out_shape) if many else vmem,
        scratch_shapes=list(scratch),
        compiler_params=FROM_HBM if space == pltpu.HBM else PARAMS,
        name=name,
    )(*inputs)


def second_parts(parts, stride):
    pairs = []
    for i in range(parts):
        step = -stride if i % stride < stride // 2 else stride
        to = i + step
        if not 0 <= to < parts:
            to = i + (stride // 2 if step < 0 else -(stride // 2))
        pairs.append((i, to))
    return pairs


def edges(parts):
    return range(BLOCK, parts, 2 * BLOCK)


def next_pairs(parts):
    most = {i: i + 1 if i % 2 else i - 1 for i in range(parts)}
    edge = {i: i ^ 1 for i in range(parts)}
    ends = [0]
    for at in edges(parts):
        ends += [at - 1, at]
        for i, j in ((at - 1, at), (at - 2, at + 2), (at + 1, at + 3)):
            edge[i], edge[j] = j, i
    ends.append(parts - 1)
    closings = [(0, BLOCK), (ends[-2], parts - 1)]
    for k in range(1, len(ends) - 4, 2):
        closings.append((ends[k], ends[k + 2]) if k % 4 == 1 else (ends[k + 1], ends[k + 3]))
    for i, j in closings:
        most[i], most[j] = j, i
    return list(most.items()), list(edge.items())


def body(positions, velocity, inv_mass, swap_lists, rim_list, contact_pair, delassus):
    parts = lax.axis_size("parts")
    stride = parts // GROUP
    grains = positions.shape[1]
    contacts = contact_pair.shape[1]
    tiles = delassus.shape[0]
    reach = 2 * REACH + 1
    float32 = functools.partial(jax.ShapeDtypeStruct, dtype=jnp.float32)
    vmem = lambda *shape: pltpu.VMEM(shape, jnp.float32)
    send = functools.partial(lax.ppermute, axis_name="parts")
    inputs = (
        positions,
        velocity,
        inv_mass.reshape(CHUNKS, TILE),
        swap_lists,
        rim_list.reshape(1, TILE),
    )
    packed = call(
        pack_kernel,
        float32((GROUP, RAW, TILE)),
        inputs,
        "pack",
        pltpu.HBM,
        [pltpu.VMEM(one.shape, one.dtype) for one in inputs]
        + [pltpu.SemaphoreType.DMA((5,))],
    )
    classes = [[r + stride * ((k - 3) % GROUP) for k in range(GROUP)] for r in range(stride)]
    raw = lax.all_to_all(packed, "parts", 0, 0, axis_index_groups=classes)

    half = jax.ShapeDtypeStruct(delassus.shape, jnp.bfloat16)
    fixed, heads, tails = call(
        fixed_kernel, (float32((FIXED, TILE)), half, half), (contact_pair, delassus), "fixed"
    )
    given = send(fixed, perm=second_parts(parts, stride))

    states = call(
        functools.partial(compose_kernel, stride),
        float32((2, FIRST_AT, TILE)),
        (raw,),
        "compose",
        scratch=[vmem(GROUP, FIRST_AT, TILE), vmem(4, FIRST_AT, TILE)],
    )
    record = (RECORD, TILE)
    mine, far, low, high = call(
        functools.partial(join_kernel, stride),
        [float32(record)] * 4,
        (states, fixed, given),
        "join",
    )
    within = [(i, i ^ 1) for i in range(parts)]
    if stride == BLOCK:
        from_far = send(far, perm=[(i, i ^ 3) for i in range(parts)])
        near = (mine, send(mine, perm=within), from_far)
        beyond = [(i, i ^ 2) for i in range(parts)]
        came = (*near, send(low, perm=beyond), send(high, perm=beyond))
    else:
        shifts = [[(i, (i + by) % parts) for i in range(parts)] for by in (1, -1, 2, -2)]
        came = (mine, *[send(mine, perm=shift) for shift in shifts])
        near = came[:3]

    here, known = call(
        functools.partial(near_kernel, stride, parts),
        (float32((tiles, TILE)), float32((4, tiles, TILE))),
        (*near, heads, tails),
        "near",
        scratch=[vmem(reach, *record), vmem(reach, FIELDS, TILE)],
    )
    most, edge = next_pairs(parts)
    other = send(here, perm=most)
    chip = send(here, perm=within)
    mid = send(here, perm=edge)
    stage, back, contact_rows = call(
        functools.partial(middle_kernel, stride, parts, len(came)),
        (
            float32((3, 5, FIELDS, TILE)),
            jax.ShapeDtypeStruct((FIELDS, TILE), jnp.int32),
            float32((3, FIXED, TILE)),
        ),
        (*came, known),
        "middle",
        scratch=[
            vmem(reach, *record),
            vmem(reach, FIELDS, TILE),
            vmem(reach, FIELDS * FIELDS, TILE),
            vmem(3, CHUNKS * FIELDS, TILE),
            vmem(3, FIELDS, TILE),
        ],
    )
    new_velocity, impulse = call(
        functools.partial(last_kernel, parts),
        (float32((3, grains)), float32((tiles, TILE))),
        (mine, stage, back, here, chip, mid, other, contact_rows),
        "last",
        scratch=[vmem(3, FIELDS * FIELDS, TILE)],
    )
    return (new_velocity, impulse.reshape(contacts))


def solution(mesh):
    in_specs = (
        P(None, "parts"),
        P(None, "parts"),
        P("parts"),
        P(None, "parts"),
        P("parts"),
        P(None, "parts"),
        P("parts", None, None),
    )
    out_specs = (P(None, "parts"), P("parts"))
    return jax.shard_map(body, mesh=mesh, in_specs=in_specs, out_specs=out_specs, check_vma=False)
```
